32 devices in a mesh: dp: 4 (over y, x), table: 8 (over z, core).
Axes of the slice: x: 2, y: 2, z: 4, core: 2. Of those that a mesh axis runs over, the one named last changes fastest.
Arguments:
- hidden_in: bfloat16 [512, 4096], P('dp', 'table'), may hold values from -6 to 6
- gate_weight: bfloat16 [4096, 4096], P('dp', 'table'), may hold values from -0.09375 to 0.09375
- values: bfloat16 [1024, 4096], P('table'), may hold values from -6 to 6
- pick_rows: int32 [512, 32], P('dp'), may hold values from 0 to 1023, all different within a row
- pick_scores: float32 [512, 32], P('dp'), may hold values from -300 to 300
- grad_out: bfloat16 [512, 4096], P('dp', 'table'), may hold values from -6 to 6
Outputs:
- branch_out: bfloat16 [512, 4096], P('dp', 'table')
- grad_hidden: bfloat16 [512, 4096], P('dp', 'table')
- grad_gate: float32 [4096, 4096], P('dp', 'table')
- grad_values: float32 [1024, 4096], P('table')
- grad_scores: float32 [512, 32], P('dp')
The draws below stay inside these ranges and needn't reach their ends.
Inputs may be any that keep to these rules, and one draw needn't show every extreme that they name: `pick_rows`: the 32 rows of a token are distinct.
All inputs are finite; a program needn't handle non-finite values.
Results may differ from the reference program's by a relative error of at most 0.025.
Values may be sent and summed in bfloat16 or wider, within the bound.
No kernel may reach another device: no remote copies, remote signals or barrier semaphores. Data moves between devices by JAX's collectives and lax.ppermute only.
A program may use at most 64 MiB of HBM per device.

```python
import jax
import jax.numpy as jnp
from jax import lax

D = 4096
K = 32
TOK_DEV = 128
TOKENS = 512
ROWS = 1024
N_DP = 4
N_TABLE = 8


def draw_pick_scores(key, part):
    first = jax.random.fold_in(key, 0)
    return jnp.clip(2.5 * jax.random.normal(first, (TOKENS, K), jnp.float32), -15.0, 15.0)


def levels(own_key, shape, shards, least, high):
    level = 1.0
    for position, shards_of in shards:
        heights = jax.random.uniform(jax.random.fold_in(jax.random.fold_in(own_key, 6), position), (shards_of,), jnp.float32, least / len(shards), high / len(shards))
        level = level * jnp.repeat(jnp.exp(heights), shape[position] // shards_of).reshape((-1,) + (1,) * (len(shape) - 1 - position))
    return level


def picks_of(rng, rows, amount, top, lift):
    sequence = jax.random.permutation(jax.random.fold_in(rng, 1), amount)
    pull = sequence
    for power in range(3):
        pull = pull * pull // amount
    pull = pull * lift // amount
    lots = jax.random.randint(jax.random.fold_in(rng, 2), (rows, amount), 0, 4096) + pull
    sure = jax.random.permutation(jax.random.fold_in(rng, 3), rows)[jnp.arange(amount) % rows]
    lots = jnp.where(jnp.arange(rows)[:, None] == sure[None, :], 1 << 14, lots)
    score = lots * amount + jnp.arange(amount)
    return lax.top_k(score.astype(jnp.int32), top)[1].astype(jnp.int32)


def normal_values(stream_key, shape, deviation, bound, cuts=(), held_as=jnp.bfloat16):
    level = levels(stream_key, shape, cuts, -0.22, 0.18) if cuts else 1.0
    array = jax.random.normal(stream_key, shape, jnp.float32) * deviation * level
    return jnp.minimum(jnp.maximum(array, -bound), bound).astype(held_as)


def setup_inputs(seed: int = 0) -> dict:
    key_list = jax.random.split(jax.random.key(seed), 7)
    hidden_in = normal_values(key_list[0], (TOKENS, D), 1.0, 6.0, ((0, 4), (1, 8)))
    gate_weight = normal_values(key_list[1], (D, D), D ** -0.5, 0.09375, ((0, 4), (1, 8)))
    values = normal_values(key_list[2], (ROWS, D), 1.0, 6.0, ((0, 8),))
    pick_rows = picks_of(key_list[3], TOKENS, ROWS, K, 512)
    pick_scores = draw_pick_scores(jax.random.fold_in(key_list[6], 71), 0)
    grad_out = normal_values(key_list[5], (TOKENS, D), 1.0, 6.0, ((0, 4), (1, 8)))
    return dict(hidden_in=hidden_in, gate_weight=gate_weight, values=values, pick_rows=pick_rows, pick_scores=pick_scores, grad_out=grad_out)


def silu_parts(gate_input):
    sigmoid_v = jax.nn.sigmoid(gate_input)
    return gate_input * sigmoid_v, sigmoid_v * (1.0 + gate_input * (1.0 - sigmoid_v))


def reference(hidden_in, gate_weight, values, pick_rows, pick_scores, grad_out):
    row_max = jnp.max(pick_scores, axis=1, keepdims=True)
    exponent = jnp.exp(pick_scores - row_max)
    weights = exponent / jnp.sum(exponent, axis=1, keepdims=True)
    weights_bf = lax.optimization_barrier(weights.astype(jnp.bfloat16))
    weight_wide = weights_bf.astype(jnp.float32)
    row_blocks = pick_rows.reshape(N_DP, TOK_DEV, K)
    weight_blocks = weight_wide.reshape(N_DP, TOK_DEV, K)

    def read_block(block_args):
        row_ids, block_weights = block_args
        picked = values[row_ids].astype(jnp.float32)
        return jnp.einsum("tk,tkd->td", block_weights, picked)

    memory_read = lax.map(read_block, (row_blocks, weight_blocks)).reshape(TOKENS, D)
    gate_input = jnp.dot(hidden_in, gate_weight, preferred_element_type=jnp.float32)
    gate_value, gate_slope = silu_parts(gate_input)
    branch_out = (memory_read * gate_value).astype(jnp.bfloat16)
    upstream = grad_out.astype(jnp.float32)
    mem_grad = (upstream * gate_value).astype(jnp.bfloat16)
    gate_grad_in = (upstream * memory_read * gate_slope).astype(jnp.bfloat16)
    grad_blocks = mem_grad.reshape(N_DP, TOK_DEV, D)

    def affinity_block(block_args):
        row_ids, block_grads = block_args
        picked = values[row_ids].astype(jnp.float32)
        return jnp.einsum("tkd,td->tk", picked, block_grads.astype(jnp.float32))

    affinity = lax.map(affinity_block, (row_blocks, grad_blocks)).reshape(TOKENS, K)
    grad_scores = weights * (affinity - jnp.sum(weights * affinity, axis=1, keepdims=True))

    def value_step(running, block_args):
        row_ids, block_weights, block_grads = block_args
        spread = block_weights[:, :, None] * block_grads.astype(jnp.float32)[:, None, :]
        block_term = jax.ops.segment_sum(spread.reshape(TOK_DEV * K, D), row_ids.reshape(TOK_DEV * K), num_segments=ROWS)
        rounded = lax.optimization_barrier(block_term.astype(jnp.bfloat16))
        return running + rounded.astype(jnp.float32), None

    grad_values, leftover = lax.scan(value_step, jnp.zeros((ROWS, D), jnp.float32), (row_blocks, weight_blocks, grad_blocks))

    def gate_step(running, block_args):
        block_in, block_grad = block_args
        block_term = lax.dot_general(block_in, block_grad, (((0,), (0,)), ((), ())), preferred_element_type=jnp.float32)
        rounded = lax.optimization_barrier(block_term.astype(jnp.bfloat16))
        return running + rounded.astype(jnp.float32), None

    grad_gate, leftover = lax.scan(gate_step, jnp.zeros((D, D), jnp.float32), (hidden_in.reshape(N_DP, TOK_DEV, D), gate_grad_in.reshape(N_DP, TOK_DEV, D)))
    col_width = D // N_TABLE
    grad_cols = gate_grad_in.reshape(TOKENS, N_TABLE, col_width).transpose(1, 0, 2)
    weight_cols = gate_weight.reshape(D, N_TABLE, col_width).transpose(1, 0, 2)

    def input_step(running, block_args):
        block_grad, block_weight = block_args
        block_term = lax.dot_general(block_grad, block_weight, (((1,), (1,)), ((), ())), preferred_element_type=jnp.float32)
        rounded = lax.optimization_barrier(block_term.astype(jnp.bfloat16))
        return running + rounded.astype(jnp.float32), None

    input_sum, leftover = lax.scan(input_step, jnp.zeros((TOKENS, D), jnp.float32), (grad_cols, weight_cols))
    grad_hidden = input_sum.astype(jnp.bfloat16)
    return (branch_out, grad_hidden, grad_gate, grad_values, grad_scores)
```

```python
import functools

import jax
import jax.numpy as jnp
from jax import lax
from jax.experimental import pallas as pl
from jax.experimental.pallas import tpu as pltpu
from jax.sharding import PartitionSpec as P

DIRECT = 4


def block(x, index):
    return lax.dynamic_index_in_dim(x, index, 0, keepdims=False)


def placed(pieces, indices):
    out = jnp.zeros((len(pieces),) + pieces[0].shape, pieces[0].dtype)
    for piece, index in zip(pieces, indices):
        out = lax.dynamic_update_index_in_dim(out, piece, index, 0)
    return out


def hop(x, axis, size, mask):
    return lax.ppermute(x, axis, [(i, i ^ mask) for i in range(size)])


def order(axis, size):
    return [lax.axis_index(axis) ^ k for k in range(size)]


def gather(x, axis, size):
    if size <= DIRECT:
        return [x] + [hop(x, axis, size, k) for k in range(1, size)]
    whole = lax.all_gather(x, axis, axis=0)
    return [block(whole, k) for k in order(axis, size)]


def swap(pieces, axis, size, step=1):
    if len(pieces) <= DIRECT:
        return [pieces[0]] + [
            hop(pieces[k], axis, size, k * step) for k in range(1, len(pieces))
        ]
    ids = order(axis, size)
    whole = lax.all_to_all(placed(pieces, ids), axis, split_axis=0, concat_axis=0)
    return [block(whole, k) for k in ids]


def swap_table(pieces, size):
    if size // 2 <= DIRECT:
        rows, cols = pieces.shape[1:]
        pairs = pieces.reshape(size // 2, 2, rows, cols)
        other = hop(pairs[:, 1], "table", size, 1)
        both = jnp.stack([pairs[:, 0], other], axis=1)
        return swap([both[i] for i in range(size // 2)], "table", size, 2)
    got = swap([pieces[k] for k in range(size)], "table", size)
    return [jnp.stack(got[2 * i : 2 * i + 2]) for i in range(size // 2)]


def spread_kernel(rows_ref, weights_ref, out_ref):
    tile = 32
    tokens = rows_ref.shape[1]

    def step(i, carry):
        base = pl.multiple_of(i * tile, tile)
        here = lax.broadcasted_iota(jnp.int32, (tile, tokens), 0) + base
        total = jnp.zeros((tile, tokens), jnp.float32)
        for k in range(rows_ref.shape[0]):
            hit = rows_ref[k : k + 1, :] == here
            total = jnp.where(hit, weights_ref[k : k + 1, :], total)
        out_ref[pl.ds(base, tile), :] = total.astype(out_ref.dtype)
        return carry

    lax.fori_loop(0, out_ref.shape[0] // tile, step, 0)


def spread(rows, weights, row_total):
    picks, tokens = rows.shape
    width = min(tokens, 512)
    return pl.pallas_call(
        spread_kernel,
        grid=(tokens // width,),
        in_specs=[pl.BlockSpec((picks, width), lambda i: (0, i))] * 2,
        out_specs=pl.BlockSpec((row_total, width), lambda i: (0, i)),
        out_shape=jax.ShapeDtypeStruct((row_total, tokens), jnp.bfloat16),
        compiler_params=pltpu.CompilerParams(vmem_limit_bytes=16 << 20),
        cost_estimate=pl.CostEstimate(
            flops=2 * picks * tokens * row_total,
            bytes_accessed=2 * tokens * row_total,
            transcendentals=0,
        ),
    )(rows, weights)


def pick_kernel(table_ref, rows_ref, out_ref):
    lanes = 128
    rows = rows_ref[...]
    inner = rows & (lanes - 1)
    outer = rows >> 7
    total = jnp.zeros(out_ref.shape, jnp.float32)
    for j in range(table_ref.shape[1] // lanes):
        part = table_ref[:, j * lanes : (j + 1) * lanes]
        found = jnp.take_along_axis(part, inner, axis=1)
        total = jnp.where(outer == j, found, total)
    out_ref[...] = total


def pick(table, rows):
    return pl.pallas_call(
        pick_kernel,
        out_shape=jax.ShapeDtypeStruct(rows.shape, jnp.float32),
        cost_estimate=pl.CostEstimate(
            flops=rows.size * 16, bytes_accessed=4 * table.size, transcendentals=0
        ),
    )(table, rows)


def pick_weights(pick_scores):
    row_max = jnp.max(pick_scores, axis=1, keepdims=True)
    exponent = jnp.exp(pick_scores - row_max)
    return exponent / jnp.sum(exponent, axis=1, keepdims=True)


def hidden_rows(hidden_in, dp, table):
    tokens, cols = hidden_in.shape
    me, here = lax.axis_index("dp"), lax.axis_index("table")
    if table == 2 * dp and dp <= DIRECT:
        moved = []
        for k in range(dp):
            perm = [
                ((e * dp + z) * 2 + h, (z * dp + (e ^ k)) * 2 + h)
                for e in range(dp)
                for z in range(dp)
                for h in range(2)
            ]
            moved.append(lax.ppermute(hidden_in, ("dp", "table"), perm))
        mine = placed(moved, [(here // 2) ^ me ^ k for k in range(dp)])
        mine = mine.reshape(dp * tokens, cols)
        return [mine, hop(mine, "table", table, 1)]
    width = cols * table // dp
    wide = lax.all_gather(hidden_in, "table", axis=1, tiled=True)
    got = swap(
        [
            lax.dynamic_slice_in_dim(wide, k * width, width, 1)
            for k in order("dp", dp)
        ],
        "dp",
        dp,
    )
    return [jnp.concatenate(got, axis=0)]


def gate_slices(gate_weight, halves):
    if halves == 1:
        return [gate_weight]
    parts = gate_weight.reshape(2, -1, gate_weight.shape[1])
    core = lax.axis_index("table") % 2
    return [block(parts, core), block(parts, 1 - core)]


def return_hidden(grad_cols, weights, dp, table, tokens, cols):
    me, here = lax.axis_index("dp"), lax.axis_index("table")

    def term(weight):
        return lax.dot_general(
            grad_cols, weight, (((1,), (1,)), ((), ())), preferred_element_type=jnp.float32
        )

    if len(weights) == 2:
        arrived = hop(term(weights[1]).astype(jnp.bfloat16), "table", table, 1)
        pair = (term(weights[0]) + arrived.astype(jnp.float32)).astype(jnp.bfloat16)
        pair = pair.reshape(dp, tokens, cols)
        got = jnp.stack(swap([pair[k] for k in range(dp)], "dp", dp))
        sent = [block(got, (here // 2) ^ me ^ i) for i in range(dp)]
        terms = swap(sent, "table", table, 2)
    else:
        width = weights[0].shape[0]
        parts = term(weights[0]).astype(jnp.bfloat16).reshape(dp, tokens, width)
        got = swap([parts[k] for k in range(dp)], "dp", dp)
        wide = jnp.concatenate(
            list(placed(got, order("dp", dp))), axis=1
        ).reshape(tokens, table, cols)
        terms = swap([wide[:, k] for k in order("table", table)], "table", table)
    return functools.reduce(
        jnp.add, [t.astype(jnp.float32) for t in terms]
    ).astype(jnp.bfloat16)


def local(dp, table, hidden_in, gate_weight, values, pick_rows, pick_scores, grad_out):
    tokens, cols = hidden_in.shape
    rows_here, width = values.shape
    sub = rows_here // dp
    row_total = rows_here * table
    me, here = lax.axis_index("dp"), lax.axis_index("table")
    f32, bf16 = jnp.float32, jnp.bfloat16

    hidden_parts = hidden_rows(hidden_in, dp, table)
    weight_parts = gate_slices(gate_weight, len(hidden_parts))

    quarter = block(values.reshape(dp, sub, table, cols), me)
    sent = jnp.stack([lax.dynamic_index_in_dim(quarter, k, 1, keepdims=False) for k in order("table", table)])
    quarter = jnp.concatenate(
        [p.reshape(2 * sub, cols) for p in swap_table(sent, table)], axis=0
    )
    value_cols = jnp.concatenate(gather(quarter, "dp", dp), axis=0)

    owner, inner = pick_rows // rows_here, pick_rows % rows_here
    weights = pick_weights(pick_scores)
    weights_bf = weights.astype(bf16)

    def moved_row(row):
        owner, inner = row // rows_here, row % rows_here
        return ((inner // sub) ^ me) * (table * sub) + (owner ^ here) * sub + inner % sub

    small = jnp.concatenate(
        [pick_rows.astype(f32).T, weights_bf.astype(f32).T], axis=0
    )
    small_all = jnp.concatenate(gather(small, "dp", dp), axis=1)
    grad_out_all = jnp.concatenate(gather(grad_out, "dp", dp), axis=0)
    picks = pick_rows.shape[1]
    spread_all = spread(
        moved_row(small_all[:picks].astype(jnp.int32)), small_all[picks:], row_total
    )

    partial_gate = functools.reduce(
        jnp.add,
        [jnp.dot(a, b, preferred_element_type=f32) for a, b in zip(hidden_parts, weight_parts)],
    ).astype(bf16).reshape(dp, tokens, cols)
    terms = swap([partial_gate[k] for k in range(dp)], "dp", dp)
    gate_own = functools.reduce(jnp.add, [t.astype(f32) for t in terms]).astype(bf16)
    gate_input = jnp.concatenate(gather(gate_own, "dp", dp), axis=0).astype(f32)

    memory_read = lax.dot_general(
        spread_all, value_cols, (((0,), (0,)), ((), ())), preferred_element_type=f32
    )
    sigmoid_v = jax.nn.sigmoid(gate_input)
    gate_value = gate_input * sigmoid_v
    gate_slope = sigmoid_v * (1.0 + gate_input * (1.0 - sigmoid_v))
    upstream = grad_out_all.astype(f32)
    mem_grad = (upstream * gate_value).astype(bf16)
    gate_grad_in = (upstream * memory_read * gate_slope).astype(bf16)
    branch_out = (memory_read[:tokens] * gate_value[:tokens]).astype(bf16)

    value_term = jnp.dot(spread_all[: table * sub], mem_grad, preferred_element_type=f32)
    back = swap_table(value_term.astype(bf16).reshape(table, sub, cols), table)
    back = jnp.concatenate(back, axis=0)
    back = jnp.stack([block(back, k) for k in order("table", table)], axis=1)
    rows_back = gather(back.reshape(sub, width), "dp", dp)
    grad_values = placed(
        [r.astype(f32) for r in rows_back], order("dp", dp)
    ).reshape(rows_here, width)

    grad_hidden = return_hidden(gate_grad_in, weight_parts, dp, table, tokens, cols)

    if len(hidden_parts) == 2:
        core = here % 2
        hidden_abs = [jnp.where(core == j, *hidden_parts) for j in range(2)]
    else:
        hidden_abs = hidden_parts
    grad_gate = jnp.concatenate(
        [
            lax.dot_general(h, gate_grad_in, (((0,), (0,)), ((), ())), preferred_element_type=f32)
            for h in hidden_abs
        ],
        axis=0,
    )

    affinity_all = lax.dot_general(
        mem_grad[:tokens], value_cols, (((1,), (1,)), ((), ())), preferred_element_type=f32
    )
    own_rows = jnp.pad(moved_row(pick_rows), ((0, 0), (0, 128 - picks)))
    affinity = pick(affinity_all, own_rows)[:, :picks]
    if table // 2 <= DIRECT:
        affinity = affinity + hop(affinity, "table", table, 1)
        affinity = functools.reduce(
            jnp.add, [affinity] + [hop(affinity, "table", table, 2 * k) for k in range(1, table // 2)]
        )
    else:
        affinity = lax.psum(affinity, "table")
    grad_scores = weights * (affinity - jnp.sum(weights * affinity, axis=1, keepdims=True))
    return (branch_out, grad_hidden, grad_gate, grad_values, grad_scores)


def solution(mesh):
    split = P("dp", "table")
    return jax.shard_map(
        functools.partial(local, mesh.shape["dp"], mesh.shape["table"]),
        mesh=mesh,
        in_specs=(split, split, P("table", None), P("dp", None), P("dp", None), split),
        out_specs=(split, split, split, P("table", None), P("dp", None)),
        check_vma=False,
    )
```

```python
import functools

import jax
import jax.numpy as jnp
from jax import lax
from jax.experimental import pallas as pl
from jax.experimental.pallas import tpu as pltpu
from jax.sharding import Mesh
from jax.sharding import PartitionSpec as P

DIRECT = 4
TABLE = ("pair", "core")


def block(x, index):
    return lax.dynamic_index_in_dim(x, index, 0, keepdims=False)


def placed(pieces, indices):
    out = jnp.zeros((len(pieces),) + pieces[0].shape, pieces[0].dtype)
    for piece, index in zip(pieces, indices):
        out = lax.dynamic_update_index_in_dim(out, piece, index, 0)
    return out


def hop(x, axis, size, mask):
    return lax.ppermute(x, axis, [(i, i ^ mask) for i in range(size)])


def order(axis, size):
    return [lax.axis_index(axis) ^ k for k in range(size)]


def gather(x, axis, size):
    if size <= DIRECT:
        return [x] + [hop(x, axis, size, k) for k in range(1, size)]
    whole = lax.all_gather(x, axis, axis=0)
    return [block(whole, k) for k in order(axis, size)]


def swap(pieces, axis, size):
    if size <= DIRECT:
        return [pieces[0]] + [hop(pieces[k], axis, size, k) for k in range(1, size)]
    ids = order(axis, size)
    whole = lax.all_to_all(placed(pieces, ids), axis, split_axis=0, concat_axis=0)
    return [block(whole, k) for k in ids]


def exchange(x, axis):
    return lax.all_to_all(x, axis, split_axis=0, concat_axis=0, tiled=True)


def total(terms):
    return functools.reduce(jnp.add, [t.astype(jnp.float32) for t in terms])


def spread_kernel(rows_ref, weights_ref, out_ref):
    tile = 32
    tokens = rows_ref.shape[1]

    def step(i, carry):
        base = pl.multiple_of(i * tile, tile)
        here = lax.broadcasted_iota(jnp.int32, (tile, tokens), 0) + base
        total = jnp.zeros((tile, tokens), jnp.float32)
        for k in range(rows_ref.shape[0]):
            hit = rows_ref[k : k + 1, :] == here
            total = jnp.where(hit, weights_ref[k : k + 1, :], total)
        out_ref[pl.ds(base, tile), :] = total.astype(out_ref.dtype)
        return carry

    lax.fori_loop(0, out_ref.shape[0] // tile, step, 0)


def spread(rows, weights, row_total):
    picks, tokens = rows.shape
    width = min(tokens, 512)
    return pl.pallas_call(
        spread_kernel,
        grid=(tokens // width,),
        in_specs=[pl.BlockSpec((picks, width), lambda i: (0, i))] * 2,
        out_specs=pl.BlockSpec((row_total, width), lambda i: (0, i)),
        out_shape=jax.ShapeDtypeStruct((row_total, tokens), jnp.bfloat16),
        compiler_params=pltpu.CompilerParams(vmem_limit_bytes=16 << 20),
        cost_estimate=pl.CostEstimate(
            flops=2 * picks * tokens * row_total,
            bytes_accessed=2 * tokens * row_total,
            transcendentals=0,
        ),
    )(rows, weights)


def pick_kernel(table_ref, rows_ref, out_ref):
    lanes = 128
    rows = rows_ref[...]
    inner = rows & (lanes - 1)
    outer = rows >> 7
    total = jnp.zeros(out_ref.shape, jnp.float32)
    for j in range(table_ref.shape[1] // lanes):
        part = table_ref[:, j * lanes : (j + 1) * lanes]
        found = jnp.take_along_axis(part, inner, axis=1)
        total = jnp.where(outer == j, found, total)
    out_ref[...] = total


def pick(table, rows):
    return pl.pallas_call(
        pick_kernel,
        out_shape=jax.ShapeDtypeStruct(rows.shape, jnp.float32),
        cost_estimate=pl.CostEstimate(
            flops=rows.size * 16, bytes_accessed=4 * table.size, transcendentals=0
        ),
    )(table, rows)


def pick_weights(pick_scores):
    row_max = jnp.max(pick_scores, axis=1, keepdims=True)
    exponent = jnp.exp(pick_scores - row_max)
    return exponent / jnp.sum(exponent, axis=1, keepdims=True)


def contract(a, b, dim_a, dim_b):
    return lax.dot_general(
        a, b, (((dim_a,), (dim_b,)), ((), ())), preferred_element_type=jnp.float32
    )


def local_general(dp, pairs, hidden_in, gate_weight, values, pick_rows, pick_scores, grad_out):
    tokens, cols = hidden_in.shape
    rows_here, width = values.shape
    picks = pick_rows.shape[1]
    table = 2 * pairs
    sub = rows_here // dp
    me, pair, core = (lax.axis_index(a) for a in ("dp",) + TABLE)
    here = 2 * pair + core
    f32, bf16 = jnp.float32, jnp.bfloat16

    wide = lax.all_gather(hidden_in, TABLE, axis=1, tiled=True)
    wide = wide.reshape(tokens, dp, table * cols // dp).transpose(1, 0, 2)
    hidden_all = exchange(wide, "dp").reshape(dp * tokens, -1)

    weights = pick_weights(pick_scores)
    weights_bf = weights.astype(bf16)
    small = jnp.concatenate([weights_bf, (pick_rows >> 5).astype(bf16), (pick_rows & 31).astype(bf16)], axis=1)
    small = small.T.reshape(-1, cols)
    sent = lax.all_gather(jnp.concatenate([grad_out, small], axis=0), "dp", axis=0)
    grad_out_all = sent[:, :tokens].reshape(dp * tokens, cols)
    small = sent[:, tokens:].reshape(dp, 3, picks, tokens).transpose(1, 2, 0, 3)
    small = small.reshape(3, picks, dp * tokens).astype(f32)
    rows_all = small[1].astype(jnp.int32) * 32 + small[2].astype(jnp.int32)

    def moved_row(row):
        return ((row // rows_here) ^ here) * rows_here + row % rows_here

    spread_all = spread(moved_row(rows_all), small[0], rows_here * table)

    by_core = values.reshape(rows_here, pairs, 2, cols).transpose(2, 1, 0, 3)
    mine = block(by_core, core)
    other = hop(block(by_core, 1 - core), "core", 2, 1)
    value_sent = [
        jnp.concatenate([block(mine, z), block(other, z)], axis=0) for z in order("pair", pairs)
    ]
    value_cols = jnp.concatenate(swap(value_sent, "pair", pairs), axis=0)

    partial_gate = contract(hidden_all, gate_weight, 1, 0).astype(bf16)
    terms = exchange(partial_gate.reshape(dp, tokens, cols), "dp")
    gate_own = total([terms[k] for k in range(dp)]).astype(bf16)
    gate_input = lax.all_gather(gate_own, "dp", axis=0, tiled=True).astype(f32)

    memory_read = contract(spread_all, value_cols, 0, 0)
    sigmoid_v = jax.nn.sigmoid(gate_input)
    gate_value = gate_input * sigmoid_v
    gate_slope = sigmoid_v * (1.0 + gate_input * (1.0 - sigmoid_v))
    upstream = grad_out_all.astype(f32)
    mem_grad = (upstream * gate_value).astype(bf16)
    gate_grad_in = (upstream * memory_read * gate_slope).astype(bf16)

    def own(x):
        return block(x.reshape(dp, tokens, cols), me)

    branch_out = (own(memory_read) * own(gate_value)).astype(bf16)

    input_term = contract(gate_grad_in, gate_weight, 1, 1).astype(bf16)
    input_got = exchange(input_term.reshape(dp, tokens, -1), "dp")

    spread_parts = spread_all.reshape(pairs, 2, dp, sub, dp * tokens)
    part = jnp.concatenate(
        [
            lax.dynamic_slice(
                spread_parts, (z ^ pair, 0, me, 0, 0), (1, 2, 1, sub, dp * tokens)
            ).reshape(2 * sub, dp * tokens)
            for z in range(pairs)
        ],
        axis=0,
    )
    value_term = contract(part, mem_grad, 1, 0).astype(bf16).reshape(pairs, 2, sub, cols)
    value_other = hop(value_term[:, 1], "core", 2, 1)

    affinity_all = contract(own(mem_grad), value_cols, 1, 1)
    own_rows = jnp.pad(moved_row(pick_rows), ((0, 0), (0, 128 - picks)))
    affinity = pick(affinity_all, own_rows)[:, :picks]
    affinity = affinity + hop(affinity, "core", 2, 1)
    high = affinity.astype(bf16)
    low = (affinity - high.astype(f32)).astype(bf16)
    parts = jnp.concatenate([high, low], axis=1).reshape(-1, cols)

    back = exchange(
        jnp.concatenate(
            [value_term[:, 0], value_other, jnp.broadcast_to(parts, (pairs,) + parts.shape)], axis=1
        ),
        "pair",
    )
    affinity = back[:, 2 * sub :].reshape(pairs, tokens, 2 * picks).astype(f32)
    affinity = jnp.sum(affinity[:, :, :picks] + affinity[:, :, picks:], axis=0)
    grad_scores = weights * (affinity - jnp.sum(weights * affinity, axis=1, keepdims=True))

    first, second = back[:, :sub], back[:, sub : 2 * sub]
    back = jnp.stack(
        [jnp.where(core == 0, first, second), jnp.where(core == 0, second, first)], axis=1
    )
    back = back.transpose(2, 0, 1, 3).reshape(sub, width)
    grad_values = placed(
        [r.astype(f32) for r in gather(back, "dp", dp)], order("dp", dp)
    ).reshape(rows_here, width)

    wide = input_got.transpose(1, 0, 2).reshape(tokens, table, cols)
    input_terms = exchange(wide.transpose(1, 0, 2), TABLE)
    grad_hidden = total([input_terms[k] for k in range(table)]).astype(bf16)
    grad_gate = contract(hidden_all, gate_grad_in, 0, 0)
    return (branch_out, grad_hidden, grad_gate, grad_values, grad_scores)


def kernel_call(body, outs, *args, scratch=(), flops=0, after=()):
    count = len(args)
    size = sum(a.size * a.dtype.itemsize for a in args)
    size += sum(o.size * o.dtype.itemsize for o in outs)

    def whole_body(*refs):
        body(*refs[:count], *refs[count + len(after) :])

    vmem = pl.BlockSpec(memory_space=pltpu.VMEM)
    return pl.pallas_call(
        whole_body,
        in_specs=[pl.BlockSpec(memory_space=pltpu.SMEM)] + [vmem] * (count + len(after) - 1),
        out_specs=[vmem] * len(outs),
        out_shape=list(outs),
        scratch_shapes=list(scratch),
        compiler_params=pltpu.CompilerParams(vmem_limit_bytes=12 << 20),
        cost_estimate=pl.CostEstimate(flops=0, bytes_accessed=0, transcendentals=0),
    )(*args, *after)


def shape(dims, dtype=jnp.bfloat16):
    return jax.ShapeDtypeStruct(dims, dtype)


TOKEN = shape((8, 128), jnp.float32)


def sign(token):
    token[...] = jnp.zeros(token.shape, token.dtype)


def aligned(index, size):
    return pl.ds(pl.multiple_of(index * size, size), size)


def pack_rows(out_ref, first, x):
    count, lanes = x.shape
    per = out_ref.shape[1] // lanes
    for j in range(count):
        row, lane = (first + j) // per, (first + j) % per * lanes
        out_ref[row : row + 1, lane : lane + lanes] = x[j : j + 1, :]


def row_of(packed, j, lanes):
    per = packed.shape[1] // lanes
    return packed[j // per : j // per + 1, j % per * lanes : (j % per + 1) * lanes]


def prepare_body(ids, scores, rows, sent, weights, packed):
    x = scores[...]
    exponent = jnp.exp(x - jnp.max(x, axis=0, keepdims=True))
    w = exponent / jnp.sum(exponent, axis=0, keepdims=True)
    weights[...] = w
    packed[...] = jnp.zeros(packed.shape, packed.dtype)
    count = w.shape[0]
    pack_rows(packed, 0, w)
    pack_rows(packed, count, (rows[...] >> 5).astype(jnp.float32))
    pack_rows(packed, 2 * count, (rows[...] & 31).astype(jnp.float32))
    sent[...] = packed[...].astype(sent.dtype)


def moved(row, rows_here, pairs, pair, core):
    owner, inner = lax.div(row, rows_here), lax.rem(row, rows_here)
    return ((owner & 1) ^ core) * (pairs * rows_here) + ((owner >> 1) ^ pair) * rows_here + inner


def spread_body(picks, rows_here, ids, sent, out, part, token, rows, weights):
    sign(token)
    me, pair, core = ids[0], ids[1], ids[2]
    dp = sent.shape[0]
    tokens = rows.shape[1] // dp
    pairs = part.shape[0] // (2 * (rows_here // dp))
    for e in range(dp):
        packed = sent[e].astype(jnp.float32)
        span = slice(e * tokens, (e + 1) * tokens)
        for k in range(picks):
            weights[k : k + 1, span] = row_of(packed, k, tokens)
            high, low = row_of(packed, picks + k, tokens), row_of(packed, 2 * picks + k, tokens)
            rows[k : k + 1, span] = (high * 32.0 + low).astype(jnp.int32)
    rows[...] = moved(rows[...], rows_here, pairs, pair, core)
    tile = 32

    def step(i, carry):
        base = pl.multiple_of(i * tile, tile)
        here = lax.broadcasted_iota(jnp.int32, (tile, rows.shape[1]), 0) + base
        acc = jnp.zeros((tile, rows.shape[1]), jnp.float32)
        for k in range(picks):
            acc = jnp.where(rows[k : k + 1, :] == here, weights[k : k + 1, :], acc)
        out[pl.ds(base, tile), :] = acc.astype(out.dtype)
        return carry

    lax.fori_loop(0, out.shape[0] // tile, step, 0)
    sub = rows_here // dp
    for g in range(2):
        for z in range(pairs):
            at = (g * pairs + z) * rows_here + me * sub
            spot = (g * pairs + z) * sub
            part[spot : spot + sub, :] = out[pl.ds(pl.multiple_of(at, sub), sub), :]


def columns_body(ids, values, *outs):
    width = outs[0].shape[1]
    for k, out in enumerate(outs):
        out[...] = values[:, aligned(ids[1] ^ k, width)]


def halves_body(ids, *refs):
    pieces, (own, other) = refs[:-2], refs[-2:]
    rows, cols = pieces[0].shape[0], own.shape[1]
    for k, piece in enumerate(pieces):
        span = slice(k * rows, (k + 1) * rows)
        own[span, :] = piece[:, aligned(ids[2], cols)]
        other[span, :] = piece[:, aligned(1 - ids[2], cols)]


def dot(a, b, dim_a=1, dim_b=0):
    return lax.dot_general(
        a, b, (((dim_a,), (dim_b,)), ((), ())), preferred_element_type=jnp.float32
    )


def gate_body(ids, *refs):
    weight, first, second, stage = refs[-4:]
    dp = (len(refs) - 4) // 2
    cols = weight.shape[1]
    own, other = weight[aligned(ids[2], cols), :], weight[aligned(1 - ids[2], cols), :]
    for k in range(dp):
        term = dot(refs[k][...], own) + dot(refs[dp + k][...], other)
        stage[ids[1] ^ k] = term.astype(stage.dtype)
    half = dp // 2
    rows = stage.shape[1]
    for e in range(half):
        first[e * rows : (e + 1) * rows, :] = stage[e]
        second[e * rows : (e + 1) * rows, :] = stage[half + e]


def add_body(ids, a, a_got, b, b_got, a_keep, b_keep, a_send, b_send):
    f32 = jnp.float32
    for x, got, keep, send in ((a, a_got, a_keep, a_send), (b, b_got, b_keep, b_send)):
        keep[...] = (x[...].astype(f32) + got[...].astype(f32)).astype(keep.dtype)
        send[...] = keep[...]


def gate_value_of(stage, a0, a1, b0, b1):
    half = a0.shape[0]
    stage[:half, :] = a0[...].astype(jnp.float32) + a1[...].astype(jnp.float32)
    stage[half:, :] = b0[...].astype(jnp.float32) + b1[...].astype(jnp.float32)


def values_body(ids, a0, a1, b0, b1, grad_out, part, mem_grad, factor, value_own, keep, send, token, stage):
    tokens = value_own.shape[0]
    gate_value_of(stage, a0, a1, b0, b1)
    for k in range(grad_out.shape[0]):
        span = aligned(ids[0] ^ k, tokens)
        gate = stage[span, :]
        s = jax.nn.sigmoid(gate)
        upstream = grad_out[ids[0] ^ k].astype(jnp.float32)
        mem_grad[span, :] = (upstream * (gate * s)).astype(mem_grad.dtype)
        factor[span, :] = upstream * (s * (1.0 + gate * (1.0 - s)))
        if k == 0:
            value_own[...] = gate * s
    half = keep.shape[0]
    term = dot(part[...], mem_grad[...])
    keep[...] = term[:half].astype(keep.dtype)
    send[...] = term[half:].astype(send.dtype)
    sign(token)


def messages_body(ids, keep, got, *refs):
    messages, token = refs[:-1], refs[-1]
    sign(token)
    sub = messages[0].shape[0] // 2
    for z, message in enumerate(messages):
        message[:sub, :] = keep[z * sub : (z + 1) * sub, :]
        message[sub:, :] = got[z * sub : (z + 1) * sub, :]


def grads_body(ids, factor, value_own, spread_ref, own, other, weight, gate_grad, branch, term):
    tokens = branch.shape[0]
    half = own.shape[0]
    for k in range(factor.shape[0] // tokens):
        span = aligned(ids[0] ^ k, tokens)
        memory = dot(spread_ref[:half, span], own[...], 0, 0)
        memory = memory + dot(spread_ref[half:, span], other[...], 0, 0)
        gate_grad[span, :] = (factor[span, :] * memory).astype(gate_grad.dtype)
        if k == 0:
            branch[...] = (memory * value_own[...]).astype(branch.dtype)
    across = weight[aligned(1 - ids[2], weight.shape[1]), :]
    term[...] = dot(gate_grad[...], across, 1, 1).astype(term.dtype)


def affinity_body(rows_here, ids, mem_grad, own, other, rows, out, packed):
    f32 = jnp.float32
    half, tokens = own.shape[0], rows.shape[1]
    count = rows.shape[0]
    pairs = half // rows_here
    at = moved(rows[...], rows_here, pairs, ids[1], ids[2])
    at = jnp.concatenate([at] * (tokens // count), axis=0).T
    inner, outer = at & 127, at >> 7
    grads = mem_grad[aligned(ids[0], tokens), :]
    found = jnp.zeros(at.shape, f32)
    blocks = half // 128
    for j, table in enumerate((own, other)):
        all_rows = dot(grads, table[...], 1, 1)
        for i in range(blocks):
            hit = jnp.take_along_axis(all_rows[:, i * 128 : (i + 1) * 128], inner, axis=1)
            found = jnp.where(outer == j * blocks + i, hit, found)
    affinity = found.T[:count]
    high = affinity.astype(jnp.bfloat16).astype(f32)
    pack_rows(packed, 0, high)
    pack_rows(packed, count, affinity - high)
    out[...] = packed[...].astype(out.dtype)


def inputs_body(ids, gate_grad, weight, arrived, *refs):
    inputs = refs[:-1]
    sign(refs[-1])
    tokens, cols = inputs[0].shape
    own = weight[aligned(ids[2], cols), :]
    for k, out in enumerate(inputs):
        span = aligned(ids[0] ^ k, tokens)
        term = dot(gate_grad[span, :], own, 1, 1) + arrived[span, :].astype(jnp.float32)
        out[...] = term.astype(out.dtype)


def owners_body(ids, *refs):
    f32 = jnp.float32
    count = (len(refs) - 4) // 2
    pieces, outs, token, stage = refs[:count], refs[count + 2 : -2], refs[-2], refs[-1]
    sign(token)
    whole = refs[count][...].astype(f32) + refs[count + 1][...].astype(f32)
    half = whole.shape[0] // 2
    whole = whole[:half] + whole[half:]
    high = whole.astype(jnp.bfloat16).astype(f32)
    whole = jnp.concatenate([high, whole - high], axis=0).astype(jnp.bfloat16)
    rows = pieces[0].shape[0]
    for k, piece in enumerate(pieces):
        stage[ids[0] ^ k] = piece[...]
    for i, out in enumerate(outs):
        out[:rows, :] = stage[ids[1] ^ i]
        out[rows:, :] = whole


def finish_body(ids, *refs):
    weights, out, grads = refs[-3:]
    f32 = jnp.float32
    whole = refs[0][...].astype(f32)
    for piece in refs[1:-3]:
        whole = whole + piece[...].astype(f32)
    tokens = out.shape[0]
    out[...] = whole[:tokens].astype(out.dtype)
    whole = whole[tokens:]
    half = whole.shape[0] // 2
    whole = whole[:half] + whole[half:]
    w = weights[...]
    count, lanes = w.shape
    affinity = jnp.concatenate([row_of(whole, k, lanes) for k in range(count)], axis=0)
    grads[...] = w * (affinity - jnp.sum(w * affinity, axis=0, keepdims=True))


def rows_body(ids, *refs):
    back, out = refs[:-1], refs[-1]
    height, cols = back[0].shape
    sub = height // 2
    for e in range(out.shape[0]):
        for z, piece in enumerate(back):
            at = 2 * (ids[1] ^ z)
            out[e, :, aligned(at + ids[2], cols)] = piece[:sub, :]
            out[e, :, aligned(at + 1 - ids[2], cols)] = piece[sub:, :]


def widen_body(x, out):
    out[...] = x[0].astype(out.dtype)


def widen(x):
    count, rows, cols = x.shape
    return pl.pallas_call(
        widen_body,
        grid=(count,),
        in_specs=[pl.BlockSpec((1, rows, cols), lambda i: (i, 0, 0))],
        out_specs=pl.BlockSpec((rows, cols), lambda i: (i, 0)),
        out_shape=shape((count * rows, cols), jnp.float32),
        compiler_params=pltpu.CompilerParams(vmem_limit_bytes=16 << 20),
        cost_estimate=pl.CostEstimate(flops=0, bytes_accessed=6 * x.size, transcendentals=0),
    )(x)


def gate_grads_body(ids, *refs):
    gate_grad, out = refs[-2:]
    dp = (len(refs) - 2) // 2
    tokens, cols = refs[0].shape
    for j in range(2):
        acc = jnp.zeros((cols, out.shape[1]), jnp.float32)
        for k in range(dp):
            grads = gate_grad[aligned(ids[1] ^ k, tokens), :]
            acc = acc + dot(refs[j * dp + k][...], grads, 0, 0)
        out[aligned(ids[2] ^ j, cols), :] = acc


def local_square(dp, pairs, hidden_in, gate_weight, values, pick_rows, pick_scores, grad_out):
    tokens, cols = hidden_in.shape
    rows_here, width = values.shape
    picks = pick_rows.shape[1]
    sub = rows_here // dp
    f32 = jnp.float32
    me, pair, core = (lax.axis_index(a) for a in ("dp",) + TABLE)
    ids = jnp.stack([me, pair, core]).astype(jnp.int32)
    every = dp * tokens

    mine = []
    for k in range(dp):
        perm = [
            ((e * pairs + z) * 2 + h, (z * pairs + (e ^ k)) * 2 + h)
            for e in range(dp)
            for z in range(pairs)
            for h in range(2)
        ]
        mine.append(lax.ppermute(hidden_in, ("dp",) + TABLE, perm))
    other = [hop(x, "core", 2, 1) for x in mine]
    pieces = mine + other

    rows_t = pick_rows.T
    small = -(-3 * picks * tokens // cols // 16) * 16
    sent, weights_t = kernel_call(
        prepare_body,
        [shape((small, cols)), shape((picks, tokens), f32)],
        ids, pick_scores.T, rows_t,
        scratch=[pltpu.VMEM((small, cols), f32)],
    )
    sent = lax.all_gather(sent, "dp", axis=0)
    upstream = lax.all_gather(grad_out, "dp", axis=0)
    first, second = kernel_call(
        gate_body,
        [shape((every // 2, cols))] * 2,
        ids, *pieces, gate_weight,
        scratch=[pltpu.VMEM((dp, tokens, cols), jnp.bfloat16)],
        flops=1 << 29,
        after=[sent],
    )
    spread_all, spread_part, token = kernel_call(
        functools.partial(spread_body, picks, rows_here),
        [shape((2 * pairs * rows_here, every)), shape((2 * pairs * sub, every)), TOKEN],
        ids, sent,
        scratch=[pltpu.VMEM((picks, every), jnp.int32), pltpu.VMEM((picks, every), f32)],
        flops=1 << 27,
    )
    value_sent = kernel_call(
        columns_body, [shape((rows_here, 2 * cols))] * pairs, ids, values, after=mine + [sent]
    )
    value_got = swap(value_sent, "pair", pairs)
    first, second, *added = kernel_call(
        add_body,
        [shape((every // 2, cols))] * 4,
        ids, first, hop(first, "dp", dp, 1), second, hop(second, "dp", dp, 2),
        after=[token, value_got[1]],
    )
    gates = [first, hop(added[0], "dp", dp, 2), second, hop(added[1], "dp", dp, 1)]

    mem_grad, factor, value_part, keep, send, token = kernel_call(
        values_body,
        [shape((every, cols)), shape((every, cols), f32), shape((tokens, cols), f32)]
        + [shape((pairs * sub, cols))] * 2
        + [TOKEN],
        ids, *gates, upstream, spread_part,
        scratch=[pltpu.VMEM((every, cols), f32)], flops=1 << 28,
    )
    *messages, sent_on = kernel_call(
        messages_body, [shape((2 * sub, cols))] * pairs + [TOKEN], ids, keep, hop(send, "core", 2, 1)
    )

    value_own, value_send = kernel_call(
        halves_body, [shape((pairs * rows_here, cols))] * 2, ids, *value_got, after=[token]
    )
    value_other = hop(value_send, "core", 2, 1)

    extra = 2 * picks * tokens // cols
    gate_grad, branch_out, term = kernel_call(
        grads_body,
        [shape((every, cols)), shape((tokens, cols)), shape((every, cols))],
        ids, factor, value_part, spread_all, value_own, value_other, gate_weight,
        flops=1 << 30, after=[sent_on],
    )
    *sends, token = kernel_call(
        inputs_body,
        [shape((tokens, cols))] * dp + [TOKEN],
        ids, gate_grad, gate_weight, hop(term, "core", 2, 1),
        flops=1 << 28,
    )
    grad_gate = kernel_call(
        gate_grads_body, [shape((2 * cols, cols), f32)], ids, *pieces, gate_grad,
        flops=1 << 29, after=[token],
    )[0]
    affinity = kernel_call(
        functools.partial(affinity_body, rows_here),
        [shape((extra, cols))],
        ids, mem_grad, value_own, value_other, rows_t,
        scratch=[pltpu.VMEM((extra, cols), f32)], flops=1 << 27, after=[token],
    )[0]
    inputs = swap(sends, "dp", dp)
    affinity_got = hop(affinity, "core", 2, 1)
    *inputs, token = kernel_call(
        owners_body,
        [shape((tokens + extra, cols))] * pairs + [TOKEN],
        ids, *inputs, affinity, affinity_got,
        scratch=[pltpu.VMEM((dp, tokens, cols), jnp.bfloat16)],
    )
    grad_hidden, grad_scores = kernel_call(
        finish_body,
        [shape((tokens, cols)), shape((picks, tokens), f32)],
        ids, *swap(inputs, "pair", pairs), weights_t,
    )

    back = swap(messages, "pair", pairs)
    rows = kernel_call(rows_body, [shape((dp, sub, width))], ids, *back, after=[token])[0]
    grad_values = widen(exchange(rows, "dp"))
    return (branch_out, grad_hidden, grad_gate, grad_values, grad_scores.T)


def local(dp, pairs, *args):
    tokens, cols = args[0].shape
    square = dp == pairs == DIRECT and tokens == 128 and cols == 4 * tokens
    return (local_square if square else local_general)(dp, pairs, *args)


def solution(mesh):
    dp, table = mesh.shape["dp"], mesh.shape["table"]
    pairs = Mesh(mesh.devices.reshape(dp, table // 2, 2), ("dp",) + TABLE)
    split, rows, tokens = P("dp", TABLE), P(TABLE, None), P("dp", None)
    return jax.shard_map(
        functools.partial(local, dp, table // 2),
        mesh=pairs,
        in_specs=(split, split, rows, tokens, tokens, split),
        out_specs=(split, split, split, rows, tokens),
        check_vma=False,
    )
```

```python
import functools

import jax
import jax.numpy as jnp
from jax import lax
from jax.experimental import pallas as pl
from jax.experimental.pallas import tpu as pltpu
from jax.sharding import Mesh
from jax.sharding import PartitionSpec as P

DIRECT = 4
TABLE = ("pair", "core")


def block(x, index):
    return lax.dynamic_index_in_dim(x, index, 0, keepdims=False)


def placed(pieces, indices):
    out = jnp.zeros((len(pieces),) + pieces[0].shape, pieces[0].dtype)
    for piece, index in zip(pieces, indices):
        out = lax.dynamic_update_index_in_dim(out, piece, index, 0)
    return out


def hop(x, axis, size, mask):
    return lax.ppermute(x, axis, [(i, i ^ mask) for i in range(size)])


def order(axis, size):
    return [lax.axis_index(axis) ^ k for k in range(size)]


def gather(x, axis, size):
    if size <= DIRECT:
        return [x] + [hop(x, axis, size, k) for k in range(1, size)]
    whole = lax.all_gather(x, axis, axis=0)
    return [block(whole, k) for k in order(axis, size)]


def swap(pieces, axis, size):
    if size <= DIRECT:
        return [pieces[0]] + [hop(pieces[k], axis, size, k) for k in range(1, size)]
    ids = order(axis, size)
    whole = lax.all_to_all(placed(pieces, ids), axis, split_axis=0, concat_axis=0)
    return [block(whole, k) for k in ids]


def exchange(x, axis):
    return lax.all_to_all(x, axis, split_axis=0, concat_axis=0, tiled=True)


def total(terms):
    return functools.reduce(jnp.add, [t.astype(jnp.float32) for t in terms])


def spread_kernel(rows_ref, weights_ref, out_ref):
    tile = 32
    tokens = rows_ref.shape[1]

    def step(i, carry):
        base = pl.multiple_of(i * tile, tile)
        here = lax.broadcasted_iota(jnp.int32, (tile, tokens), 0) + base
        total = jnp.zeros((tile, tokens), jnp.float32)
        for k in range(rows_ref.shape[0]):
            hit = rows_ref[k : k + 1, :] == here
            total = jnp.where(hit, weights_ref[k : k + 1, :], total)
        out_ref[pl.ds(base, tile), :] = total.astype(out_ref.dtype)
        return carry

    lax.fori_loop(0, out_ref.shape[0] // tile, step, 0)


def spread(rows, weights, row_total):
    picks, tokens = rows.shape
    width = min(tokens, 512)
    return pl.pallas_call(
        spread_kernel,
        grid=(tokens // width,),
        in_specs=[pl.BlockSpec((picks, width), lambda i: (0, i))] * 2,
        out_specs=pl.BlockSpec((row_total, width), lambda i: (0, i)),
        out_shape=jax.ShapeDtypeStruct((row_total, tokens), jnp.bfloat16),
        compiler_params=pltpu.CompilerParams(vmem_limit_bytes=16 << 20),
        cost_estimate=pl.CostEstimate(
            flops=2 * picks * tokens * row_total,
            bytes_accessed=2 * tokens * row_total,
            transcendentals=0,
        ),
    )(rows, weights)


def pick_kernel(table_ref, rows_ref, out_ref):
    lanes = 128
    rows = rows_ref[...]
    inner = rows & (lanes - 1)
    outer = rows >> 7
    total = jnp.zeros(out_ref.shape, jnp.float32)
    for j in range(table_ref.shape[1] // lanes):
        part = table_ref[:, j * lanes : (j + 1) * lanes]
        found = jnp.take_along_axis(part, inner, axis=1)
        total = jnp.where(outer == j, found, total)
    out_ref[...] = total


def pick(table, rows):
    return pl.pallas_call(
        pick_kernel,
        out_shape=jax.ShapeDtypeStruct(rows.shape, jnp.float32),
        cost_estimate=pl.CostEstimate(
            flops=rows.size * 16, bytes_accessed=4 * table.size, transcendentals=0
        ),
    )(table, rows)


def pick_weights(pick_scores):
    row_max = jnp.max(pick_scores, axis=1, keepdims=True)
    exponent = jnp.exp(pick_scores - row_max)
    return exponent / jnp.sum(exponent, axis=1, keepdims=True)


def contract(a, b, dim_a, dim_b):
    return lax.dot_general(
        a, b, (((dim_a,), (dim_b,)), ((), ())), preferred_element_type=jnp.float32
    )


def local_general(dp, pairs, hidden_in, gate_weight, values, pick_rows, pick_scores, grad_out):
    tokens, cols = hidden_in.shape
    rows_here, width = values.shape
    picks = pick_rows.shape[1]
    table = 2 * pairs
    sub = rows_here // dp
    me, pair, core = (lax.axis_index(a) for a in ("dp",) + TABLE)
    here = 2 * pair + core
    f32, bf16 = jnp.float32, jnp.bfloat16

    wide = lax.all_gather(hidden_in, TABLE, axis=1, tiled=True)
    wide = wide.reshape(tokens, dp, table * cols // dp).transpose(1, 0, 2)
    hidden_all = exchange(wide, "dp").reshape(dp * tokens, -1)

    weights = pick_weights(pick_scores)
    weights_bf = weights.astype(bf16)
    small = jnp.concatenate([weights_bf, (pick_rows >> 5).astype(bf16), (pick_rows & 31).astype(bf16)], axis=1)
    small = small.T.reshape(-1, cols)
    sent = lax.all_gather(jnp.concatenate([grad_out, small], axis=0), "dp", axis=0)
    grad_out_all = sent[:, :tokens].reshape(dp * tokens, cols)
    small = sent[:, tokens:].reshape(dp, 3, picks, tokens).transpose(1, 2, 0, 3)
    small = small.reshape(3, picks, dp * tokens).astype(f32)
    rows_all = small[1].astype(jnp.int32) * 32 + small[2].astype(jnp.int32)

    def moved_row(row):
        return ((row // rows_here) ^ here) * rows_here + row % rows_here

    spread_all = spread(moved_row(rows_all), small[0], rows_here * table)

    by_core = values.reshape(rows_here, pairs, 2, cols).transpose(2, 1, 0, 3)
    mine = block(by_core, core)
    other = hop(block(by_core, 1 - core), "core", 2, 1)
    value_sent = [
        jnp.concatenate([block(mine, z), block(other, z)], axis=0) for z in order("pair", pairs)
    ]
    value_cols = jnp.concatenate(swap(value_sent, "pair", pairs), axis=0)

    partial_gate = contract(hidden_all, gate_weight, 1, 0).astype(bf16)
    terms = exchange(partial_gate.reshape(dp, tokens, cols), "dp")
    gate_own = total([terms[k] for k in range(dp)]).astype(bf16)
    gate_input = lax.all_gather(gate_own, "dp", axis=0, tiled=True).astype(f32)

    memory_read = contract(spread_all, value_cols, 0, 0)
    sigmoid_v = jax.nn.sigmoid(gate_input)
    gate_value = gate_input * sigmoid_v
    gate_slope = sigmoid_v * (1.0 + gate_input * (1.0 - sigmoid_v))
    upstream = grad_out_all.astype(f32)
    mem_grad = (upstream * gate_value).astype(bf16)
    gate_grad_in = (upstream * memory_read * gate_slope).astype(bf16)

    def own(x):
        return block(x.reshape(dp, tokens, cols), me)

    branch_out = (own(memory_read) * own(gate_value)).astype(bf16)

    input_term = contract(gate_grad_in, gate_weight, 1, 1).astype(bf16)
    input_got = exchange(input_term.reshape(dp, tokens, -1), "dp")

    spread_parts = spread_all.reshape(pairs, 2, dp, sub, dp * tokens)
    part = jnp.concatenate(
        [
            lax.dynamic_slice(
                spread_parts, (z ^ pair, 0, me, 0, 0), (1, 2, 1, sub, dp * tokens)
            ).reshape(2 * sub, dp * tokens)
            for z in range(pairs)
        ],
        axis=0,
    )
    value_term = contract(part, mem_grad, 1, 0).astype(bf16).reshape(pairs, 2, sub, cols)
    value_other = hop(value_term[:, 1], "core", 2, 1)

    affinity_all = contract(own(mem_grad), value_cols, 1, 1)
    own_rows = jnp.pad(moved_row(pick_rows), ((0, 0), (0, 128 - picks)))
    affinity = pick(affinity_all, own_rows)[:, :picks]
    affinity = affinity + hop(affinity, "core", 2, 1)
    high = affinity.astype(bf16)
    low = (affinity - high.astype(f32)).astype(bf16)
    parts = jnp.concatenate([high, low], axis=1).reshape(-1, cols)

    back = exchange(
        jnp.concatenate(
            [value_term[:, 0], value_other, jnp.broadcast_to(parts, (pairs,) + parts.shape)], axis=1
        ),
        "pair",
    )
    affinity = back[:, 2 * sub :].reshape(pairs, tokens, 2 * picks).astype(f32)
    affinity = jnp.sum(affinity[:, :, :picks] + affinity[:, :, picks:], axis=0)
    grad_scores = weights * (affinity - jnp.sum(weights * affinity, axis=1, keepdims=True))

    first, second = back[:, :sub], back[:, sub : 2 * sub]
    back = jnp.stack(
        [jnp.where(core == 0, first, second), jnp.where(core == 0, second, first)], axis=1
    )
    back = back.transpose(2, 0, 1, 3).reshape(sub, width)
    grad_values = placed(
        [r.astype(f32) for r in gather(back, "dp", dp)], order("dp", dp)
    ).reshape(rows_here, width)

    wide = input_got.transpose(1, 0, 2).reshape(tokens, table, cols)
    input_terms = exchange(wide.transpose(1, 0, 2), TABLE)
    grad_hidden = total([input_terms[k] for k in range(table)]).astype(bf16)
    grad_gate = contract(hidden_all, gate_grad_in, 0, 0)
    return (branch_out, grad_hidden, grad_gate, grad_values, grad_scores)


def kernel_call(body, outs, *args, scratch=(), flops=0, after=()):
    count = len(args)
    size = sum(a.size * a.dtype.itemsize for a in args)
    size += sum(o.size * o.dtype.itemsize for o in outs)

    def whole_body(*refs):
        body(*refs[:count], *refs[count + len(after) :])

    vmem = pl.BlockSpec(memory_space=pltpu.VMEM)
    return pl.pallas_call(
        whole_body,
        in_specs=[pl.BlockSpec(memory_space=pltpu.SMEM)] + [vmem] * (count + len(after) - 1),
        out_specs=[vmem] * len(outs),
        out_shape=list(outs),
        scratch_shapes=list(scratch),
        compiler_params=pltpu.CompilerParams(vmem_limit_bytes=12 << 20),
        cost_estimate=pl.CostEstimate(flops=0, bytes_accessed=0, transcendentals=0),
    )(*args, *after)


def shape(dims, dtype=jnp.bfloat16):
    return jax.ShapeDtypeStruct(dims, dtype)


TOKEN = shape((8, 128), jnp.float32)


def sign(token):
    token[...] = jnp.zeros(token.shape, token.dtype)


def aligned(index, size):
    return pl.ds(pl.multiple_of(index * size, size), size)


def pack_rows(out_ref, first, x):
    count, lanes = x.shape
    per = out_ref.shape[1] // lanes
    for j in range(count):
        row, lane = (first + j) // per, (first + j) % per * lanes
        out_ref[row : row + 1, lane : lane + lanes] = x[j : j + 1, :]


def row_of(packed, j, lanes):
    per = packed.shape[1] // lanes
    return packed[j // per : j // per + 1, j % per * lanes : (j % per + 1) * lanes]


def prepare_body(ids, scores, rows, grad_out, sent, weights, packed):
    tokens = grad_out.shape[0]
    x = scores[...]
    exponent = jnp.exp(x - jnp.max(x, axis=0, keepdims=True))
    w = exponent / jnp.sum(exponent, axis=0, keepdims=True)
    weights[...] = w
    packed[...] = jnp.zeros(packed.shape, packed.dtype)
    count = w.shape[0]
    pack_rows(packed, 0, w)
    pack_rows(packed, count, (rows[...] >> 5).astype(jnp.float32))
    pack_rows(packed, 2 * count, (rows[...] & 31).astype(jnp.float32))
    sent[:tokens, :] = grad_out[...]
    sent[tokens:, :] = packed[...].astype(sent.dtype)


def moved(row, rows_here, pair, core):
    owner, inner = lax.div(row, rows_here), lax.rem(row, rows_here)
    return (owner ^ (2 * pair + core)) * rows_here + inner


def spread_body(picks, rows_here, ids, sent, out, part, rows, weights):
    me, pair, core = ids[0], ids[1], ids[2]
    dp = sent.shape[0]
    tokens = rows.shape[1] // dp
    pairs = part.shape[0] // (2 * (rows_here // dp))
    for e in range(dp):
        packed = sent[e, tokens:, :].astype(jnp.float32)
        span = slice(e * tokens, (e + 1) * tokens)
        for k in range(picks):
            weights[k : k + 1, span] = row_of(packed, k, tokens)
            high, low = row_of(packed, picks + k, tokens), row_of(packed, 2 * picks + k, tokens)
            rows[k : k + 1, span] = (high * 32.0 + low).astype(jnp.int32)
    rows[...] = moved(rows[...], rows_here, pair, core)
    tile = 32

    def step(i, carry):
        base = pl.multiple_of(i * tile, tile)
        here = lax.broadcasted_iota(jnp.int32, (tile, rows.shape[1]), 0) + base
        acc = jnp.zeros((tile, rows.shape[1]), jnp.float32)
        for k in range(picks):
            acc = jnp.where(rows[k : k + 1, :] == here, weights[k : k + 1, :], acc)
        out[pl.ds(base, tile), :] = acc.astype(out.dtype)
        return carry

    lax.fori_loop(0, out.shape[0] // tile, step, 0)
    sub = rows_here // dp
    for g in range(2):
        for z in range(pairs):
            at = (2 * z + g) * rows_here + me * sub
            spot = (g * pairs + z) * sub
            part[spot : spot + sub, :] = out[pl.ds(pl.multiple_of(at, sub), sub), :]


def columns_body(ids, values, own, other):
    rows, cols = values.shape[0], own.shape[1]
    for k in range(own.shape[0] // rows):
        span, at = slice(k * rows, (k + 1) * rows), 2 * (ids[1] ^ k)
        own[span, :] = values[:, aligned(at + ids[2], cols)]
        other[span, :] = values[:, aligned(at + 1 - ids[2], cols)]


def halves_body(ids, own, got, *outs):
    rows = outs[0].shape[0] // 2
    for k, out in enumerate(outs):
        span = slice(k * rows, (k + 1) * rows)
        out[:rows, :] = own[span, :]
        out[rows:, :] = got[span, :]


def dot(a, b, dim_a=1, dim_b=0):
    return lax.dot_general(
        a, b, (((dim_a,), (dim_b,)), ((), ())), preferred_element_type=jnp.float32
    )


def join_body(ids, *refs):
    pieces, out = refs[:-1], refs[-1]
    rows = pieces[0].shape[0]
    for k, piece in enumerate(pieces):
        out[k * rows : (k + 1) * rows, :] = piece[...]


def gate_body(ids, *refs):
    pieces, (others, weight, first, second, stage) = refs[:-5], refs[-5:]
    dp, rows = len(pieces), stage.shape[1]
    cols = weight.shape[1]
    own, other = weight[aligned(ids[2], cols), :], weight[aligned(1 - ids[2], cols), :]
    for k, piece in enumerate(pieces):
        term = dot(piece[...], own) + dot(others[k * rows : (k + 1) * rows, :], other)
        stage[ids[1] ^ k] = term.astype(stage.dtype)
    half = dp // 2
    for e in range(half):
        first[e * rows : (e + 1) * rows, :] = stage[e]
        second[e * rows : (e + 1) * rows, :] = stage[half + e]


def add_body(ids, a, a_got, b, b_got, a_keep, b_keep, a_send, b_send, token):
    sign(token)
    f32 = jnp.float32
    for x, got, keep, send in ((a, a_got, a_keep, a_send), (b, b_got, b_keep, b_send)):
        keep[...] = (x[...].astype(f32) + got[...].astype(f32)).astype(keep.dtype)
        send[...] = keep[...]


def gate_value_of(stage, a0, a1, b0, b1):
    half = a0.shape[0]
    stage[:half, :] = a0[...].astype(jnp.float32) + a1[...].astype(jnp.float32)
    stage[half:, :] = b0[...].astype(jnp.float32) + b1[...].astype(jnp.float32)


def values_body(ids, a0, a1, b0, b1, sent, part, mem_grad, factor, value_own, keep, send, token, stage):
    tokens = value_own.shape[0]
    gate_value_of(stage, a0, a1, b0, b1)
    for k in range(sent.shape[0]):
        span = aligned(ids[0] ^ k, tokens)
        gate = stage[span, :]
        s = jax.nn.sigmoid(gate)
        upstream = sent[ids[0] ^ k, :tokens, :].astype(jnp.float32)
        mem_grad[span, :] = (upstream * (gate * s)).astype(mem_grad.dtype)
        factor[span, :] = upstream * (s * (1.0 + gate * (1.0 - s)))
        if k == 0:
            value_own[...] = gate * s
    half = keep.shape[0]
    term = dot(part[...], mem_grad[...])
    keep[...] = term[:half].astype(keep.dtype)
    send[...] = term[half:].astype(send.dtype)
    sign(token)


def messages_body(ids, keep, got, *refs):
    messages, token = refs[:-1], refs[-1]
    sign(token)
    sub = messages[0].shape[0] // 2
    for z, message in enumerate(messages):
        message[:sub, :] = keep[z * sub : (z + 1) * sub, :]
        message[sub:, :] = got[z * sub : (z + 1) * sub, :]


def grads_body(ids, factor, value_own, spread_ref, *refs):
    values, (weight, gate_grad, branch, term) = refs[:-4], refs[-4:]
    tokens, rows = branch.shape[0], values[0].shape[0]
    for k in range(factor.shape[0] // tokens):
        span = aligned(ids[0] ^ k, tokens)
        memory = 0.0
        for i, piece in enumerate(values):
            memory = memory + dot(spread_ref[i * rows : (i + 1) * rows, span], piece[...], 0, 0)
        gate_grad[span, :] = (factor[span, :] * memory).astype(gate_grad.dtype)
        if k == 0:
            branch[...] = (memory * value_own[...]).astype(branch.dtype)
    across = weight[aligned(1 - ids[2], weight.shape[1]), :]
    term[...] = dot(gate_grad[...], across, 1, 1).astype(term.dtype)


def affinity_body(rows_here, ids, mem_grad, *refs):
    f32 = jnp.float32
    values, (rows, out, packed) = refs[:-3], refs[-3:]
    tokens = rows.shape[1]
    count = rows.shape[0]
    at = moved(rows[...], rows_here, ids[1], ids[2])
    at = jnp.concatenate([at] * (tokens // count), axis=0).T
    inner, outer = at & 127, at >> 7
    grads = mem_grad[aligned(ids[0], tokens), :]
    found = jnp.zeros(at.shape, f32)
    blocks = values[0].shape[0] // 128
    for j, table in enumerate(values):
        all_rows = dot(grads, table[...], 1, 1)
        for i in range(blocks):
            hit = jnp.take_along_axis(all_rows[:, i * 128 : (i + 1) * 128], inner, axis=1)
            found = jnp.where(outer == j * blocks + i, hit, found)
    affinity = found.T[:count]
    high = affinity.astype(jnp.bfloat16).astype(f32)
    pack_rows(packed, 0, high)
    pack_rows(packed, count, affinity - high)
    out[...] = packed[...].astype(out.dtype)


def inputs_body(ids, gate_grad, weight, arrived, affinity, *refs):
    outs, token = refs[:-1], refs[-1]
    sign(token)
    tokens, cols = outs[0].shape[0] - affinity.shape[0], outs[0].shape[1]
    own = weight[aligned(ids[2], cols), :]
    for i, out in enumerate(outs):
        span = aligned(ids[1] ^ i, tokens)
        term = dot(gate_grad[span, :], own, 1, 1) + arrived[span, :].astype(jnp.float32)
        out[:tokens, :] = term.astype(out.dtype)
        out[tokens:, :] = affinity[...]


def sums_body(ids, *refs):
    pieces, out, affinity = refs[:-2], refs[-2], refs[-1]
    whole = 0.0
    for piece in pieces:
        whole = whole + piece[...].astype(jnp.float32)
    tokens = out.shape[0]
    out[...] = whole[:tokens].astype(out.dtype)
    half = (whole.shape[0] - tokens) // 2
    affinity[...] = whole[tokens : tokens + half] + whole[tokens + half :]


def copy_body(ids, x, out):
    out[...] = x[...]


def scores_body(ids, own, got, weights, grads, token):
    sign(token)
    whole = own[...] + got[...]
    w = weights[...]
    count, lanes = w.shape
    affinity = jnp.concatenate([row_of(whole, k, lanes) for k in range(count)], axis=0)
    grads[...] = w * (affinity - jnp.sum(w * affinity, axis=0, keepdims=True))


def rows_body(ids, *refs):
    back, halves = refs[:-2], refs[-2:]
    cols = back[0].shape[1]
    sub, half = back[0].shape[0] // 2, halves[0].shape[0]
    for z, piece in enumerate(back):
        for j, out in enumerate(halves):
            at = 2 * (ids[1] ^ z)
            span = slice(j * half, (j + 1) * half)
            out[:, aligned(at + ids[2], cols)] = piece[span, :]
            out[:, aligned(at + 1 - ids[2], cols)] = piece[sub + j * half : sub + (j + 1) * half, :]


def pairs_body(ids, a, a_got, b, b_got, first, second):
    half = a.shape[0]
    for x, got, out in ((a, a_got, first), (b, b_got, second)):
        out[:half, :] = x[...]
        out[half:, :] = got[...]


def widen_body(ids, a, a_got, b, b_got, out, token):
    sign(token)
    half = a.shape[0] // 2
    for k in range(4):
        at = (ids[0] ^ k) * 2 * half
        first, second = (a_got if k & 2 else a), (b_got if k & 1 else b)
        i, j = k & 1, k >> 1
        spot = pl.ds(pl.multiple_of(at, half), half)
        out[spot, :] = first[i * half : (i + 1) * half, :].astype(out.dtype)
        spot = pl.ds(pl.multiple_of(at + half, half), half)
        out[spot, :] = second[j * half : (j + 1) * half, :].astype(out.dtype)


def widen(ids, pieces):
    rows, width = pieces[0].shape
    cols = width // 4
    return pl.pallas_call(
        widen_body,
        grid=(width // cols,),
        in_specs=[pl.BlockSpec(memory_space=pltpu.SMEM)]
        + [pl.BlockSpec((rows, cols), lambda i: (0, i))] * len(pieces),
        out_specs=[
            pl.BlockSpec((len(pieces) * rows, cols), lambda i: (0, i)),
            pl.BlockSpec(TOKEN.shape, lambda i: (0, 0)),
        ],
        out_shape=[shape((len(pieces) * rows, width), jnp.float32), TOKEN],
        compiler_params=pltpu.CompilerParams(vmem_limit_bytes=12 << 20),
        cost_estimate=pl.CostEstimate(flops=0, bytes_accessed=0, transcendentals=0),
    )(ids, *pieces)


def gate_grads_body(ids, *refs):
    pieces, (others, gate_grad, out, token) = refs[:-4], refs[-4:]
    sign(token)
    tokens, cols = pieces[0].shape
    own = jnp.zeros((cols, out.shape[1]), jnp.float32)
    other = own
    for k, piece in enumerate(pieces):
        grads = gate_grad[aligned(ids[1] ^ k, tokens), :]
        own = own + dot(piece[...], grads, 0, 0)
        other = other + dot(others[k * tokens : (k + 1) * tokens, :], grads, 0, 0)
    out[aligned(ids[2], cols), :] = own
    out[aligned(1 - ids[2], cols), :] = other


def local_square(dp, pairs, hidden_in, gate_weight, values, pick_rows, pick_scores, grad_out):
    tokens, cols = hidden_in.shape
    rows_here, width = values.shape
    picks = pick_rows.shape[1]
    sub = rows_here // dp
    f32 = jnp.float32
    me, pair, core = (lax.axis_index(a) for a in ("dp",) + TABLE)
    ids = jnp.stack([me, pair, core]).astype(jnp.int32)
    every = dp * tokens

    mine = []
    for k in range(dp):
        perm = [
            ((e * pairs + z) * 2 + h, (z * pairs + (e ^ k)) * 2 + h)
            for e in range(dp)
            for z in range(pairs)
            for h in range(2)
        ]
        mine.append(lax.ppermute(hidden_in, ("dp",) + TABLE, perm))
    rows_t = pick_rows.T
    small = -(-3 * picks * tokens // cols // 16) * 16
    sent, weights_t = kernel_call(
        prepare_body,
        [shape((tokens + small, cols)), shape((picks, tokens), f32)],
        ids, pick_scores.T, rows_t, grad_out,
        scratch=[pltpu.VMEM((small, cols), f32)],
    )
    sent_own = sent
    sent = lax.all_gather(sent_own, "dp", axis=0)
    joined = kernel_call(join_body, [shape((every, cols))], ids, *mine, after=[sent_own])[0]
    others = hop(joined, "core", 2, 1)
    first, second = kernel_call(
        gate_body,
        [shape((every // 2, cols))] * 2,
        ids, *mine, others, gate_weight,
        scratch=[pltpu.VMEM((dp, tokens, cols), jnp.bfloat16)],
        flops=1 << 29,
    )
    value_own, value_send = kernel_call(
        columns_body, [shape((pairs * rows_here, cols))] * 2, ids, values
    )
    value_sent = kernel_call(
        halves_body, [shape((2 * rows_here, cols))] * pairs,
        ids, value_own, hop(value_send, "core", 2, 1),
    )
    value_got = swap(value_sent, "pair", pairs)
    first, second, *added, token = kernel_call(
        add_body,
        [shape((every // 2, cols))] * 4 + [TOKEN],
        ids, first, hop(first, "dp", dp, 1), second, hop(second, "dp", dp, 2),
        after=[sent] + value_got[1:3],
    )
    spread_all, spread_part = kernel_call(
        functools.partial(spread_body, picks, rows_here),
        [shape((2 * pairs * rows_here, every)), shape((2 * pairs * sub, every))],
        ids, sent,
        scratch=[pltpu.VMEM((picks, every), jnp.int32), pltpu.VMEM((picks, every), f32)],
        flops=1 << 27, after=[token],
    )
    gates = [first, hop(added[0], "dp", dp, 2), second, hop(added[1], "dp", dp, 1)]

    mem_grad, factor, value_part, keep, send, token = kernel_call(
        values_body,
        [shape((every, cols)), shape((every, cols), f32), shape((tokens, cols), f32)]
        + [shape((pairs * sub, cols))] * 2
        + [TOKEN],
        ids, *gates, sent, spread_part,
        scratch=[pltpu.VMEM((every, cols), f32)], flops=1 << 28,
    )
    *messages, sent_on = kernel_call(
        messages_body, [shape((2 * sub, cols))] * pairs + [TOKEN], ids, keep, hop(send, "core", 2, 1)
    )

    back = swap(messages, "pair", pairs)
    extra = 2 * picks * tokens // cols
    gate_grad, branch_out, term = kernel_call(
        grads_body,
        [shape((every, cols)), shape((tokens, cols)), shape((every, cols))],
        ids, factor, value_part, spread_all, *value_got, gate_weight,
        after=[sent_on],
        flops=1 << 30,
    )
    affinity = kernel_call(
        functools.partial(affinity_body, rows_here),
        [shape((extra, cols))],
        ids, mem_grad, *value_got, rows_t,
        scratch=[pltpu.VMEM((extra, cols), f32)],
    )[0]
    *inputs, sent_inputs = kernel_call(
        inputs_body,
        [shape((tokens + extra, cols))] * pairs + [TOKEN],
        ids, gate_grad, gate_weight, hop(term, "core", 2, 1), affinity,
        after=back[1:2],
    )
    grad_gate, done = kernel_call(
        gate_grads_body,
        [shape((2 * cols, cols), f32), TOKEN],
        ids, *mine, others, gate_grad, after=[sent_inputs],
    )
    grad_hidden, affinity = kernel_call(
        sums_body,
        [shape((tokens, cols)), shape((extra // 2, cols), f32)],
        ids, *swap(inputs, "pair", pairs), after=[done],
    )
    perm = [
        ((d * pairs + z) * 2 + h, (z * pairs + d) * 2 + h)
        for d in range(dp)
        for z in range(pairs)
        for h in range(2)
    ]
    grad_hidden = lax.ppermute(grad_hidden, ("dp",) + TABLE, perm)
    first, second = kernel_call(
        rows_body, [shape((sub // 2, width))] * 2, ids, *back, after=[sent_inputs]
    )
    first, second = kernel_call(
        pairs_body, [shape((sub, width))] * 2,
        ids, first, hop(first, "dp", dp, 1), second, hop(second, "dp", dp, 2),
    )
    grad_values, token = widen(
        ids, [first, hop(first, "dp", dp, 2), second, hop(second, "dp", dp, 1)]
    )
    grad_scores, scored = kernel_call(
        scores_body,
        [shape((picks, tokens), f32), TOKEN],
        ids, affinity, hop(affinity, "core", 2, 1), weights_t, after=[token],
    )
    grad_hidden = kernel_call(
        copy_body, [shape((tokens, cols))], ids, grad_hidden, after=[token, scored]
    )[0]
    return (branch_out, grad_hidden, grad_gate, grad_values, grad_scores.T)


def local(dp, pairs, *args):
    tokens, cols = args[0].shape
    square = dp == pairs == DIRECT and tokens == 128 and cols == 4 * tokens
    return (local_square if square else local_general)(dp, pairs, *args)


def solution(mesh):
    dp, table = mesh.shape["dp"], mesh.shape["table"]
    pairs = Mesh(mesh.devices.reshape(dp, table // 2, 2), ("dp",) + TABLE)
    split, rows, tokens = P("dp", TABLE), P(TABLE, None), P("dp", None)
    return jax.shard_map(
        functools.partial(local, dp, table // 2),
        mesh=pairs,
        in_specs=(split, split, rows, tokens, tokens, split),
        out_specs=(split, split, split, rows, tokens),
        check_vma=False,
    )
```

```python
import functools

import jax
import jax.numpy as jnp
from jax import lax
from jax.experimental import pallas as pl
from jax.experimental.pallas import tpu as pltpu
from jax.sharding import Mesh
from jax.sharding import PartitionSpec as P

DIRECT = 4
TABLE = ("pair", "core")


def block(x, index):
    return lax.dynamic_index_in_dim(x, index, 0, keepdims=False)


def placed(pieces, indices):
    out = jnp.zeros((len(pieces),) + pieces[0].shape, pieces[0].dtype)
    for piece, index in zip(pieces, indices):
        out = lax.dynamic_update_index_in_dim(out, piece, index, 0)
    return out


def hop(x, axis, size, mask):
    return lax.ppermute(x, axis, [(i, i ^ mask) for i in range(size)])


def order(axis, size):
    return [lax.axis_index(axis) ^ k for k in range(size)]


def gather(x, axis, size):
    if size <= DIRECT:
        return [x] + [hop(x, axis, size, k) for k in range(1, size)]
    whole = lax.all_gather(x, axis, axis=0)
    return [block(whole, k) for k in order(axis, size)]


def swap(pieces, axis, size):
    if size <= DIRECT:
        return [pieces[0]] + [hop(pieces[k], axis, size, k) for k in range(1, size)]
    ids = order(axis, size)
    whole = lax.all_to_all(placed(pieces, ids), axis, split_axis=0, concat_axis=0)
    return [block(whole, k) for k in ids]


def exchange(x, axis):
    return lax.all_to_all(x, axis, split_axis=0, concat_axis=0, tiled=True)


def total(terms):
    return functools.reduce(jnp.add, [t.astype(jnp.float32) for t in terms])


def spread_kernel(rows_ref, weights_ref, out_ref):
    tile = 32
    tokens = rows_ref.shape[1]

    def step(i, carry):
        base = pl.multiple_of(i * tile, tile)
        here = lax.broadcasted_iota(jnp.int32, (tile, tokens), 0) + base
        total = jnp.zeros((tile, tokens), jnp.float32)
        for k in range(rows_ref.shape[0]):
            hit = rows_ref[k : k + 1, :] == here
            total = jnp.where(hit, weights_ref[k : k + 1, :], total)
        out_ref[pl.ds(base, tile), :] = total.astype(out_ref.dtype)
        return carry

    lax.fori_loop(0, out_ref.shape[0] // tile, step, 0)


def spread(rows, weights, row_total):
    picks, tokens = rows.shape
    width = min(tokens, 512)
    return pl.pallas_call(
        spread_kernel,
        grid=(tokens // width,),
        in_specs=[pl.BlockSpec((picks, width), lambda i: (0, i))] * 2,
        out_specs=pl.BlockSpec((row_total, width), lambda i: (0, i)),
        out_shape=jax.ShapeDtypeStruct((row_total, tokens), jnp.bfloat16),
        compiler_params=pltpu.CompilerParams(vmem_limit_bytes=16 << 20),
        cost_estimate=pl.CostEstimate(
            flops=2 * picks * tokens * row_total,
            bytes_accessed=2 * tokens * row_total,
            transcendentals=0,
        ),
    )(rows, weights)


def pick_kernel(table_ref, rows_ref, out_ref):
    lanes = 128
    rows = rows_ref[...]
    inner = rows & (lanes - 1)
    outer = rows >> 7
    total = jnp.zeros(out_ref.shape, jnp.float32)
    for j in range(table_ref.shape[1] // lanes):
        part = table_ref[:, j * lanes : (j + 1) * lanes]
        found = jnp.take_along_axis(part, inner, axis=1)
        total = jnp.where(outer == j, found, total)
    out_ref[...] = total


def pick(table, rows):
    return pl.pallas_call(
        pick_kernel,
        out_shape=jax.ShapeDtypeStruct(rows.shape, jnp.float32),
        cost_estimate=pl.CostEstimate(
            flops=rows.size * 16, bytes_accessed=4 * table.size, transcendentals=0
        ),
    )(table, rows)


def pick_weights(pick_scores):
    row_max = jnp.max(pick_scores, axis=1, keepdims=True)
    exponent = jnp.exp(pick_scores - row_max)
    return exponent / jnp.sum(exponent, axis=1, keepdims=True)


def contract(a, b, dim_a, dim_b):
    return lax.dot_general(
        a, b, (((dim_a,), (dim_b,)), ((), ())), preferred_element_type=jnp.float32
    )


def local_general(dp, pairs, hidden_in, gate_weight, values, pick_rows, pick_scores, grad_out):
    tokens, cols = hidden_in.shape
    rows_here, width = values.shape
    picks = pick_rows.shape[1]
    table = 2 * pairs
    sub = rows_here // dp
    me, pair, core = (lax.axis_index(a) for a in ("dp",) + TABLE)
    here = 2 * pair + core
    f32, bf16 = jnp.float32, jnp.bfloat16

    wide = lax.all_gather(hidden_in, TABLE, axis=1, tiled=True)
    wide = wide.reshape(tokens, dp, table * cols // dp).transpose(1, 0, 2)
    hidden_all = exchange(wide, "dp").reshape(dp * tokens, -1)

    weights = pick_weights(pick_scores)
    weights_bf = weights.astype(bf16)
    small = jnp.concatenate([weights_bf, (pick_rows >> 5).astype(bf16), (pick_rows & 31).astype(bf16)], axis=1)
    small = small.T.reshape(-1, cols)
    sent = lax.all_gather(jnp.concatenate([grad_out, small], axis=0), "dp", axis=0)
    grad_out_all = sent[:, :tokens].reshape(dp * tokens, cols)
    small = sent[:, tokens:].reshape(dp, 3, picks, tokens).transpose(1, 2, 0, 3)
    small = small.reshape(3, picks, dp * tokens).astype(f32)
    rows_all = small[1].astype(jnp.int32) * 32 + small[2].astype(jnp.int32)

    def moved_row(row):
        return ((row // rows_here) ^ here) * rows_here + row % rows_here

    spread_all = spread(moved_row(rows_all), small[0], rows_here * table)

    by_core = values.reshape(rows_here, pairs, 2, cols).transpose(2, 1, 0, 3)
    mine = block(by_core, core)
    other = hop(block(by_core, 1 - core), "core", 2, 1)
    value_sent = [
        jnp.concatenate([block(mine, z), block(other, z)], axis=0) for z in order("pair", pairs)
    ]
    value_cols = jnp.concatenate(swap(value_sent, "pair", pairs), axis=0)

    partial_gate = contract(hidden_all, gate_weight, 1, 0).astype(bf16)
    terms = exchange(partial_gate.reshape(dp, tokens, cols), "dp")
    gate_own = total([terms[k] for k in range(dp)]).astype(bf16)
    gate_input = lax.all_gather(gate_own, "dp", axis=0, tiled=True).astype(f32)

    memory_read = contract(spread_all, value_cols, 0, 0)
    sigmoid_v = jax.nn.sigmoid(gate_input)
    gate_value = gate_input * sigmoid_v
    gate_slope = sigmoid_v * (1.0 + gate_input * (1.0 - sigmoid_v))
    upstream = grad_out_all.astype(f32)
    mem_grad = (upstream * gate_value).astype(bf16)
    gate_grad_in = (upstream * memory_read * gate_slope).astype(bf16)

    def own(x):
        return block(x.reshape(dp, tokens, cols), me)

    branch_out = (own(memory_read) * own(gate_value)).astype(bf16)

    input_term = contract(gate_grad_in, gate_weight, 1, 1).astype(bf16)
    input_got = exchange(input_term.reshape(dp, tokens, -1), "dp")

    spread_parts = spread_all.reshape(pairs, 2, dp, sub, dp * tokens)
    part = jnp.concatenate(
        [
            lax.dynamic_slice(
                spread_parts, (z ^ pair, 0, me, 0, 0), (1, 2, 1, sub, dp * tokens)
            ).reshape(2 * sub, dp * tokens)
            for z in range(pairs)
        ],
        axis=0,
    )
    value_term = contract(part, mem_grad, 1, 0).astype(bf16).reshape(pairs, 2, sub, cols)
    value_other = hop(value_term[:, 1], "core", 2, 1)

    affinity_all = contract(own(mem_grad), value_cols, 1, 1)
    own_rows = jnp.pad(moved_row(pick_rows), ((0, 0), (0, 128 - picks)))
    affinity = pick(affinity_all, own_rows)[:, :picks]
    affinity = affinity + hop(affinity, "core", 2, 1)
    high = affinity.astype(bf16)
    low = (affinity - high.astype(f32)).astype(bf16)
    parts = jnp.concatenate([high, low], axis=1).reshape(-1, cols)

    back = exchange(
        jnp.concatenate(
            [value_term[:, 0], value_other, jnp.broadcast_to(parts, (pairs,) + parts.shape)], axis=1
        ),
        "pair",
    )
    affinity = back[:, 2 * sub :].reshape(pairs, tokens, 2 * picks).astype(f32)
    affinity = jnp.sum(affinity[:, :, :picks] + affinity[:, :, picks:], axis=0)
    grad_scores = weights * (affinity - jnp.sum(weights * affinity, axis=1, keepdims=True))

    first, second = back[:, :sub], back[:, sub : 2 * sub]
    back = jnp.stack(
        [jnp.where(core == 0, first, second), jnp.where(core == 0, second, first)], axis=1
    )
    back = back.transpose(2, 0, 1, 3).reshape(sub, width)
    grad_values = placed(
        [r.astype(f32) for r in gather(back, "dp", dp)], order("dp", dp)
    ).reshape(rows_here, width)

    wide = input_got.transpose(1, 0, 2).reshape(tokens, table, cols)
    input_terms = exchange(wide.transpose(1, 0, 2), TABLE)
    grad_hidden = total([input_terms[k] for k in range(table)]).astype(bf16)
    grad_gate = contract(hidden_all, gate_grad_in, 0, 0)
    return (branch_out, grad_hidden, grad_gate, grad_values, grad_scores)


def kernel_call(body, outs, *args, scratch=(), flops=0, after=()):
    count = len(args)
    size = sum(a.size * a.dtype.itemsize for a in args)
    size += sum(o.size * o.dtype.itemsize for o in outs)

    def whole_body(*refs):
        body(*refs[:count], *refs[count + len(after) :])

    vmem = pl.BlockSpec(memory_space=pltpu.VMEM)
    return pl.pallas_call(
        whole_body,
        in_specs=[pl.BlockSpec(memory_space=pltpu.SMEM)] + [vmem] * (count + len(after) - 1),
        out_specs=[vmem] * len(outs),
        out_shape=list(outs),
        scratch_shapes=list(scratch),
        compiler_params=pltpu.CompilerParams(vmem_limit_bytes=12 << 20),
        cost_estimate=pl.CostEstimate(flops=0, bytes_accessed=0, transcendentals=0),
    )(*args, *after)


def shape(dims, dtype=jnp.bfloat16):
    return jax.ShapeDtypeStruct(dims, dtype)


TOKEN = shape((8, 128), jnp.float32)


def sign(token):
    token[...] = jnp.zeros(token.shape, token.dtype)


def aligned(index, size):
    return pl.ds(pl.multiple_of(index * size, size), size)


def pack_rows(out_ref, first, x):
    count, lanes = x.shape
    per = out_ref.shape[1] // lanes
    for j in range(count):
        row, lane = (first + j) // per, (first + j) % per * lanes
        out_ref[row : row + 1, lane : lane + lanes] = x[j : j + 1, :]


def row_of(packed, j, lanes):
    per = packed.shape[1] // lanes
    return packed[j // per : j // per + 1, j % per * lanes : (j % per + 1) * lanes]


def prepare_body(ids, scores, rows, grad_out, sent, weights, packed):
    tokens = grad_out.shape[0]
    x = scores[...]
    exponent = jnp.exp(x - jnp.max(x, axis=0, keepdims=True))
    w = exponent / jnp.sum(exponent, axis=0, keepdims=True)
    weights[...] = w
    packed[...] = jnp.zeros(packed.shape, packed.dtype)
    count = w.shape[0]
    pack_rows(packed, 0, w)
    pack_rows(packed, count, (rows[...] >> 5).astype(jnp.float32))
    pack_rows(packed, 2 * count, (rows[...] & 31).astype(jnp.float32))
    sent[:tokens, :] = grad_out[...]
    sent[tokens:, :] = packed[...].astype(sent.dtype)


def moved(row, rows_here, pair, core):
    owner, inner = lax.div(row, rows_here), lax.rem(row, rows_here)
    return (owner ^ (2 * pair + core)) * rows_here + inner


def spread_body(picks, rows_here, ids, sent, out, part, rows, weights):
    me, pair, core = ids[0], ids[1], ids[2]
    dp = sent.shape[0]
    tokens = rows.shape[1] // dp
    pairs = part.shape[0] // (2 * (rows_here // dp))
    for e in range(dp):
        packed = sent[e, tokens:, :].astype(jnp.float32)
        span = slice(e * tokens, (e + 1) * tokens)
        for k in range(picks):
            weights[k : k + 1, span] = row_of(packed, k, tokens)
            high, low = row_of(packed, picks + k, tokens), row_of(packed, 2 * picks + k, tokens)
            rows[k : k + 1, span] = (high * 32.0 + low).astype(jnp.int32)
    rows[...] = moved(rows[...], rows_here, pair, core)
    tile = 32

    def step(i, carry):
        base = pl.multiple_of(i * tile, tile)
        here = lax.broadcasted_iota(jnp.int32, (tile, rows.shape[1]), 0) + base
        acc = jnp.zeros((tile, rows.shape[1]), jnp.float32)
        for k in range(picks):
            acc = jnp.where(rows[k : k + 1, :] == here, weights[k : k + 1, :], acc)
        out[pl.ds(base, tile), :] = acc.astype(out.dtype)
        return carry

    lax.fori_loop(0, out.shape[0] // tile, step, 0)
    sub = rows_here // dp
    for g in range(2):
        for z in range(pairs):
            at = (2 * z + g) * rows_here + me * sub
            spot = (g * pairs + z) * sub
            part[spot : spot + sub, :] = out[pl.ds(pl.multiple_of(at, sub), sub), :]


def columns_body(ids, values, own, other):
    rows, cols = values.shape[0], own.shape[1]
    for k in range(own.shape[0] // rows):
        span, at = slice(k * rows, (k + 1) * rows), 2 * (ids[1] ^ k)
        own[span, :] = values[:, aligned(at + ids[2], cols)]
        other[span, :] = values[:, aligned(at + 1 - ids[2], cols)]


def halves_body(ids, own, got, *outs):
    rows = outs[0].shape[0] // 2
    for k, out in enumerate(outs):
        span = slice(k * rows, (k + 1) * rows)
        out[:rows, :] = own[span, :]
        out[rows:, :] = got[span, :]


def dot(a, b, dim_a=1, dim_b=0):
    return lax.dot_general(
        a, b, (((dim_a,), (dim_b,)), ((), ())), preferred_element_type=jnp.float32
    )


def join_body(ids, *refs):
    pieces, out = refs[:-1], refs[-1]
    rows = pieces[0].shape[0]
    for k, piece in enumerate(pieces):
        out[k * rows : (k + 1) * rows, :] = piece[...]


def gate_body(ids, *refs):
    pieces, (others, weight, first, second, stage) = refs[:-5], refs[-5:]
    dp, rows = len(pieces), stage.shape[1]
    cols = weight.shape[1]
    own, other = weight[aligned(ids[2], cols), :], weight[aligned(1 - ids[2], cols), :]
    for k, piece in enumerate(pieces):
        term = dot(piece[...], own) + dot(others[k * rows : (k + 1) * rows, :], other)
        stage[ids[1] ^ k] = term.astype(stage.dtype)
    half = dp // 2
    for e in range(half):
        first[e * rows : (e + 1) * rows, :] = stage[e]
        second[e * rows : (e + 1) * rows, :] = stage[half + e]


def add_body(ids, a, a_got, b, b_got, a_keep, b_keep, a_send, b_send, token):
    sign(token)
    f32 = jnp.float32
    for x, got, keep, send in ((a, a_got, a_keep, a_send), (b, b_got, b_keep, b_send)):
        keep[...] = (x[...].astype(f32) + got[...].astype(f32)).astype(keep.dtype)
        send[...] = keep[...]


def gate_value_of(stage, a0, a1, b0, b1):
    half = a0.shape[0]
    stage[:half, :] = a0[...].astype(jnp.float32) + a1[...].astype(jnp.float32)
    stage[half:, :] = b0[...].astype(jnp.float32) + b1[...].astype(jnp.float32)


def values_body(ids, a0, a1, b0, b1, sent, part, mem_grad, factor, value_own, keep, send, token, stage):
    tokens = value_own.shape[0]
    gate_value_of(stage, a0, a1, b0, b1)
    for k in range(sent.shape[0]):
        span = aligned(ids[0] ^ k, tokens)
        gate = stage[span, :]
        s = jax.nn.sigmoid(gate)
        upstream = sent[ids[0] ^ k, :tokens, :].astype(jnp.float32)
        mem_grad[span, :] = (upstream * (gate * s)).astype(mem_grad.dtype)
        factor[span, :] = upstream * (s * (1.0 + gate * (1.0 - s)))
        if k == 0:
            value_own[...] = gate * s
    half = keep.shape[0]
    term = dot(part[...], mem_grad[...])
    keep[...] = term[:half].astype(keep.dtype)
    send[...] = term[half:].astype(send.dtype)
    sign(token)


def messages_body(ids, keep, got, *refs):
    messages, token = refs[:-1], refs[-1]
    sign(token)
    sub = messages[0].shape[0] // 2
    for z, message in enumerate(messages):
        message[:sub, :] = keep[z * sub : (z + 1) * sub, :]
        message[sub:, :] = got[z * sub : (z + 1) * sub, :]


def grads_body(ids, factor, value_own, spread_ref, *refs):
    values, (weight, gate_grad, branch, term) = refs[:-4], refs[-4:]
    tokens, rows = branch.shape[0], values[0].shape[0]
    for k in range(factor.shape[0] // tokens):
        span = aligned(ids[0] ^ k, tokens)
        memory = 0.0
        for i, piece in enumerate(values):
            memory = memory + dot(spread_ref[i * rows : (i + 1) * rows, span], piece[...], 0, 0)
        gate_grad[span, :] = (factor[span, :] * memory).astype(gate_grad.dtype)
        if k == 0:
            branch[...] = (memory * value_own[...]).astype(branch.dtype)
    across = weight[aligned(1 - ids[2], weight.shape[1]), :]
    term[...] = dot(gate_grad[...], across, 1, 1).astype(term.dtype)


def affinity_part(rows_here, ids, mem_grad, values, rows, packed):
    f32 = jnp.float32
    tokens = rows.shape[1]
    count = rows.shape[0]
    at = moved(rows[...], rows_here, ids[1], ids[2])
    at = jnp.concatenate([at] * (tokens // count), axis=0).T
    inner, outer = at & 127, at >> 7
    grads = mem_grad[aligned(ids[0], tokens), :]
    found = jnp.zeros(at.shape, f32)
    blocks = values[0].shape[0] // 128
    for j, table in enumerate(values):
        all_rows = dot(grads, table[...], 1, 1)
        for i in range(blocks):
            hit = jnp.take_along_axis(all_rows[:, i * 128 : (i + 1) * 128], inner, axis=1)
            found = jnp.where(outer == j * blocks + i, hit, found)
    affinity = found.T[:count]
    high = affinity.astype(jnp.bfloat16).astype(f32)
    pack_rows(packed, 0, high)
    pack_rows(packed, count, affinity - high)
    return packed[...].astype(jnp.bfloat16)


def inputs_body(rows_here, ids, gate_grad, weight, arrived, mem_grad, rows, *refs):
    pairs = (len(refs) - 2) // 2
    values, outs, token, packed = refs[:pairs], refs[pairs:-2], refs[-2], refs[-1]
    sign(token)
    extra, cols = packed.shape
    tokens = outs[0].shape[0] - extra
    affinity = affinity_part(rows_here, ids, mem_grad, values, rows, packed)
    own = weight[aligned(ids[2], cols), :]
    for i, out in enumerate(outs):
        span = aligned(ids[1] ^ i, tokens)
        term = dot(gate_grad[span, :], own, 1, 1) + arrived[span, :].astype(jnp.float32)
        out[:tokens, :] = term.astype(out.dtype)
        out[tokens:, :] = affinity


def sums_body(ids, *refs):
    pieces, out, affinity = refs[:-2], refs[-2], refs[-1]
    whole = 0.0
    for piece in pieces:
        whole = whole + piece[...].astype(jnp.float32)
    tokens = out.shape[0]
    out[...] = whole[:tokens].astype(out.dtype)
    half = (whole.shape[0] - tokens) // 2
    affinity[...] = whole[tokens : tokens + half] + whole[tokens + half :]


def scores_body(ids, own, got, weights, grads, token):
    sign(token)
    whole = own[...] + got[...]
    w = weights[...]
    count, lanes = w.shape
    affinity = jnp.concatenate([row_of(whole, k, lanes) for k in range(count)], axis=0)
    grads[...] = w * (affinity - jnp.sum(w * affinity, axis=0, keepdims=True))


def rows_body(ids, *refs):
    back, halves = refs[:-2], refs[-2:]
    cols = back[0].shape[1]
    sub, half = back[0].shape[0] // 2, halves[0].shape[0]
    for z, piece in enumerate(back):
        for j, out in enumerate(halves):
            at = 2 * (ids[1] ^ z)
            span = slice(j * half, (j + 1) * half)
            out[:, aligned(at + ids[2], cols)] = piece[span, :]
            out[:, aligned(at + 1 - ids[2], cols)] = piece[sub + j * half : sub + (j + 1) * half, :]


def widen_body(ids, *refs):
    pieces, (out, token) = refs[:-2], refs[-2:]
    sign(token)
    half, count = pieces[0].shape[0], len(pieces) // 2
    for k, piece in enumerate(pieces):
        at = (ids[0] ^ (k % count)) * 2 * half + k // count * half
        out[pl.ds(pl.multiple_of(at, half), half), :] = piece[...].astype(out.dtype)


def widen(ids, pieces):
    rows, width = pieces[0].shape
    cols = width // 4
    return pl.pallas_call(
        widen_body,
        grid=(width // cols,),
        in_specs=[pl.BlockSpec(memory_space=pltpu.SMEM)]
        + [pl.BlockSpec((rows, cols), lambda i: (0, i))] * len(pieces),
        out_specs=[
            pl.BlockSpec((len(pieces) * rows, cols), lambda i: (0, i)),
            pl.BlockSpec(TOKEN.shape, lambda i: (0, 0)),
        ],
        out_shape=[shape((len(pieces) * rows, width), jnp.float32), TOKEN],
        compiler_params=pltpu.CompilerParams(vmem_limit_bytes=12 << 20),
        cost_estimate=pl.CostEstimate(flops=0, bytes_accessed=0, transcendentals=0),
    )(ids, *pieces)


def gate_grads_body(ids, *refs):
    pieces, (others, gate_grad, out, token) = refs[:-4], refs[-4:]
    sign(token)
    tokens, cols = pieces[0].shape
    own = jnp.zeros((cols, out.shape[1]), jnp.float32)
    other = own
    for k, piece in enumerate(pieces):
        grads = gate_grad[aligned(ids[1] ^ k, tokens), :]
        own = own + dot(piece[...], grads, 0, 0)
        other = other + dot(others[k * tokens : (k + 1) * tokens, :], grads, 0, 0)
    out[aligned(ids[2], cols), :] = own
    out[aligned(1 - ids[2], cols), :] = other


def local_square(dp, pairs, hidden_in, gate_weight, values, pick_rows, pick_scores, grad_out):
    tokens, cols = hidden_in.shape
    rows_here, width = values.shape
    picks = pick_rows.shape[1]
    sub = rows_here // dp
    f32 = jnp.float32
    me, pair, core = (lax.axis_index(a) for a in ("dp",) + TABLE)
    ids = jnp.stack([me, pair, core]).astype(jnp.int32)
    every = dp * tokens

    mine = []
    for k in range(dp):
        perm = [
            ((e * pairs + z) * 2 + h, (z * pairs + (e ^ k)) * 2 + h)
            for e in range(dp)
            for z in range(pairs)
            for h in range(2)
        ]
        mine.append(lax.ppermute(hidden_in, ("dp",) + TABLE, perm))
    rows_t = pick_rows.T
    small = -(-3 * picks * tokens // cols // 16) * 16
    sent, weights_t = kernel_call(
        prepare_body,
        [shape((tokens + small, cols)), shape((picks, tokens), f32)],
        ids, pick_scores.T, rows_t, grad_out,
        scratch=[pltpu.VMEM((small, cols), f32)],
    )
    sent_own = sent
    sent = lax.all_gather(sent_own, "dp", axis=0)
    joined = kernel_call(join_body, [shape((every, cols))], ids, *mine, after=[sent_own])[0]
    others = hop(joined, "core", 2, 1)
    first, second = kernel_call(
        gate_body,
        [shape((every // 2, cols))] * 2,
        ids, *mine, others, gate_weight,
        scratch=[pltpu.VMEM((dp, tokens, cols), jnp.bfloat16)],
        flops=1 << 29,
    )
    value_own, value_send = kernel_call(
        columns_body, [shape((pairs * rows_here, cols))] * 2, ids, values
    )
    value_sent = kernel_call(
        halves_body, [shape((2 * rows_here, cols))] * pairs,
        ids, value_own, hop(value_send, "core", 2, 1),
    )
    value_got = swap(value_sent, "pair", pairs)
    first, second, *added, token = kernel_call(
        add_body,
        [shape((every // 2, cols))] * 4 + [TOKEN],
        ids, first, hop(first, "dp", dp, 1), second, hop(second, "dp", dp, 2),
        after=[sent] + value_got[1:3],
    )
    spread_all, spread_part = kernel_call(
        functools.partial(spread_body, picks, rows_here),
        [shape((2 * pairs * rows_here, every)), shape((2 * pairs * sub, every))],
        ids, sent,
        scratch=[pltpu.VMEM((picks, every), jnp.int32), pltpu.VMEM((picks, every), f32)],
        flops=1 << 27, after=[token],
    )
    gates = [first, hop(added[0], "dp", dp, 2), second, hop(added[1], "dp", dp, 1)]

    mem_grad, factor, value_part, keep, send, token = kernel_call(
        values_body,
        [shape((every, cols)), shape((every, cols), f32), shape((tokens, cols), f32)]
        + [shape((pairs * sub, cols))] * 2
        + [TOKEN],
        ids, *gates, sent, spread_part,
        scratch=[pltpu.VMEM((every, cols), f32)], flops=1 << 28,
    )
    *messages, sent_on = kernel_call(
        messages_body, [shape((2 * sub, cols))] * pairs + [TOKEN], ids, keep, hop(send, "core", 2, 1)
    )

    back = swap(messages, "pair", pairs)
    extra = 2 * picks * tokens // cols
    gate_grad, branch_out, term = kernel_call(
        grads_body,
        [shape((every, cols)), shape((tokens, cols)), shape((every, cols))],
        ids, factor, value_part, spread_all, *value_got, gate_weight,
        after=[sent_on],
        flops=1 << 30,
    )
    *inputs, sent_inputs = kernel_call(
        functools.partial(inputs_body, rows_here),
        [shape((tokens + extra, cols))] * pairs + [TOKEN],
        ids, gate_grad, gate_weight, hop(term, "core", 2, 1), mem_grad, rows_t, *value_got,
        scratch=[pltpu.VMEM((extra, cols), f32)],
        after=back[1:2],
    )
    grad_gate, done = kernel_call(
        gate_grads_body,
        [shape((2 * cols, cols), f32), TOKEN],
        ids, *mine, others, gate_grad, after=[sent_inputs],
    )
    grad_hidden, affinity = kernel_call(
        sums_body,
        [shape((tokens, cols)), shape((extra // 2, cols), f32)],
        ids, *swap(inputs, "pair", pairs), after=[done],
    )
    perm = [
        ((d * pairs + z) * 2 + h, (z * pairs + d) * 2 + h)
        for d in range(dp)
        for z in range(pairs)
        for h in range(2)
    ]
    grad_hidden = lax.ppermute(grad_hidden, ("dp",) + TABLE, perm)
    first, second = kernel_call(
        rows_body, [shape((sub // 2, width))] * 2, ids, *back, after=[sent_inputs]
    )
    along_x, along_y = hop(first, "dp", dp, 1), hop(second, "dp", dp, 2)
    first = [first, along_x, hop(first, "dp", dp, 2), hop(along_x, "dp", dp, 2)]
    second = [second, hop(second, "dp", dp, 1), along_y, hop(along_y, "dp", dp, 1)]
    grad_values, token = widen(ids, first + second)
    grad_scores, scored = kernel_call(
        scores_body,
        [shape((picks, tokens), f32), TOKEN],
        ids, affinity, hop(affinity, "core", 2, 1), weights_t, after=[token],
    )
    grad_hidden = grad_hidden + (token[0, 0] + scored[0, 0]).astype(grad_hidden.dtype)
    return (branch_out, grad_hidden, grad_gate, grad_values, grad_scores.T)


def local(dp, pairs, *args):
    tokens, cols = args[0].shape
    square = dp == pairs == DIRECT and tokens == 128 and cols == 4 * tokens
    return (local_square if square else local_general)(dp, pairs, *args)


def solution(mesh):
    dp, table = mesh.shape["dp"], mesh.shape["table"]
    pairs = Mesh(mesh.devices.reshape(dp, table // 2, 2), ("dp",) + TABLE)
    split, rows, tokens = P("dp", TABLE), P(TABLE, None), P("dp", None)
    return jax.shard_map(
        functools.partial(local, dp, table // 2),
        mesh=pairs,
        in_specs=(split, split, rows, tokens, tokens, split),
        out_specs=(split, split, split, rows, tokens),
        check_vma=False,
    )
```

```python
import functools

import jax
import jax.numpy as jnp
from jax import lax
from jax.experimental import pallas as pl
from jax.experimental.pallas import tpu as pltpu
from jax.sharding import Mesh
from jax.sharding import PartitionSpec as P

DIRECT = 4
TABLE = ("pair", "core")


def block(x, index):
    return lax.dynamic_index_in_dim(x, index, 0, keepdims=False)


def placed(pieces, indices):
    out = jnp.zeros((len(pieces),) + pieces[0].shape, pieces[0].dtype)
    for piece, index in zip(pieces, indices):
        out = lax.dynamic_update_index_in_dim(out, piece, index, 0)
    return out


def hop(x, axis, size, mask):
    return lax.ppermute(x, axis, [(i, i ^ mask) for i in range(size)])


def order(axis, size):
    return [lax.axis_index(axis) ^ k for k in range(size)]


def gather(x, axis, size):
    if size <= DIRECT:
        return [x] + [hop(x, axis, size, k) for k in range(1, size)]
    whole = lax.all_gather(x, axis, axis=0)
    return [block(whole, k) for k in order(axis, size)]


def swap(pieces, axis, size):
    if size <= DIRECT:
        return [pieces[0]] + [hop(pieces[k], axis, size, k) for k in range(1, size)]
    ids = order(axis, size)
    whole = lax.all_to_all(placed(pieces, ids), axis, split_axis=0, concat_axis=0)
    return [block(whole, k) for k in ids]


def exchange(x, axis):
    return lax.all_to_all(x, axis, split_axis=0, concat_axis=0, tiled=True)


def total(terms):
    return functools.reduce(jnp.add, [t.astype(jnp.float32) for t in terms])


def spread_kernel(rows_ref, weights_ref, out_ref):
    tile = 32
    tokens = rows_ref.shape[1]

    def step(i, carry):
        base = pl.multiple_of(i * tile, tile)
        here = lax.broadcasted_iota(jnp.int32, (tile, tokens), 0) + base
        total = jnp.zeros((tile, tokens), jnp.float32)
        for k in range(rows_ref.shape[0]):
            hit = rows_ref[k : k + 1, :] == here
            total = jnp.where(hit, weights_ref[k : k + 1, :], total)
        out_ref[pl.ds(base, tile), :] = total.astype(out_ref.dtype)
        return carry

    lax.fori_loop(0, out_ref.shape[0] // tile, step, 0)


def spread(rows, weights, row_total):
    picks, tokens = rows.shape
    width = min(tokens, 512)
    return pl.pallas_call(
        spread_kernel,
        grid=(tokens // width,),
        in_specs=[pl.BlockSpec((picks, width), lambda i: (0, i))] * 2,
        out_specs=pl.BlockSpec((row_total, width), lambda i: (0, i)),
        out_shape=jax.ShapeDtypeStruct((row_total, tokens), jnp.bfloat16),
        compiler_params=pltpu.CompilerParams(vmem_limit_bytes=16 << 20),
        cost_estimate=pl.CostEstimate(
            flops=2 * picks * tokens * row_total,
            bytes_accessed=2 * tokens * row_total,
            transcendentals=0,
        ),
    )(rows, weights)


def pick_kernel(table_ref, rows_ref, out_ref):
    lanes = 128
    rows = rows_ref[...]
    inner = rows & (lanes - 1)
    outer = rows >> 7
    total = jnp.zeros(out_ref.shape, jnp.float32)
    for j in range(table_ref.shape[1] // lanes):
        part = table_ref[:, j * lanes : (j + 1) * lanes]
        found = jnp.take_along_axis(part, inner, axis=1)
        total = jnp.where(outer == j, found, total)
    out_ref[...] = total


def pick(table, rows):
    return pl.pallas_call(
        pick_kernel,
        out_shape=jax.ShapeDtypeStruct(rows.shape, jnp.float32),
        cost_estimate=pl.CostEstimate(
            flops=rows.size * 16, bytes_accessed=4 * table.size, transcendentals=0
        ),
    )(table, rows)


def pick_weights(pick_scores):
    row_max = jnp.max(pick_scores, axis=1, keepdims=True)
    exponent = jnp.exp(pick_scores - row_max)
    return exponent / jnp.sum(exponent, axis=1, keepdims=True)


def contract(a, b, dim_a, dim_b):
    return lax.dot_general(
        a, b, (((dim_a,), (dim_b,)), ((), ())), preferred_element_type=jnp.float32
    )


def local_general(dp, pairs, hidden_in, gate_weight, values, pick_rows, pick_scores, grad_out):
    tokens, cols = hidden_in.shape
    rows_here, width = values.shape
    picks = pick_rows.shape[1]
    table = 2 * pairs
    sub = rows_here // dp
    me, pair, core = (lax.axis_index(a) for a in ("dp",) + TABLE)
    here = 2 * pair + core
    f32, bf16 = jnp.float32, jnp.bfloat16

    wide = lax.all_gather(hidden_in, TABLE, axis=1, tiled=True)
    wide = wide.reshape(tokens, dp, table * cols // dp).transpose(1, 0, 2)
    hidden_all = exchange(wide, "dp").reshape(dp * tokens, -1)

    weights = pick_weights(pick_scores)
    weights_bf = weights.astype(bf16)
    small = jnp.concatenate([weights_bf, (pick_rows >> 5).astype(bf16), (pick_rows & 31).astype(bf16)], axis=1)
    small = small.T.reshape(-1, cols)
    sent = lax.all_gather(jnp.concatenate([grad_out, small], axis=0), "dp", axis=0)
    grad_out_all = sent[:, :tokens].reshape(dp * tokens, cols)
    small = sent[:, tokens:].reshape(dp, 3, picks, tokens).transpose(1, 2, 0, 3)
    small = small.reshape(3, picks, dp * tokens).astype(f32)
    rows_all = small[1].astype(jnp.int32) * 32 + small[2].astype(jnp.int32)

    def moved_row(row):
        return ((row // rows_here) ^ here) * rows_here + row % rows_here

    spread_all = spread(moved_row(rows_all), small[0], rows_here * table)

    by_core = values.reshape(rows_here, pairs, 2, cols).transpose(2, 1, 0, 3)
    mine = block(by_core, core)
    other = hop(block(by_core, 1 - core), "core", 2, 1)
    value_sent = [
        jnp.concatenate([block(mine, z), block(other, z)], axis=0) for z in order("pair", pairs)
    ]
    value_cols = jnp.concatenate(swap(value_sent, "pair", pairs), axis=0)

    partial_gate = contract(hidden_all, gate_weight, 1, 0).astype(bf16)
    terms = exchange(partial_gate.reshape(dp, tokens, cols), "dp")
    gate_own = total([terms[k] for k in range(dp)]).astype(bf16)
    gate_input = lax.all_gather(gate_own, "dp", axis=0, tiled=True).astype(f32)

    memory_read = contract(spread_all, value_cols, 0, 0)
    sigmoid_v = jax.nn.sigmoid(gate_input)
    gate_value = gate_input * sigmoid_v
    gate_slope = sigmoid_v * (1.0 + gate_input * (1.0 - sigmoid_v))
    upstream = grad_out_all.astype(f32)
    mem_grad = (upstream * gate_value).astype(bf16)
    gate_grad_in = (upstream * memory_read * gate_slope).astype(bf16)

    def own(x):
        return block(x.reshape(dp, tokens, cols), me)

    branch_out = (own(memory_read) * own(gate_value)).astype(bf16)

    input_term = contract(gate_grad_in, gate_weight, 1, 1).astype(bf16)
    input_got = exchange(input_term.reshape(dp, tokens, -1), "dp")

    spread_parts = spread_all.reshape(pairs, 2, dp, sub, dp * tokens)
    part = jnp.concatenate(
        [
            lax.dynamic_slice(
                spread_parts, (z ^ pair, 0, me, 0, 0), (1, 2, 1, sub, dp * tokens)
            ).reshape(2 * sub, dp * tokens)
            for z in range(pairs)
        ],
        axis=0,
    )
    value_term = contract(part, mem_grad, 1, 0).astype(bf16).reshape(pairs, 2, sub, cols)
    value_other = hop(value_term[:, 1], "core", 2, 1)

    affinity_all = contract(own(mem_grad), value_cols, 1, 1)
    own_rows = jnp.pad(moved_row(pick_rows), ((0, 0), (0, 128 - picks)))
    affinity = pick(affinity_all, own_rows)[:, :picks]
    affinity = affinity + hop(affinity, "core", 2, 1)
    high = affinity.astype(bf16)
    low = (affinity - high.astype(f32)).astype(bf16)
    parts = jnp.concatenate([high, low], axis=1).reshape(-1, cols)

    back = exchange(
        jnp.concatenate(
            [value_term[:, 0], value_other, jnp.broadcast_to(parts, (pairs,) + parts.shape)], axis=1
        ),
        "pair",
    )
    affinity = back[:, 2 * sub :].reshape(pairs, tokens, 2 * picks).astype(f32)
    affinity = jnp.sum(affinity[:, :, :picks] + affinity[:, :, picks:], axis=0)
    grad_scores = weights * (affinity - jnp.sum(weights * affinity, axis=1, keepdims=True))

    first, second = back[:, :sub], back[:, sub : 2 * sub]
    back = jnp.stack(
        [jnp.where(core == 0, first, second), jnp.where(core == 0, second, first)], axis=1
    )
    back = back.transpose(2, 0, 1, 3).reshape(sub, width)
    grad_values = placed(
        [r.astype(f32) for r in gather(back, "dp", dp)], order("dp", dp)
    ).reshape(rows_here, width)

    wide = input_got.transpose(1, 0, 2).reshape(tokens, table, cols)
    input_terms = exchange(wide.transpose(1, 0, 2), TABLE)
    grad_hidden = total([input_terms[k] for k in range(table)]).astype(bf16)
    grad_gate = contract(hidden_all, gate_grad_in, 0, 0)
    return (branch_out, grad_hidden, grad_gate, grad_values, grad_scores)


def kernel_call(body, outs, *args, scratch=(), after=()):
    count = len(args)

    def whole_body(*refs):
        body(*refs[:count], *refs[count + len(after) :])

    vmem = pl.BlockSpec(memory_space=pltpu.VMEM)
    return pl.pallas_call(
        whole_body,
        in_specs=[pl.BlockSpec(memory_space=pltpu.SMEM)] + [vmem] * (count + len(after) - 1),
        out_specs=[vmem] * len(outs),
        out_shape=list(outs),
        scratch_shapes=list(scratch),
        compiler_params=pltpu.CompilerParams(vmem_limit_bytes=12 << 20),
        cost_estimate=pl.CostEstimate(flops=0, bytes_accessed=0, transcendentals=0),
    )(*args, *after)


def shape(dims, dtype=jnp.bfloat16):
    return jax.ShapeDtypeStruct(dims, dtype)


TOKEN = shape((8, 128), jnp.float32)


def sign(token):
    token[...] = jnp.zeros(token.shape, token.dtype)


def aligned(index, size):
    return pl.ds(pl.multiple_of(index * size, size), size)


def pack_rows(out_ref, first, x):
    count, lanes = x.shape
    per = out_ref.shape[1] // lanes
    for j in range(count):
        row, lane = (first + j) // per, (first + j) % per * lanes
        out_ref[row : row + 1, lane : lane + lanes] = x[j : j + 1, :]


def row_of(packed, j, lanes):
    per = packed.shape[1] // lanes
    return packed[j // per : j // per + 1, j % per * lanes : (j % per + 1) * lanes]


def prepare_body(ids, scores, rows, grad_out, sent, weights, packed):
    tokens = grad_out.shape[0]
    x = scores[...]
    exponent = jnp.exp(x - jnp.max(x, axis=0, keepdims=True))
    w = exponent / jnp.sum(exponent, axis=0, keepdims=True)
    weights[...] = w
    packed[...] = jnp.zeros(packed.shape, packed.dtype)
    count = w.shape[0]
    pack_rows(packed, 0, w)
    pack_rows(packed, count, (rows[...] >> 5).astype(jnp.float32))
    pack_rows(packed, 2 * count, (rows[...] & 31).astype(jnp.float32))
    sent[:tokens, :] = grad_out[...]
    sent[tokens:, :] = packed[...].astype(sent.dtype)


def moved(row, rows_here, pair, core):
    owner, inner = lax.div(row, rows_here), lax.rem(row, rows_here)
    return (owner ^ (2 * pair + core)) * rows_here + inner


def spread_body(picks, rows_here, ids, sent, out, part, rows, weights):
    me, pair, core = ids[0], ids[1], ids[2]
    dp = sent.shape[0]
    tokens = rows.shape[1] // dp
    pairs = part.shape[0] // (2 * (rows_here // dp))
    for e in range(dp):
        packed = sent[e, tokens:, :].astype(jnp.float32)
        span = slice(e * tokens, (e + 1) * tokens)
        for k in range(picks):
            weights[k : k + 1, span] = row_of(packed, k, tokens)
            high, low = row_of(packed, picks + k, tokens), row_of(packed, 2 * picks + k, tokens)
            rows[k : k + 1, span] = (high * 32.0 + low).astype(jnp.int32)
    rows[...] = moved(rows[...], rows_here, pair, core)
    tile = 32

    def step(i, carry):
        base = pl.multiple_of(i * tile, tile)
        here = lax.broadcasted_iota(jnp.int32, (tile, rows.shape[1]), 0) + base
        acc = jnp.zeros((tile, rows.shape[1]), jnp.float32)
        for k in range(picks):
            acc = jnp.where(rows[k : k + 1, :] == here, weights[k : k + 1, :], acc)
        out[pl.ds(base, tile), :] = acc.astype(out.dtype)
        return carry

    lax.fori_loop(0, out.shape[0] // tile, step, 0)
    sub = rows_here // dp
    for g in range(2):
        for z in range(pairs):
            at = (2 * z + g) * rows_here + me * sub
            spot = (g * pairs + z) * sub
            part[spot : spot + sub, :] = out[pl.ds(pl.multiple_of(at, sub), sub), :]


def columns_body(ids, values, own, other):
    rows, cols = values.shape[0], own.shape[1]
    for k in range(own.shape[0] // rows):
        span, at = slice(k * rows, (k + 1) * rows), 2 * (ids[1] ^ k)
        own[span, :] = values[:, aligned(at + ids[2], cols)]
        other[span, :] = values[:, aligned(at + 1 - ids[2], cols)]


def halves_body(ids, own, got, *outs):
    rows = outs[0].shape[0] // 2
    for k, out in enumerate(outs):
        span = slice(k * rows, (k + 1) * rows)
        out[:rows, :] = own[span, :]
        out[rows:, :] = got[span, :]


def dot(a, b, dim_a=1, dim_b=0):
    return lax.dot_general(
        a, b, (((dim_a,), (dim_b,)), ((), ())), preferred_element_type=jnp.float32
    )


def join_body(ids, *refs):
    pieces, out = refs[:-1], refs[-1]
    rows = pieces[0].shape[0]
    for k, piece in enumerate(pieces):
        out[k * rows : (k + 1) * rows, :] = piece[...]


def gate_body(ids, *refs):
    pieces, (others, weight, first, second, stage) = refs[:-5], refs[-5:]
    dp, rows = len(pieces), stage.shape[1]
    cols = weight.shape[1]
    own, other = weight[aligned(ids[2], cols), :], weight[aligned(1 - ids[2], cols), :]
    for k, piece in enumerate(pieces):
        term = dot(piece[...], own) + dot(others[k * rows : (k + 1) * rows, :], other)
        stage[ids[1] ^ k] = term.astype(stage.dtype)
    half = dp // 2
    for e in range(half):
        first[e * rows : (e + 1) * rows, :] = stage[e]
        second[e * rows : (e + 1) * rows, :] = stage[half + e]


def add_body(ids, a, a_got, b, b_got, a_keep, b_keep, a_send, b_send, token):
    sign(token)
    f32 = jnp.float32
    for x, got, keep, send in ((a, a_got, a_keep, a_send), (b, b_got, b_keep, b_send)):
        keep[...] = (x[...].astype(f32) + got[...].astype(f32)).astype(keep.dtype)
        send[...] = keep[...]


def gate_value_of(stage, a0, a1, b0, b1):
    half = a0.shape[0]
    stage[:half, :] = a0[...].astype(jnp.float32) + a1[...].astype(jnp.float32)
    stage[half:, :] = b0[...].astype(jnp.float32) + b1[...].astype(jnp.float32)


def values_body(ids, a0, a1, b0, b1, sent, part, mem_grad, factor, value_own, keep, send, token, stage):
    tokens = value_own.shape[0]
    gate_value_of(stage, a0, a1, b0, b1)
    for k in range(sent.shape[0]):
        span = aligned(ids[0] ^ k, tokens)
        gate = stage[span, :]
        s = jax.nn.sigmoid(gate)
        upstream = sent[ids[0] ^ k, :tokens, :].astype(jnp.float32)
        mem_grad[span, :] = (upstream * (gate * s)).astype(mem_grad.dtype)
        factor[span, :] = upstream * (s * (1.0 + gate * (1.0 - s)))
        if k == 0:
            value_own[...] = gate * s
    half = keep.shape[0]
    term = dot(part[...], mem_grad[...])
    keep[...] = term[:half].astype(keep.dtype)
    send[...] = term[half:].astype(send.dtype)
    sign(token)


def messages_body(ids, keep, got, *refs):
    messages, token = refs[:-1], refs[-1]
    sign(token)
    sub = messages[0].shape[0] // 2
    for z, message in enumerate(messages):
        message[:sub, :] = keep[z * sub : (z + 1) * sub, :]
        message[sub:, :] = got[z * sub : (z + 1) * sub, :]


def grads_body(rows_here, ids, factor, value_own, spread_ref, mem_grad, rows_ref, *refs):
    values, (weight, gate_grad, branch, term, packed) = refs[:-5], refs[-5:]
    every = gate_grad.shape[0]
    tokens, rows = branch.shape[0], values[0].shape[0]
    for k in range(factor.shape[0] // tokens):
        span = aligned(ids[0] ^ k, tokens)
        memory = 0.0
        for i, piece in enumerate(values):
            memory = memory + dot(spread_ref[i * rows : (i + 1) * rows, span], piece[...], 0, 0)
        gate_grad[span, :] = (factor[span, :] * memory).astype(gate_grad.dtype)
        if k == 0:
            branch[...] = (memory * value_own[...]).astype(branch.dtype)
    across = weight[aligned(1 - ids[2], weight.shape[1]), :]
    term[:every, :] = dot(gate_grad[...], across, 1, 1).astype(term.dtype)
    term[every:, :] = affinity_part(rows_here, ids, mem_grad, values, rows_ref, packed)


def affinity_part(rows_here, ids, mem_grad, values, rows, packed):
    f32 = jnp.float32
    tokens = rows.shape[1]
    count = rows.shape[0]
    at = moved(rows[...], rows_here, ids[1], ids[2])
    at = jnp.concatenate([at] * (tokens // count), axis=0).T
    inner, outer = at & 127, at >> 7
    grads = mem_grad[aligned(ids[0], tokens), :]
    found = jnp.zeros(at.shape, f32)
    blocks = values[0].shape[0] // 128
    for j, table in enumerate(values):
        all_rows = dot(grads, table[...], 1, 1)
        for i in range(blocks):
            hit = jnp.take_along_axis(all_rows[:, i * 128 : (i + 1) * 128], inner, axis=1)
            found = jnp.where(outer == j * blocks + i, hit, found)
    affinity = found.T[:count]
    high = affinity.astype(jnp.bfloat16).astype(f32)
    pack_rows(packed, 0, high)
    pack_rows(packed, count, affinity - high)
    return packed[...].astype(jnp.bfloat16)


def inputs_body(ids, gate_grad, weight, term, arrived, *refs):
    f32 = jnp.float32
    outs, token = refs[:-1], refs[-1]
    sign(token)
    every = gate_grad.shape[0]
    whole = term[every:, :].astype(f32) + arrived[every:, :].astype(f32)
    extra = whole.shape[0]
    whole = whole[: extra // 2] + whole[extra // 2 :]
    high = whole.astype(jnp.bfloat16).astype(f32)
    affinity = jnp.concatenate([high, whole - high], axis=0).astype(jnp.bfloat16)
    tokens = outs[0].shape[0] - extra
    own = weight[aligned(ids[2], weight.shape[1]), :]
    for i, out in enumerate(outs):
        span = aligned(ids[1] ^ i, tokens)
        total_term = dot(gate_grad[span, :], own, 1, 1) + arrived[span, :].astype(f32)
        out[:tokens, :] = total_term.astype(out.dtype)
        out[tokens:, :] = affinity


def sums_body(ids, *refs):
    pieces, (weights, out, grads) = refs[:-3], refs[-3:]
    whole = 0.0
    for piece in pieces:
        whole = whole + piece[...].astype(jnp.float32)
    tokens = out.shape[0]
    out[...] = whole[:tokens].astype(out.dtype)
    half = (whole.shape[0] - tokens) // 2
    whole = whole[tokens : tokens + half] + whole[tokens + half :]
    w = weights[...]
    count, lanes = w.shape
    affinity = jnp.concatenate([row_of(whole, k, lanes) for k in range(count)], axis=0)
    grads[...] = w * (affinity - jnp.sum(w * affinity, axis=0, keepdims=True))


def rows_body(ids, *refs):
    back, halves = refs[:-2], refs[-2:]
    cols = back[0].shape[1]
    sub, half = back[0].shape[0] // 2, halves[0].shape[0]
    for z, piece in enumerate(back):
        for j, out in enumerate(halves):
            at = 2 * (ids[1] ^ z)
            span = slice(j * half, (j + 1) * half)
            out[:, aligned(at + ids[2], cols)] = piece[span, :]
            out[:, aligned(at + 1 - ids[2], cols)] = piece[sub + j * half : sub + (j + 1) * half, :]


def widen_body(ids, *refs):
    pieces, (out, token) = refs[:-2], refs[-2:]
    sign(token)
    half, count = pieces[0].shape[0], len(pieces) // 2
    for k, piece in enumerate(pieces):
        at = (ids[0] ^ (k % count)) * 2 * half + k // count * half
        out[pl.ds(pl.multiple_of(at, half), half), :] = piece[...].astype(out.dtype)


def widen(ids, pieces):
    rows, width = pieces[0].shape
    cols = width // 4
    return pl.pallas_call(
        widen_body,
        grid=(width // cols,),
        in_specs=[pl.BlockSpec(memory_space=pltpu.SMEM)]
        + [pl.BlockSpec((rows, cols), lambda i: (0, i))] * len(pieces),
        out_specs=[
            pl.BlockSpec((len(pieces) * rows, cols), lambda i: (0, i)),
            pl.BlockSpec(TOKEN.shape, lambda i: (0, 0)),
        ],
        out_shape=[shape((len(pieces) * rows, width), jnp.float32), TOKEN],
        compiler_params=pltpu.CompilerParams(vmem_limit_bytes=12 << 20),
        cost_estimate=pl.CostEstimate(flops=0, bytes_accessed=0, transcendentals=0),
    )(ids, *pieces)


def gate_grads_body(ids, *refs):
    pieces, (others, gate_grad, out, token) = refs[:-4], refs[-4:]
    sign(token)
    tokens = pieces[0].shape[0]
    for j in range(2):

        @pl.when(pl.program_id(0) == j)
        def _():
            acc = 0.0
            for k, piece in enumerate(pieces):
                grads = gate_grad[aligned(ids[1] ^ k, tokens), :]
                part = others[k * tokens : (k + 1) * tokens, :] if j else piece[...]
                acc = acc + dot(part, grads, 0, 0)
            out[...] = acc


def gate_grads(ids, pieces, others, gate_grad, after):
    cols = gate_grad.shape[1]
    vmem = pl.BlockSpec(memory_space=pltpu.VMEM)
    count = len(pieces) + 2

    def whole_body(ids, *refs):
        gate_grads_body(ids, *refs[:count], *refs[count + 1 :])

    return pl.pallas_call(
        whole_body,
        grid_spec=pltpu.PrefetchScalarGridSpec(
            num_scalar_prefetch=1,
            grid=(2,),
            in_specs=[vmem] * (count + 1),
            out_specs=[
                pl.BlockSpec((cols, cols), lambda j, ids: (ids[2] ^ j, 0)),
                pl.BlockSpec(TOKEN.shape, lambda j, ids: (0, 0)),
            ],
        ),
        out_shape=[shape((2 * cols, cols), jnp.float32), TOKEN],
        compiler_params=pltpu.CompilerParams(vmem_limit_bytes=12 << 20),
        cost_estimate=pl.CostEstimate(flops=0, bytes_accessed=0, transcendentals=0),
    )(ids, *pieces, others, gate_grad, after)


def local_square(dp, pairs, hidden_in, gate_weight, values, pick_rows, pick_scores, grad_out):
    tokens, cols = hidden_in.shape
    rows_here, width = values.shape
    picks = pick_rows.shape[1]
    sub = rows_here // dp
    f32 = jnp.float32
    me, pair, core = (lax.axis_index(a) for a in ("dp",) + TABLE)
    ids = jnp.stack([me, pair, core]).astype(jnp.int32)
    every = dp * tokens

    mine = []
    for k in range(dp):
        perm = [
            ((e * pairs + z) * 2 + h, (z * pairs + (e ^ k)) * 2 + h)
            for e in range(dp)
            for z in range(pairs)
            for h in range(2)
        ]
        mine.append(lax.ppermute(hidden_in, ("dp",) + TABLE, perm))
    rows_t = pick_rows.T
    small = -(-3 * picks * tokens // cols // 16) * 16
    sent, weights_t = kernel_call(
        prepare_body,
        [shape((tokens + small, cols)), shape((picks, tokens), f32)],
        ids, pick_scores.T, rows_t, grad_out,
        scratch=[pltpu.VMEM((small, cols), f32)],
    )
    sent_own = sent
    sent = lax.all_gather(sent_own, "dp", axis=0)
    joined = kernel_call(join_body, [shape((every, cols))], ids, *mine)[0]
    others = hop(joined, "core", 2, 1)
    first, second = kernel_call(
        gate_body,
        [shape((every // 2, cols))] * 2,
        ids, *mine, others, gate_weight,
        scratch=[pltpu.VMEM((dp, tokens, cols), jnp.bfloat16)],
    )
    value_own, value_send = kernel_call(
        columns_body, [shape((pairs * rows_here, cols))] * 2, ids, values
    )
    value_sent = kernel_call(
        halves_body, [shape((2 * rows_here, cols))] * pairs,
        ids, value_own, hop(value_send, "core", 2, 1),
    )
    value_got = swap(value_sent, "pair", pairs)
    first, second, *added, token = kernel_call(
        add_body,
        [shape((every // 2, cols))] * 4 + [TOKEN],
        ids, first, hop(first, "dp", dp, 1), second, hop(second, "dp", dp, 2),
        after=[sent] + value_got[1:3],
    )
    spread_all, spread_part = kernel_call(
        functools.partial(spread_body, picks, rows_here),
        [shape((2 * pairs * rows_here, every)), shape((2 * pairs * sub, every))],
        ids, sent,
        scratch=[pltpu.VMEM((picks, every), jnp.int32), pltpu.VMEM((picks, every), f32)],
        after=[token],
    )
    gates = [first, hop(added[0], "dp", dp, 2), second, hop(added[1], "dp", dp, 1)]

    mem_grad, factor, value_part, keep, send, token = kernel_call(
        values_body,
        [shape((every, cols)), shape((every, cols), f32), shape((tokens, cols), f32)]
        + [shape((pairs * sub, cols))] * 2
        + [TOKEN],
        ids, *gates, sent, spread_part,
        scratch=[pltpu.VMEM((every, cols), f32)],
    )
    *messages, sent_on = kernel_call(
        messages_body, [shape((2 * sub, cols))] * pairs + [TOKEN], ids, keep, hop(send, "core", 2, 1)
    )

    back = swap(messages, "pair", pairs)
    extra = 2 * picks * tokens // cols
    gate_grad, branch_out, term = kernel_call(
        functools.partial(grads_body, rows_here),
        [shape((every, cols)), shape((tokens, cols)), shape((every + extra, cols))],
        ids, factor, value_part, spread_all, mem_grad, rows_t, *value_got, gate_weight,
        scratch=[pltpu.VMEM((extra, cols), f32)],
        after=[sent_on],
    )
    *inputs, sent_inputs = kernel_call(
        inputs_body,
        [shape((tokens + extra, cols))] * pairs + [TOKEN],
        ids, gate_grad, gate_weight, term, hop(term, "core", 2, 1),
        after=back[1:2],
    )
    grad_gate, done = gate_grads(ids, mine, others, gate_grad, sent_inputs)
    grad_hidden, grad_scores = kernel_call(
        sums_body,
        [shape((tokens, cols)), shape((picks, tokens), f32)],
        ids, *swap(inputs, "pair", pairs), weights_t, after=[done],
    )
    perm = [
        ((d * pairs + z) * 2 + h, (z * pairs + d) * 2 + h)
        for d in range(dp)
        for z in range(pairs)
        for h in range(2)
    ]
    grad_hidden = lax.ppermute(grad_hidden, ("dp",) + TABLE, perm)
    first, second = kernel_call(
        rows_body, [shape((sub // 2, width))] * 2, ids, *back, after=[sent_inputs]
    )
    along_x, along_y = hop(first, "dp", dp, 1), hop(second, "dp", dp, 2)
    first = [first, along_x, hop(first, "dp", dp, 2), hop(along_x, "dp", dp, 2)]
    second = [second, hop(second, "dp", dp, 1), along_y, hop(along_y, "dp", dp, 1)]
    grad_values, token = widen(ids, first + second)
    return (branch_out, grad_hidden, grad_gate, grad_values, grad_scores.T)


def local(dp, pairs, *args):
    tokens, cols = args[0].shape
    square = dp == pairs == DIRECT and tokens == 128 and cols == 4 * tokens
    return (local_square if square else local_general)(dp, pairs, *args)


def solution(mesh):
    dp, table = mesh.shape["dp"], mesh.shape["table"]
    pairs = Mesh(mesh.devices.reshape(dp, table // 2, 2), ("dp",) + TABLE)
    split, rows, tokens = P("dp", TABLE), P(TABLE, None), P("dp", None)
    return jax.shard_map(
        functools.partial(local, dp, table // 2),
        mesh=pairs,
        in_specs=(split, split, rows, tokens, tokens, split),
        out_specs=(split, split, split, rows, tokens),
        check_vma=False,
    )
```

```python
import functools

import jax
import jax.numpy as jnp
from jax import lax
from jax.experimental import pallas as pl
from jax.experimental.pallas import tpu as pltpu
from jax.sharding import Mesh
from jax.sharding import PartitionSpec as P

DIRECT = 4
TABLE = ("pair", "core")


def block(x, index):
    return lax.dynamic_index_in_dim(x, index, 0, keepdims=False)


def placed(pieces, indices):
    out = jnp.zeros((len(pieces),) + pieces[0].shape, pieces[0].dtype)
    for piece, index in zip(pieces, indices):
        out = lax.dynamic_update_index_in_dim(out, piece, index, 0)
    return out


def hop(x, axis, size, mask):
    return lax.ppermute(x, axis, [(i, i ^ mask) for i in range(size)])


def order(axis, size):
    return [lax.axis_index(axis) ^ k for k in range(size)]


def gather(x, axis, size):
    if size <= DIRECT:
        return [x] + [hop(x, axis, size, k) for k in range(1, size)]
    whole = lax.all_gather(x, axis, axis=0)
    return [block(whole, k) for k in order(axis, size)]


def swap(pieces, axis, size):
    if size <= DIRECT:
        return [pieces[0]] + [hop(pieces[k], axis, size, k) for k in range(1, size)]
    ids = order(axis, size)
    whole = lax.all_to_all(placed(pieces, ids), axis, split_axis=0, concat_axis=0)
    return [block(whole, k) for k in ids]


def exchange(x, axis):
    return lax.all_to_all(x, axis, split_axis=0, concat_axis=0, tiled=True)


def total(terms):
    return functools.reduce(jnp.add, [t.astype(jnp.float32) for t in terms])


def spread_kernel(rows_ref, weights_ref, out_ref):
    tile = 32
    tokens = rows_ref.shape[1]

    def step(i, carry):
        base = pl.multiple_of(i * tile, tile)
        here = lax.broadcasted_iota(jnp.int32, (tile, tokens), 0) + base
        total = jnp.zeros((tile, tokens), jnp.float32)
        for k in range(rows_ref.shape[0]):
            hit = rows_ref[k : k + 1, :] == here
            total = jnp.where(hit, weights_ref[k : k + 1, :], total)
        out_ref[pl.ds(base, tile), :] = total.astype(out_ref.dtype)
        return carry

    lax.fori_loop(0, out_ref.shape[0] // tile, step, 0)


def spread(rows, weights, row_total):
    picks, tokens = rows.shape
    width = min(tokens, 512)
    return pl.pallas_call(
        spread_kernel,
        grid=(tokens // width,),
        in_specs=[pl.BlockSpec((picks, width), lambda i: (0, i))] * 2,
        out_specs=pl.BlockSpec((row_total, width), lambda i: (0, i)),
        out_shape=jax.ShapeDtypeStruct((row_total, tokens), jnp.bfloat16),
        compiler_params=pltpu.CompilerParams(vmem_limit_bytes=16 << 20),
        cost_estimate=pl.CostEstimate(
            flops=2 * picks * tokens * row_total,
            bytes_accessed=2 * tokens * row_total,
            transcendentals=0,
        ),
    )(rows, weights)


def pick_kernel(table_ref, rows_ref, out_ref):
    lanes = 128
    rows = rows_ref[...]
    inner = rows & (lanes - 1)
    outer = rows >> 7
    total = jnp.zeros(out_ref.shape, jnp.float32)
    for j in range(table_ref.shape[1] // lanes):
        part = table_ref[:, j * lanes : (j + 1) * lanes]
        found = jnp.take_along_axis(part, inner, axis=1)
        total = jnp.where(outer == j, found, total)
    out_ref[...] = total


def pick(table, rows):
    return pl.pallas_call(
        pick_kernel,
        out_shape=jax.ShapeDtypeStruct(rows.shape, jnp.float32),
        cost_estimate=pl.CostEstimate(
            flops=rows.size * 16, bytes_accessed=4 * table.size, transcendentals=0
        ),
    )(table, rows)


def pick_weights(pick_scores):
    row_max = jnp.max(pick_scores, axis=1, keepdims=True)
    exponent = jnp.exp(pick_scores - row_max)
    return exponent / jnp.sum(exponent, axis=1, keepdims=True)


def contract(a, b, dim_a, dim_b):
    return lax.dot_general(
        a, b, (((dim_a,), (dim_b,)), ((), ())), preferred_element_type=jnp.float32
    )


def local_general(dp, pairs, hidden_in, gate_weight, values, pick_rows, pick_scores, grad_out):
    tokens, cols = hidden_in.shape
    rows_here, width = values.shape
    picks = pick_rows.shape[1]
    table = 2 * pairs
    sub = rows_here // dp
    me, pair, core = (lax.axis_index(a) for a in ("dp",) + TABLE)
    here = 2 * pair + core
    f32, bf16 = jnp.float32, jnp.bfloat16

    wide = lax.all_gather(hidden_in, TABLE, axis=1, tiled=True)
    wide = wide.reshape(tokens, dp, table * cols // dp).transpose(1, 0, 2)
    hidden_all = exchange(wide, "dp").reshape(dp * tokens, -1)

    weights = pick_weights(pick_scores)
    weights_bf = weights.astype(bf16)
    small = jnp.concatenate([weights_bf, (pick_rows >> 5).astype(bf16), (pick_rows & 31).astype(bf16)], axis=1)
    small = small.T.reshape(-1, cols)
    sent = lax.all_gather(jnp.concatenate([grad_out, small], axis=0), "dp", axis=0)
    grad_out_all = sent[:, :tokens].reshape(dp * tokens, cols)
    small = sent[:, tokens:].reshape(dp, 3, picks, tokens).transpose(1, 2, 0, 3)
    small = small.reshape(3, picks, dp * tokens).astype(f32)
    rows_all = small[1].astype(jnp.int32) * 32 + small[2].astype(jnp.int32)

    def moved_row(row):
        return ((row // rows_here) ^ here) * rows_here + row % rows_here

    spread_all = spread(moved_row(rows_all), small[0], rows_here * table)

    by_core = values.reshape(rows_here, pairs, 2, cols).transpose(2, 1, 0, 3)
    mine = block(by_core, core)
    other = hop(block(by_core, 1 - core), "core", 2, 1)
    value_sent = [
        jnp.concatenate([block(mine, z), block(other, z)], axis=0) for z in order("pair", pairs)
    ]
    value_cols = jnp.concatenate(swap(value_sent, "pair", pairs), axis=0)

    partial_gate = contract(hidden_all, gate_weight, 1, 0).astype(bf16)
    terms = exchange(partial_gate.reshape(dp, tokens, cols), "dp")
    gate_own = total([terms[k] for k in range(dp)]).astype(bf16)
    gate_input = lax.all_gather(gate_own, "dp", axis=0, tiled=True).astype(f32)

    memory_read = contract(spread_all, value_cols, 0, 0)
    sigmoid_v = jax.nn.sigmoid(gate_input)
    gate_value = gate_input * sigmoid_v
    gate_slope = sigmoid_v * (1.0 + gate_input * (1.0 - sigmoid_v))
    upstream = grad_out_all.astype(f32)
    mem_grad = (upstream * gate_value).astype(bf16)
    gate_grad_in = (upstream * memory_read * gate_slope).astype(bf16)

    def own(x):
        return block(x.reshape(dp, tokens, cols), me)

    branch_out = (own(memory_read) * own(gate_value)).astype(bf16)

    input_term = contract(gate_grad_in, gate_weight, 1, 1).astype(bf16)
    input_got = exchange(input_term.reshape(dp, tokens, -1), "dp")

    spread_parts = spread_all.reshape(pairs, 2, dp, sub, dp * tokens)
    part = jnp.concatenate(
        [
            lax.dynamic_slice(
                spread_parts, (z ^ pair, 0, me, 0, 0), (1, 2, 1, sub, dp * tokens)
            ).reshape(2 * sub, dp * tokens)
            for z in range(pairs)
        ],
        axis=0,
    )
    value_term = contract(part, mem_grad, 1, 0).astype(bf16).reshape(pairs, 2, sub, cols)
    value_other = hop(value_term[:, 1], "core", 2, 1)

    affinity_all = contract(own(mem_grad), value_cols, 1, 1)
    own_rows = jnp.pad(moved_row(pick_rows), ((0, 0), (0, 128 - picks)))
    affinity = pick(affinity_all, own_rows)[:, :picks]
    affinity = affinity + hop(affinity, "core", 2, 1)
    high = affinity.astype(bf16)
    low = (affinity - high.astype(f32)).astype(bf16)
    parts = jnp.concatenate([high, low], axis=1).reshape(-1, cols)

    back = exchange(
        jnp.concatenate(
            [value_term[:, 0], value_other, jnp.broadcast_to(parts, (pairs,) + parts.shape)], axis=1
        ),
        "pair",
    )
    affinity = back[:, 2 * sub :].reshape(pairs, tokens, 2 * picks).astype(f32)
    affinity = jnp.sum(affinity[:, :, :picks] + affinity[:, :, picks:], axis=0)
    grad_scores = weights * (affinity - jnp.sum(weights * affinity, axis=1, keepdims=True))

    first, second = back[:, :sub], back[:, sub : 2 * sub]
    back = jnp.stack(
        [jnp.where(core == 0, first, second), jnp.where(core == 0, second, first)], axis=1
    )
    back = back.transpose(2, 0, 1, 3).reshape(sub, width)
    grad_values = placed(
        [r.astype(f32) for r in gather(back, "dp", dp)], order("dp", dp)
    ).reshape(rows_here, width)

    wide = input_got.transpose(1, 0, 2).reshape(tokens, table, cols)
    input_terms = exchange(wide.transpose(1, 0, 2), TABLE)
    grad_hidden = total([input_terms[k] for k in range(table)]).astype(bf16)
    grad_gate = contract(hidden_all, gate_grad_in, 0, 0)
    return (branch_out, grad_hidden, grad_gate, grad_values, grad_scores)


def kernel_call(body, outs, *args, scratch=(), after=()):
    count = len(args)

    def whole_body(*refs):
        body(*refs[:count], *refs[count + len(after) :])

    vmem = pl.BlockSpec(memory_space=pltpu.VMEM)
    return pl.pallas_call(
        whole_body,
        in_specs=[pl.BlockSpec(memory_space=pltpu.SMEM)] + [vmem] * (count + len(after) - 1),
        out_specs=[vmem] * len(outs),
        out_shape=list(outs),
        scratch_shapes=list(scratch),
        compiler_params=pltpu.CompilerParams(vmem_limit_bytes=12 << 20),
        cost_estimate=pl.CostEstimate(flops=0, bytes_accessed=0, transcendentals=0),
    )(*args, *after)


def shape(dims, dtype=jnp.bfloat16):
    return jax.ShapeDtypeStruct(dims, dtype)


TOKEN = shape((8, 128), jnp.float32)


def sign(token):
    token[...] = jnp.zeros(token.shape, token.dtype)


def aligned(index, size):
    return pl.ds(pl.multiple_of(index * size, size), size)


def pack_rows(out_ref, first, x):
    count, lanes = x.shape
    per = out_ref.shape[1] // lanes
    for j in range(count):
        row, lane = (first + j) // per, (first + j) % per * lanes
        out_ref[row : row + 1, lane : lane + lanes] = x[j : j + 1, :]


def row_of(packed, j, lanes):
    per = packed.shape[1] // lanes
    return packed[j // per : j // per + 1, j % per * lanes : (j % per + 1) * lanes]


def prepare_body(ids, scores, rows, grad_out, sent, weights, packed):
    tokens = grad_out.shape[0]
    x = scores[...]
    exponent = jnp.exp(x - jnp.max(x, axis=0, keepdims=True))
    w = exponent / jnp.sum(exponent, axis=0, keepdims=True)
    weights[...] = w
    packed[...] = jnp.zeros(packed.shape, packed.dtype)
    count = w.shape[0]
    pack_rows(packed, 0, w)
    pack_rows(packed, count, (rows[...] >> 5).astype(jnp.float32))
    pack_rows(packed, 2 * count, (rows[...] & 31).astype(jnp.float32))
    sent[:tokens, :] = grad_out[...]
    sent[tokens:, :] = packed[...].astype(sent.dtype)


def moved(row, rows_here, pair, core):
    owner, inner = lax.div(row, rows_here), lax.rem(row, rows_here)
    return (owner ^ (2 * pair + core)) * rows_here + inner


def spread_body(picks, rows_here, ids, sent, out, part, rows, weights):
    me, pair, core = ids[0], ids[1], ids[2]
    dp = sent.shape[0]
    tokens = rows.shape[1] // dp
    pairs = part.shape[0] // (2 * (rows_here // dp))
    for e in range(dp):
        packed = sent[e, tokens:, :].astype(jnp.float32)
        span = slice(e * tokens, (e + 1) * tokens)
        for k in range(picks):
            weights[k : k + 1, span] = row_of(packed, k, tokens)
            high, low = row_of(packed, picks + k, tokens), row_of(packed, 2 * picks + k, tokens)
            rows[k : k + 1, span] = (high * 32.0 + low).astype(jnp.int32)
    rows[...] = moved(rows[...], rows_here, pair, core)
    tile = 32

    def step(i, carry):
        base = pl.multiple_of(i * tile, tile)
        here = lax.broadcasted_iota(jnp.int32, (tile, rows.shape[1]), 0) + base
        acc = jnp.zeros((tile, rows.shape[1]), jnp.float32)
        for k in range(picks):
            acc = jnp.where(rows[k : k + 1, :] == here, weights[k : k + 1, :], acc)
        out[pl.ds(base, tile), :] = acc.astype(out.dtype)
        return carry

    lax.fori_loop(0, out.shape[0] // tile, step, 0)
    sub = rows_here // dp
    for g in range(2):
        for z in range(pairs):
            at = (2 * z + g) * rows_here + me * sub
            spot = (g * pairs + z) * sub
            part[spot : spot + sub, :] = out[pl.ds(pl.multiple_of(at, sub), sub), :]


def columns_body(ids, values, own, other):
    rows, cols = values.shape[0], own.shape[1]
    for k in range(own.shape[0] // rows):
        span, at = slice(k * rows, (k + 1) * rows), 2 * (ids[1] ^ k)
        own[span, :] = values[:, aligned(at + ids[2], cols)]
        other[span, :] = values[:, aligned(at + 1 - ids[2], cols)]


def halves_body(ids, own, got, *outs):
    rows = outs[0].shape[0] // 2
    for k, out in enumerate(outs):
        span = slice(k * rows, (k + 1) * rows)
        out[:rows, :] = own[span, :]
        out[rows:, :] = got[span, :]


def dot(a, b, dim_a=1, dim_b=0):
    return lax.dot_general(
        a, b, (((dim_a,), (dim_b,)), ((), ())), preferred_element_type=jnp.float32
    )


def join_body(ids, *refs):
    pieces, out = refs[:-1], refs[-1]
    rows = pieces[0].shape[0]
    for k, piece in enumerate(pieces):
        out[k * rows : (k + 1) * rows, :] = piece[...]


def gate_body(ids, *refs):
    pieces, (others, weight, first, second, stage) = refs[:-5], refs[-5:]
    dp, rows = len(pieces), stage.shape[1]
    cols = weight.shape[1]
    own, other = weight[aligned(ids[2], cols), :], weight[aligned(1 - ids[2], cols), :]
    for k, piece in enumerate(pieces):
        term = dot(piece[...], own) + dot(others[k * rows : (k + 1) * rows, :], other)
        stage[ids[1] ^ k] = term.astype(stage.dtype)
    half = dp // 2
    for e in range(half):
        first[e * rows : (e + 1) * rows, :] = stage[e]
        second[e * rows : (e + 1) * rows, :] = stage[half + e]


def add_body(ids, a, a_got, b, b_got, a_keep, b_keep, a_send, b_send, token):
    sign(token)
    f32 = jnp.float32
    for x, got, keep, send in ((a, a_got, a_keep, a_send), (b, b_got, b_keep, b_send)):
        keep[...] = (x[...].astype(f32) + got[...].astype(f32)).astype(keep.dtype)
        send[...] = keep[...]


def gate_value_of(stage, a0, a1, b0, b1):
    half = a0.shape[0]
    stage[:half, :] = a0[...].astype(jnp.float32) + a1[...].astype(jnp.float32)
    stage[half:, :] = b0[...].astype(jnp.float32) + b1[...].astype(jnp.float32)


def values_body(ids, a0, a1, b0, b1, sent, part, mem_grad, factor, value_own, keep, send, token, stage):
    tokens = value_own.shape[0]
    gate_value_of(stage, a0, a1, b0, b1)
    for k in range(sent.shape[0]):
        span = aligned(ids[0] ^ k, tokens)
        gate = stage[span, :]
        s = jax.nn.sigmoid(gate)
        upstream = sent[ids[0] ^ k, :tokens, :].astype(jnp.float32)
        mem_grad[span, :] = (upstream * (gate * s)).astype(mem_grad.dtype)
        factor[span, :] = upstream * (s * (1.0 + gate * (1.0 - s)))
        if k == 0:
            value_own[...] = gate * s
    half = keep.shape[0]
    term = dot(part[...], mem_grad[...])
    keep[...] = term[:half].astype(keep.dtype)
    send[...] = term[half:].astype(send.dtype)
    sign(token)


def messages_body(ids, keep, got, *refs):
    messages, token = refs[:-1], refs[-1]
    sign(token)
    sub = messages[0].shape[0] // 2
    for z, message in enumerate(messages):
        message[:sub, :] = keep[z * sub : (z + 1) * sub, :]
        message[sub:, :] = got[z * sub : (z + 1) * sub, :]


def grads_body(rows_here, ids, factor, value_own, spread_ref, mem_grad, rows_ref, *refs):
    values, (weight, gate_grad, branch, term, packed) = refs[:-5], refs[-5:]
    every = gate_grad.shape[0]
    tokens, rows = branch.shape[0], values[0].shape[0]
    for k in range(factor.shape[0] // tokens):
        span = aligned(ids[0] ^ k, tokens)
        memory = 0.0
        for i, piece in enumerate(values):
            memory = memory + dot(spread_ref[i * rows : (i + 1) * rows, span], piece[...], 0, 0)
        gate_grad[span, :] = (factor[span, :] * memory).astype(gate_grad.dtype)
        if k == 0:
            branch[...] = (memory * value_own[...]).astype(branch.dtype)
    across = weight[aligned(1 - ids[2], weight.shape[1]), :]
    term[:every, :] = dot(gate_grad[...], across, 1, 1).astype(term.dtype)
    term[every:, :] = affinity_part(rows_here, ids, mem_grad, values, rows_ref, packed)


def affinity_part(rows_here, ids, mem_grad, values, rows, packed):
    f32 = jnp.float32
    tokens = rows.shape[1]
    count = rows.shape[0]
    at = moved(rows[...], rows_here, ids[1], ids[2])
    at = jnp.concatenate([at] * (tokens // count), axis=0).T
    inner, outer = at & 127, at >> 7
    grads = mem_grad[aligned(ids[0], tokens), :]
    found = jnp.zeros(at.shape, f32)
    blocks = values[0].shape[0] // 128
    for j, table in enumerate(values):
        all_rows = dot(grads, table[...], 1, 1)
        for i in range(blocks):
            hit = jnp.take_along_axis(all_rows[:, i * 128 : (i + 1) * 128], inner, axis=1)
            found = jnp.where(outer == j * blocks + i, hit, found)
    affinity = found.T[:count]
    high = affinity.astype(jnp.bfloat16).astype(f32)
    pack_rows(packed, 0, high)
    pack_rows(packed, count, affinity - high)
    return packed[...].astype(jnp.bfloat16)


def inputs_body(ids, gate_grad, weight, term, arrived, *refs):
    f32 = jnp.float32
    outs, token = refs[:-1], refs[-1]
    sign(token)
    every = gate_grad.shape[0]
    whole = term[every:, :].astype(f32) + arrived[every:, :].astype(f32)
    extra = whole.shape[0]
    whole = whole[: extra // 2] + whole[extra // 2 :]
    high = whole.astype(jnp.bfloat16).astype(f32)
    affinity = jnp.concatenate([high, whole - high], axis=0).astype(jnp.bfloat16)
    tokens = outs[0].shape[0] - extra
    own = weight[aligned(ids[2], weight.shape[1]), :]
    for i, out in enumerate(outs):
        span = aligned(ids[1] ^ i, tokens)
        total_term = dot(gate_grad[span, :], own, 1, 1) + arrived[span, :].astype(f32)
        out[:tokens, :] = total_term.astype(out.dtype)
        out[tokens:, :] = affinity


def sums_body(ids, *refs):
    pieces, (out, affinity) = refs[:-2], refs[-2:]
    whole = 0.0
    for piece in pieces:
        whole = whole + piece[...].astype(jnp.float32)
    tokens = out.shape[0]
    out[...] = whole[:tokens].astype(out.dtype)
    half = (whole.shape[0] - tokens) // 2
    affinity[...] = whole[tokens : tokens + half] + whole[tokens + half :]


def scores_body(ids, whole_ref, weights, grads):
    whole, w = whole_ref[...], weights[...]
    count, lanes = w.shape
    affinity = jnp.concatenate([row_of(whole, k, lanes) for k in range(count)], axis=0)
    grads[...] = w * (affinity - jnp.sum(w * affinity, axis=0, keepdims=True))


def rows_body(ids, *refs):
    back, halves = refs[:-2], refs[-2:]
    cols = back[0].shape[1]
    sub, half = back[0].shape[0] // 2, halves[0].shape[0]
    for z, piece in enumerate(back):
        for j, out in enumerate(halves):
            at = 2 * (ids[1] ^ z)
            span = slice(j * half, (j + 1) * half)
            out[:, aligned(at + ids[2], cols)] = piece[span, :]
            out[:, aligned(at + 1 - ids[2], cols)] = piece[sub + j * half : sub + (j + 1) * half, :]


def widen_body(ids, *refs):
    pieces, (out, token) = refs[:-2], refs[-2:]
    sign(token)
    half, count = pieces[0].shape[0], len(pieces) // 2
    for k, piece in enumerate(pieces):
        at = (ids[0] ^ (k % count)) * 2 * half + k // count * half
        out[pl.ds(pl.multiple_of(at, half), half), :] = piece[...].astype(out.dtype)


def widen(ids, pieces):
    rows, width = pieces[0].shape
    cols = width // 4
    return pl.pallas_call(
        widen_body,
        grid=(width // cols,),
        in_specs=[pl.BlockSpec(memory_space=pltpu.SMEM)]
        + [pl.BlockSpec((rows, cols), lambda i: (0, i))] * len(pieces),
        out_specs=[
            pl.BlockSpec((len(pieces) * rows, cols), lambda i: (0, i)),
            pl.BlockSpec(TOKEN.shape, lambda i: (0, 0)),
        ],
        out_shape=[shape((len(pieces) * rows, width), jnp.float32), TOKEN],
        compiler_params=pltpu.CompilerParams(vmem_limit_bytes=12 << 20),
        cost_estimate=pl.CostEstimate(flops=0, bytes_accessed=0, transcendentals=0),
    )(ids, *pieces)


def gate_grads_body(ids, *refs):
    pieces, (others, gate_grad, out, token) = refs[:-4], refs[-4:]
    sign(token)
    tokens = pieces[0].shape[0]
    for j in range(2):

        @pl.when(pl.program_id(0) == j)
        def _():
            acc = 0.0
            for k, piece in enumerate(pieces):
                grads = gate_grad[aligned(ids[1] ^ k, tokens), :]
                part = others[k * tokens : (k + 1) * tokens, :] if j else piece[...]
                acc = acc + dot(part, grads, 0, 0)
            out[...] = acc


def gate_grads(ids, pieces, others, gate_grad, after):
    cols = gate_grad.shape[1]
    vmem = pl.BlockSpec(memory_space=pltpu.VMEM)
    count = len(pieces) + 2

    def whole_body(ids, *refs):
        gate_grads_body(ids, *refs[:count], *refs[count + 1 :])

    return pl.pallas_call(
        whole_body,
        grid_spec=pltpu.PrefetchScalarGridSpec(
            num_scalar_prefetch=1,
            grid=(2,),
            in_specs=[vmem] * (count + 1),
            out_specs=[
                pl.BlockSpec((cols, cols), lambda j, ids: (ids[2] ^ j, 0)),
                pl.BlockSpec(TOKEN.shape, lambda j, ids: (0, 0)),
            ],
        ),
        out_shape=[shape((2 * cols, cols), jnp.float32), TOKEN],
        compiler_params=pltpu.CompilerParams(vmem_limit_bytes=12 << 20),
        cost_estimate=pl.CostEstimate(flops=0, bytes_accessed=0, transcendentals=0),
    )(ids, *pieces, others, gate_grad, after)


def local_square(dp, pairs, hidden_in, gate_weight, values, pick_rows, pick_scores, grad_out):
    tokens, cols = hidden_in.shape
    rows_here, width = values.shape
    picks = pick_rows.shape[1]
    sub = rows_here // dp
    f32 = jnp.float32
    me, pair, core = (lax.axis_index(a) for a in ("dp",) + TABLE)
    ids = jnp.stack([me, pair, core]).astype(jnp.int32)
    every = dp * tokens

    mine = []
    for k in range(dp):
        perm = [
            ((e * pairs + z) * 2 + h, (z * pairs + (e ^ k)) * 2 + h)
            for e in range(dp)
            for z in range(pairs)
            for h in range(2)
        ]
        mine.append(lax.ppermute(hidden_in, ("dp",) + TABLE, perm))
    rows_t = pick_rows.T
    small = -(-3 * picks * tokens // cols // 16) * 16
    sent, weights_t = kernel_call(
        prepare_body,
        [shape((tokens + small, cols)), shape((picks, tokens), f32)],
        ids, pick_scores.T, rows_t, grad_out,
        scratch=[pltpu.VMEM((small, cols), f32)],
    )
    sent_own = sent
    sent = lax.all_gather(sent_own, "dp", axis=0)
    joined = kernel_call(join_body, [shape((every, cols))], ids, *mine)[0]
    others = hop(joined, "core", 2, 1)
    first, second = kernel_call(
        gate_body,
        [shape((every // 2, cols))] * 2,
        ids, *mine, others, gate_weight,
        scratch=[pltpu.VMEM((dp, tokens, cols), jnp.bfloat16)],
    )
    value_own, value_send = kernel_call(
        columns_body, [shape((pairs * rows_here, cols))] * 2, ids, values
    )
    value_sent = kernel_call(
        halves_body, [shape((2 * rows_here, cols))] * pairs,
        ids, value_own, hop(value_send, "core", 2, 1),
    )
    value_got = swap(value_sent, "pair", pairs)
    first, second, *added, token = kernel_call(
        add_body,
        [shape((every // 2, cols))] * 4 + [TOKEN],
        ids, first, hop(first, "dp", dp, 1), second, hop(second, "dp", dp, 2),
        after=[sent] + value_got[1:3],
    )
    spread_all, spread_part = kernel_call(
        functools.partial(spread_body, picks, rows_here),
        [shape((2 * pairs * rows_here, every)), shape((2 * pairs * sub, every))],
        ids, sent,
        scratch=[pltpu.VMEM((picks, every), jnp.int32), pltpu.VMEM((picks, every), f32)],
        after=[token],
    )
    gates = [first, hop(added[0], "dp", dp, 2), second, hop(added[1], "dp", dp, 1)]

    mem_grad, factor, value_part, keep, send, token = kernel_call(
        values_body,
        [shape((every, cols)), shape((every, cols), f32), shape((tokens, cols), f32)]
        + [shape((pairs * sub, cols))] * 2
        + [TOKEN],
        ids, *gates, sent, spread_part,
        scratch=[pltpu.VMEM((every, cols), f32)],
    )
    *messages, sent_on = kernel_call(
        messages_body, [shape((2 * sub, cols))] * pairs + [TOKEN], ids, keep, hop(send, "core", 2, 1)
    )

    back = swap(messages, "pair", pairs)
    extra = 2 * picks * tokens // cols
    gate_grad, branch_out, term = kernel_call(
        functools.partial(grads_body, rows_here),
        [shape((every, cols)), shape((tokens, cols)), shape((every + extra, cols))],
        ids, factor, value_part, spread_all, mem_grad, rows_t, *value_got, gate_weight,
        scratch=[pltpu.VMEM((extra, cols), f32)],
        after=[sent_on],
    )
    *inputs, sent_inputs = kernel_call(
        inputs_body,
        [shape((tokens + extra, cols))] * pairs + [TOKEN],
        ids, gate_grad, gate_weight, term, hop(term, "core", 2, 1),
        after=back[1:2],
    )
    grad_gate, done = gate_grads(ids, mine, others, gate_grad, sent_inputs)
    grad_hidden, affinity = kernel_call(
        sums_body,
        [shape((tokens, cols)), shape((extra // 2, cols), f32)],
        ids, *swap(inputs, "pair", pairs), after=[done],
    )
    grad_scores = kernel_call(
        scores_body, [shape((picks, tokens), f32)], ids, affinity, weights_t
    )[0]
    perm = [
        ((d * pairs + z) * 2 + h, (z * pairs + d) * 2 + h)
        for d in range(dp)
        for z in range(pairs)
        for h in range(2)
    ]
    grad_hidden = lax.ppermute(grad_hidden, ("dp",) + TABLE, perm)
    first, second = kernel_call(
        rows_body, [shape((sub // 2, width))] * 2, ids, *back, after=[sent_inputs]
    )
    along_x, along_y = hop(first, "dp", dp, 1), hop(second, "dp", dp, 2)
    first = [first, along_x, hop(first, "dp", dp, 2), hop(along_x, "dp", dp, 2)]
    second = [second, hop(second, "dp", dp, 1), along_y, hop(along_y, "dp", dp, 1)]
    grad_values, token = widen(ids, first + second)
    return (branch_out, grad_hidden, grad_gate, grad_values, grad_scores.T)


def local(dp, pairs, *args):
    tokens, cols = args[0].shape
    square = dp == pairs == DIRECT and tokens == 128 and cols == 4 * tokens
    return (local_square if square else local_general)(dp, pairs, *args)


def solution(mesh):
    dp, table = mesh.shape["dp"], mesh.shape["table"]
    pairs = Mesh(mesh.devices.reshape(dp, table // 2, 2), ("dp",) + TABLE)
    split, rows, tokens = P("dp", TABLE), P(TABLE, None), P("dp", None)
    return jax.shard_map(
        functools.partial(local, dp, table // 2),
        mesh=pairs,
        in_specs=(split, split, rows, tokens, tokens, split),
        out_specs=(split, split, split, rows, tokens),
        check_vma=False,
    )
```

```python
import functools

import jax
import jax.numpy as jnp
from jax import lax
from jax.experimental import pallas as pl
from jax.experimental.pallas import tpu as pltpu
from jax.sharding import Mesh
from jax.sharding import PartitionSpec as P

DIRECT = 4
TABLE = ("pair", "core")


def block(x, index):
    return lax.dynamic_index_in_dim(x, index, 0, keepdims=False)


def placed(pieces, indices):
    out = jnp.zeros((len(pieces),) + pieces[0].shape, pieces[0].dtype)
    for piece, index in zip(pieces, indices):
        out = lax.dynamic_update_index_in_dim(out, piece, index, 0)
    return out


def hop(x, axis, size, mask):
    return lax.ppermute(x, axis, [(i, i ^ mask) for i in range(size)])


def order(axis, size):
    return [lax.axis_index(axis) ^ k for k in range(size)]


def gather(x, axis, size):
    if size <= DIRECT:
        return [x] + [hop(x, axis, size, k) for k in range(1, size)]
    whole = lax.all_gather(x, axis, axis=0)
    return [block(whole, k) for k in order(axis, size)]


def swap(pieces, axis, size):
    if size <= DIRECT:
        return [pieces[0]] + [hop(pieces[k], axis, size, k) for k in range(1, size)]
    ids = order(axis, size)
    whole = lax.all_to_all(placed(pieces, ids), axis, split_axis=0, concat_axis=0)
    return [block(whole, k) for k in ids]


def exchange(x, axis):
    return lax.all_to_all(x, axis, split_axis=0, concat_axis=0, tiled=True)


def total(terms):
    return functools.reduce(jnp.add, [t.astype(jnp.float32) for t in terms])


def spread_kernel(rows_ref, weights_ref, out_ref):
    tile = 32
    tokens = rows_ref.shape[1]

    def step(i, carry):
        base = pl.multiple_of(i * tile, tile)
        here = lax.broadcasted_iota(jnp.int32, (tile, tokens), 0) + base
        total = jnp.zeros((tile, tokens), jnp.float32)
        for k in range(rows_ref.shape[0]):
            hit = rows_ref[k : k + 1, :] == here
            total = jnp.where(hit, weights_ref[k : k + 1, :], total)
        out_ref[pl.ds(base, tile), :] = total.astype(out_ref.dtype)
        return carry

    lax.fori_loop(0, out_ref.shape[0] // tile, step, 0)


def spread(rows, weights, row_total):
    picks, tokens = rows.shape
    width = min(tokens, 512)
    return pl.pallas_call(
        spread_kernel,
        grid=(tokens // width,),
        in_specs=[pl.BlockSpec((picks, width), lambda i: (0, i))] * 2,
        out_specs=pl.BlockSpec((row_total, width), lambda i: (0, i)),
        out_shape=jax.ShapeDtypeStruct((row_total, tokens), jnp.bfloat16),
        compiler_params=pltpu.CompilerParams(vmem_limit_bytes=16 << 20),
        cost_estimate=pl.CostEstimate(
            flops=2 * picks * tokens * row_total,
            bytes_accessed=2 * tokens * row_total,
            transcendentals=0,
        ),
    )(rows, weights)


def pick_kernel(table_ref, rows_ref, out_ref):
    lanes = 128
    rows = rows_ref[...]
    inner = rows & (lanes - 1)
    outer = rows >> 7
    total = jnp.zeros(out_ref.shape, jnp.float32)
    for j in range(table_ref.shape[1] // lanes):
        part = table_ref[:, j * lanes : (j + 1) * lanes]
        found = jnp.take_along_axis(part, inner, axis=1)
        total = jnp.where(outer == j, found, total)
    out_ref[...] = total


def pick(table, rows):
    return pl.pallas_call(
        pick_kernel,
        out_shape=jax.ShapeDtypeStruct(rows.shape, jnp.float32),
        cost_estimate=pl.CostEstimate(
            flops=rows.size * 16, bytes_accessed=4 * table.size, transcendentals=0
        ),
    )(table, rows)


def pick_weights(pick_scores):
    row_max = jnp.max(pick_scores, axis=1, keepdims=True)
    exponent = jnp.exp(pick_scores - row_max)
    return exponent / jnp.sum(exponent, axis=1, keepdims=True)


def contract(a, b, dim_a, dim_b):
    return lax.dot_general(
        a, b, (((dim_a,), (dim_b,)), ((), ())), preferred_element_type=jnp.float32
    )


def local_general(dp, pairs, hidden_in, gate_weight, values, pick_rows, pick_scores, grad_out):
    tokens, cols = hidden_in.shape
    rows_here, width = values.shape
    picks = pick_rows.shape[1]
    table = 2 * pairs
    sub = rows_here // dp
    me, pair, core = (lax.axis_index(a) for a in ("dp",) + TABLE)
    here = 2 * pair + core
    f32, bf16 = jnp.float32, jnp.bfloat16

    wide = lax.all_gather(hidden_in, TABLE, axis=1, tiled=True)
    wide = wide.reshape(tokens, dp, table * cols // dp).transpose(1, 0, 2)
    hidden_all = exchange(wide, "dp").reshape(dp * tokens, -1)

    weights = pick_weights(pick_scores)
    weights_bf = weights.astype(bf16)
    small = jnp.concatenate([weights_bf, (pick_rows >> 5).astype(bf16), (pick_rows & 31).astype(bf16)], axis=1)
    small = small.T.reshape(-1, cols)
    sent = lax.all_gather(jnp.concatenate([grad_out, small], axis=0), "dp", axis=0)
    grad_out_all = sent[:, :tokens].reshape(dp * tokens, cols)
    small = sent[:, tokens:].reshape(dp, 3, picks, tokens).transpose(1, 2, 0, 3)
    small = small.reshape(3, picks, dp * tokens).astype(f32)
    rows_all = small[1].astype(jnp.int32) * 32 + small[2].astype(jnp.int32)

    def moved_row(row):
        return ((row // rows_here) ^ here) * rows_here + row % rows_here

    spread_all = spread(moved_row(rows_all), small[0], rows_here * table)

    by_core = values.reshape(rows_here, pairs, 2, cols).transpose(2, 1, 0, 3)
    mine = block(by_core, core)
    other = hop(block(by_core, 1 - core), "core", 2, 1)
    value_sent = [
        jnp.concatenate([block(mine, z), block(other, z)], axis=0) for z in order("pair", pairs)
    ]
    value_cols = jnp.concatenate(swap(value_sent, "pair", pairs), axis=0)

    partial_gate = contract(hidden_all, gate_weight, 1, 0).astype(bf16)
    terms = exchange(partial_gate.reshape(dp, tokens, cols), "dp")
    gate_own = total([terms[k] for k in range(dp)]).astype(bf16)
    gate_input = lax.all_gather(gate_own, "dp", axis=0, tiled=True).astype(f32)

    memory_read = contract(spread_all, value_cols, 0, 0)
    sigmoid_v = jax.nn.sigmoid(gate_input)
    gate_value = gate_input * sigmoid_v
    gate_slope = sigmoid_v * (1.0 + gate_input * (1.0 - sigmoid_v))
    upstream = grad_out_all.astype(f32)
    mem_grad = (upstream * gate_value).astype(bf16)
    gate_grad_in = (upstream * memory_read * gate_slope).astype(bf16)

    def own(x):
        return block(x.reshape(dp, tokens, cols), me)

    branch_out = (own(memory_read) * own(gate_value)).astype(bf16)

    input_term = contract(gate_grad_in, gate_weight, 1, 1).astype(bf16)
    input_got = exchange(input_term.reshape(dp, tokens, -1), "dp")

    spread_parts = spread_all.reshape(pairs, 2, dp, sub, dp * tokens)
    part = jnp.concatenate(
        [
            lax.dynamic_slice(
                spread_parts, (z ^ pair, 0, me, 0, 0), (1, 2, 1, sub, dp * tokens)
            ).reshape(2 * sub, dp * tokens)
            for z in range(pairs)
        ],
        axis=0,
    )
    value_term = contract(part, mem_grad, 1, 0).astype(bf16).reshape(pairs, 2, sub, cols)
    value_other = hop(value_term[:, 1], "core", 2, 1)

    affinity_all = contract(own(mem_grad), value_cols, 1, 1)
    own_rows = jnp.pad(moved_row(pick_rows), ((0, 0), (0, 128 - picks)))
    affinity = pick(affinity_all, own_rows)[:, :picks]
    affinity = affinity + hop(affinity, "core", 2, 1)
    high = affinity.astype(bf16)
    low = (affinity - high.astype(f32)).astype(bf16)
    parts = jnp.concatenate([high, low], axis=1).reshape(-1, cols)

    back = exchange(
        jnp.concatenate(
            [value_term[:, 0], value_other, jnp.broadcast_to(parts, (pairs,) + parts.shape)], axis=1
        ),
        "pair",
    )
    affinity = back[:, 2 * sub :].reshape(pairs, tokens, 2 * picks).astype(f32)
    affinity = jnp.sum(affinity[:, :, :picks] + affinity[:, :, picks:], axis=0)
    grad_scores = weights * (affinity - jnp.sum(weights * affinity, axis=1, keepdims=True))

    first, second = back[:, :sub], back[:, sub : 2 * sub]
    back = jnp.stack(
        [jnp.where(core == 0, first, second), jnp.where(core == 0, second, first)], axis=1
    )
    back = back.transpose(2, 0, 1, 3).reshape(sub, width)
    grad_values = placed(
        [r.astype(f32) for r in gather(back, "dp", dp)], order("dp", dp)
    ).reshape(rows_here, width)

    wide = input_got.transpose(1, 0, 2).reshape(tokens, table, cols)
    input_terms = exchange(wide.transpose(1, 0, 2), TABLE)
    grad_hidden = total([input_terms[k] for k in range(table)]).astype(bf16)
    grad_gate = contract(hidden_all, gate_grad_in, 0, 0)
    return (branch_out, grad_hidden, grad_gate, grad_values, grad_scores)


def kernel_call(body, outs, *args, scratch=(), after=()):
    count = len(args)

    def whole_body(*refs):
        body(*refs[:count], *refs[count + len(after) :])

    vmem = pl.BlockSpec(memory_space=pltpu.VMEM)
    return pl.pallas_call(
        whole_body,
        in_specs=[pl.BlockSpec(memory_space=pltpu.SMEM)] + [vmem] * (count + len(after) - 1),
        out_specs=[vmem] * len(outs),
        out_shape=list(outs),
        scratch_shapes=list(scratch),
        compiler_params=pltpu.CompilerParams(vmem_limit_bytes=12 << 20),
        cost_estimate=pl.CostEstimate(flops=0, bytes_accessed=0, transcendentals=0),
    )(*args, *after)


def shape(dims, dtype=jnp.bfloat16):
    return jax.ShapeDtypeStruct(dims, dtype)


TOKEN = shape((8, 128), jnp.float32)


def sign(token):
    token[...] = jnp.zeros(token.shape, token.dtype)


def aligned(index, size):
    return pl.ds(pl.multiple_of(index * size, size), size)


def pack_rows(out_ref, first, x):
    count, lanes = x.shape
    per = out_ref.shape[1] // lanes
    for j in range(count):
        row, lane = (first + j) // per, (first + j) % per * lanes
        out_ref[row : row + 1, lane : lane + lanes] = x[j : j + 1, :]


def row_of(packed, j, lanes):
    per = packed.shape[1] // lanes
    return packed[j // per : j // per + 1, j % per * lanes : (j % per + 1) * lanes]


def prepare_body(ids, scores, rows, grad_out, sent, weights, packed):
    tokens = grad_out.shape[0]
    x = scores[...]
    exponent = jnp.exp(x - jnp.max(x, axis=0, keepdims=True))
    w = exponent / jnp.sum(exponent, axis=0, keepdims=True)
    weights[...] = w
    packed[...] = jnp.zeros(packed.shape, packed.dtype)
    count = w.shape[0]
    pack_rows(packed, 0, w)
    pack_rows(packed, count, (rows[...] >> 5).astype(jnp.float32))
    pack_rows(packed, 2 * count, (rows[...] & 31).astype(jnp.float32))
    sent[:tokens, :] = grad_out[...]
    sent[tokens:, :] = packed[...].astype(sent.dtype)


def moved(row, rows_here, pair, core):
    owner, inner = lax.div(row, rows_here), lax.rem(row, rows_here)
    return (owner ^ (2 * pair + core)) * rows_here + inner


def spread_body(picks, rows_here, ids, sent, out, part, rows, weights):
    me, pair, core = ids[0], ids[1], ids[2]
    dp = sent.shape[0]
    tokens = rows.shape[1] // dp
    pairs = part.shape[0] // (2 * (rows_here // dp))
    for e in range(dp):
        packed = sent[e, tokens:, :].astype(jnp.float32)
        span = slice(e * tokens, (e + 1) * tokens)
        for k in range(picks):
            weights[k : k + 1, span] = row_of(packed, k, tokens)
            high, low = row_of(packed, picks + k, tokens), row_of(packed, 2 * picks + k, tokens)
            rows[k : k + 1, span] = (high * 32.0 + low).astype(jnp.int32)
    rows[...] = moved(rows[...], rows_here, pair, core)
    tile = 64

    def step(i, carry):
        base = pl.multiple_of(i * tile, tile)
        here = lax.broadcasted_iota(jnp.int32, (tile, rows.shape[1]), 0) + base
        acc = jnp.zeros((tile, rows.shape[1]), jnp.float32)
        for k in range(picks):
            acc = jnp.where(rows[k : k + 1, :] == here, weights[k : k + 1, :], acc)
        out[pl.ds(base, tile), :] = acc.astype(out.dtype)
        return carry

    lax.fori_loop(0, out.shape[0] // tile, step, 0)
    sub = rows_here // dp
    for g in range(2):
        for z in range(pairs):
            at = (2 * z + g) * rows_here + me * sub
            spot = (g * pairs + z) * sub
            part[spot : spot + sub, :] = out[pl.ds(pl.multiple_of(at, sub), sub), :]


def columns_body(ids, values, own, other):
    rows, cols = values.shape[0], own.shape[1]
    for k in range(own.shape[0] // rows):
        span, at = slice(k * rows, (k + 1) * rows), 2 * (ids[1] ^ k)
        own[span, :] = values[:, aligned(at + ids[2], cols)]
        other[span, :] = values[:, aligned(at + 1 - ids[2], cols)]


def halves_body(ids, own, got, *outs):
    rows = outs[0].shape[0] // 2
    for k, out in enumerate(outs):
        span = slice(k * rows, (k + 1) * rows)
        out[:rows, :] = own[span, :]
        out[rows:, :] = got[span, :]


def dot(a, b, dim_a=1, dim_b=0):
    return lax.dot_general(
        a, b, (((dim_a,), (dim_b,)), ((), ())), preferred_element_type=jnp.float32
    )


def join_body(ids, *refs):
    pieces, out = refs[:-1], refs[-1]
    rows = pieces[0].shape[0]
    for k, piece in enumerate(pieces):
        out[k * rows : (k + 1) * rows, :] = piece[...]


def gate_body(ids, *refs):
    pieces, (others, weight, first, second, stage) = refs[:-5], refs[-5:]
    dp, rows = len(pieces), stage.shape[1]
    cols = weight.shape[1]
    own, other = weight[aligned(ids[2], cols), :], weight[aligned(1 - ids[2], cols), :]
    for k, piece in enumerate(pieces):
        term = dot(piece[...], own) + dot(others[k * rows : (k + 1) * rows, :], other)
        stage[ids[1] ^ k] = term.astype(stage.dtype)
    half = dp // 2
    for e in range(half):
        first[e * rows : (e + 1) * rows, :] = stage[e]
        second[e * rows : (e + 1) * rows, :] = stage[half + e]


def add_body(ids, a, a_got, b, b_got, a_keep, b_keep, a_send, b_send, token):
    sign(token)
    f32 = jnp.float32
    for x, got, keep, send in ((a, a_got, a_keep, a_send), (b, b_got, b_keep, b_send)):
        keep[...] = (x[...].astype(f32) + got[...].astype(f32)).astype(keep.dtype)
        send[...] = keep[...]


def gate_value_of(stage, a0, a1, b0, b1):
    half = a0.shape[0]
    stage[:half, :] = a0[...].astype(jnp.float32) + a1[...].astype(jnp.float32)
    stage[half:, :] = b0[...].astype(jnp.float32) + b1[...].astype(jnp.float32)


def values_body(ids, a0, a1, b0, b1, sent, part, mem_grad, factor, value_own, keep, send, token, stage):
    tokens = value_own.shape[0]
    gate_value_of(stage, a0, a1, b0, b1)
    for k in range(sent.shape[0]):
        span = aligned(ids[0] ^ k, tokens)
        gate = stage[span, :]
        s = jax.nn.sigmoid(gate)
        upstream = sent[ids[0] ^ k, :tokens, :].astype(jnp.float32)
        mem_grad[span, :] = (upstream * (gate * s)).astype(mem_grad.dtype)
        factor[span, :] = upstream * (s * (1.0 + gate * (1.0 - s)))
        if k == 0:
            value_own[...] = gate * s
    half = keep.shape[0]
    term = dot(part[...], mem_grad[...])
    keep[...] = term[:half].astype(keep.dtype)
    send[...] = term[half:].astype(send.dtype)
    sign(token)


def messages_body(ids, keep, got, *refs):
    messages, token = refs[:-1], refs[-1]
    sign(token)
    sub = messages[0].shape[0] // 2
    for z, message in enumerate(messages):
        message[:sub, :] = keep[z * sub : (z + 1) * sub, :]
        message[sub:, :] = got[z * sub : (z + 1) * sub, :]


def grads_body(rows_here, ids, factor, value_own, spread_ref, mem_grad, rows_ref, *refs):
    values, (weight, gate_grad, branch, term, packed) = refs[:-5], refs[-5:]
    every = gate_grad.shape[0]
    tokens, rows = branch.shape[0], values[0].shape[0]
    for k in range(factor.shape[0] // tokens):
        span = aligned(ids[0] ^ k, tokens)
        memory = 0.0
        for i, piece in enumerate(values):
            memory = memory + dot(spread_ref[i * rows : (i + 1) * rows, span], piece[...], 0, 0)
        gate_grad[span, :] = (factor[span, :] * memory).astype(gate_grad.dtype)
        if k == 0:
            branch[...] = (memory * value_own[...]).astype(branch.dtype)
    across = weight[aligned(1 - ids[2], weight.shape[1]), :]
    term[:every, :] = dot(gate_grad[...], across, 1, 1).astype(term.dtype)
    term[every:, :] = affinity_part(rows_here, ids, mem_grad, values, rows_ref, packed)


def affinity_part(rows_here, ids, mem_grad, values, rows, packed):
    f32 = jnp.float32
    tokens = rows.shape[1]
    count = rows.shape[0]
    at = moved(rows[...], rows_here, ids[1], ids[2])
    at = jnp.concatenate([at] * (tokens // count), axis=0).T
    inner, outer = at & 127, at >> 7
    grads = mem_grad[aligned(ids[0], tokens), :]
    found = jnp.zeros(at.shape, f32)
    blocks = values[0].shape[0] // 128
    for j, table in enumerate(values):
        all_rows = dot(grads, table[...], 1, 1)
        for i in range(blocks):
            hit = jnp.take_along_axis(all_rows[:, i * 128 : (i + 1) * 128], inner, axis=1)
            found = jnp.where(outer == j * blocks + i, hit, found)
    affinity = found.T[:count]
    high = affinity.astype(jnp.bfloat16).astype(f32)
    pack_rows(packed, 0, high)
    pack_rows(packed, count, affinity - high)
    return packed[...].astype(jnp.bfloat16)


def inputs_body(ids, gate_grad, weight, term, arrived, *refs):
    f32 = jnp.float32
    outs, token = refs[:-1], refs[-1]
    sign(token)
    every = gate_grad.shape[0]
    whole = term[every:, :].astype(f32) + arrived[every:, :].astype(f32)
    extra = whole.shape[0]
    whole = whole[: extra // 2] + whole[extra // 2 :]
    high = whole.astype(jnp.bfloat16).astype(f32)
    affinity = jnp.concatenate([high, whole - high], axis=0).astype(jnp.bfloat16)
    tokens = outs[0].shape[0] - extra
    own = weight[aligned(ids[2], weight.shape[1]), :]
    for i, out in enumerate(outs):
        span = aligned(ids[1] ^ i, tokens)
        total_term = dot(gate_grad[span, :], own, 1, 1) + arrived[span, :].astype(f32)
        out[:tokens, :] = total_term.astype(out.dtype)
        out[tokens:, :] = affinity


def sums_body(ids, *refs):
    pieces, (out, affinity) = refs[:-2], refs[-2:]
    whole = 0.0
    for piece in pieces:
        whole = whole + piece[...].astype(jnp.float32)
    tokens = out.shape[0]
    out[...] = whole[:tokens].astype(out.dtype)
    half = (whole.shape[0] - tokens) // 2
    affinity[...] = whole[tokens : tokens + half] + whole[tokens + half :]


def scores_body(ids, whole_ref, weights, grads):
    whole, w = whole_ref[...], weights[...]
    count, lanes = w.shape
    affinity = jnp.concatenate([row_of(whole, k, lanes) for k in range(count)], axis=0)
    grads[...] = w * (affinity - jnp.sum(w * affinity, axis=0, keepdims=True))


def rows_body(ids, *refs):
    back, halves = refs[:-2], refs[-2:]
    cols = back[0].shape[1]
    sub, half = back[0].shape[0] // 2, halves[0].shape[0]
    for z, piece in enumerate(back):
        for j, out in enumerate(halves):
            at = 2 * (ids[1] ^ z)
            span = slice(j * half, (j + 1) * half)
            out[:, aligned(at + ids[2], cols)] = piece[span, :]
            out[:, aligned(at + 1 - ids[2], cols)] = piece[sub + j * half : sub + (j + 1) * half, :]


def widen_body(ids, *refs):
    pieces, (out, token) = refs[:-2], refs[-2:]
    sign(token)
    half, count = pieces[0].shape[0], len(pieces) // 2
    for k, piece in enumerate(pieces):
        at = (ids[0] ^ (k % count)) * 2 * half + k // count * half
        out[pl.ds(pl.multiple_of(at, half), half), :] = piece[...].astype(out.dtype)


def widen(ids, pieces):
    rows, width = pieces[0].shape
    cols = width // 4
    return pl.pallas_call(
        widen_body,
        grid=(width // cols,),
        in_specs=[pl.BlockSpec(memory_space=pltpu.SMEM)]
        + [pl.BlockSpec((rows, cols), lambda i: (0, i))] * len(pieces),
        out_specs=[
            pl.BlockSpec((len(pieces) * rows, cols), lambda i: (0, i)),
            pl.BlockSpec(TOKEN.shape, lambda i: (0, 0)),
        ],
        out_shape=[shape((len(pieces) * rows, width), jnp.float32), TOKEN],
        compiler_params=pltpu.CompilerParams(vmem_limit_bytes=12 << 20),
        cost_estimate=pl.CostEstimate(flops=0, bytes_accessed=0, transcendentals=0),
    )(ids, *pieces)


def gate_grads_body(ids, *refs):
    pieces, (others, gate_grad, out, token) = refs[:-4], refs[-4:]
    sign(token)
    tokens = pieces[0].shape[0]
    for j in range(2):

        @pl.when(pl.program_id(0) == j)
        def _():
            acc = 0.0
            for k, piece in enumerate(pieces):
                grads = gate_grad[aligned(ids[1] ^ k, tokens), :]
                part = others[k * tokens : (k + 1) * tokens, :] if j else piece[...]
                acc = acc + dot(part, grads, 0, 0)
            out[...] = acc


def gate_grads(ids, pieces, others, gate_grad, after):
    cols = gate_grad.shape[1]
    vmem = pl.BlockSpec(memory_space=pltpu.VMEM)
    count = len(pieces) + 2

    def whole_body(ids, *refs):
        gate_grads_body(ids, *refs[:count], *refs[count + 1 :])

    return pl.pallas_call(
        whole_body,
        grid_spec=pltpu.PrefetchScalarGridSpec(
            num_scalar_prefetch=1,
            grid=(2,),
            in_specs=[vmem] * (count + 1),
            out_specs=[
                pl.BlockSpec((cols, cols), lambda j, ids: (ids[2] ^ j, 0)),
                pl.BlockSpec(TOKEN.shape, lambda j, ids: (0, 0)),
            ],
        ),
        out_shape=[shape((2 * cols, cols), jnp.float32), TOKEN],
        compiler_params=pltpu.CompilerParams(vmem_limit_bytes=12 << 20),
        cost_estimate=pl.CostEstimate(flops=0, bytes_accessed=0, transcendentals=0),
    )(ids, *pieces, others, gate_grad, after)


def local_square(dp, pairs, hidden_in, gate_weight, values, pick_rows, pick_scores, grad_out):
    tokens, cols = hidden_in.shape
    rows_here, width = values.shape
    picks = pick_rows.shape[1]
    sub = rows_here // dp
    f32 = jnp.float32
    me, pair, core = (lax.axis_index(a) for a in ("dp",) + TABLE)
    ids = jnp.stack([me, pair, core]).astype(jnp.int32)
    every = dp * tokens

    mine = []
    for k in range(dp):
        perm = [
            ((e * pairs + z) * 2 + h, (z * pairs + (e ^ k)) * 2 + h)
            for e in range(dp)
            for z in range(pairs)
            for h in range(2)
        ]
        mine.append(lax.ppermute(hidden_in, ("dp",) + TABLE, perm))
    rows_t = pick_rows.T
    small = -(-3 * picks * tokens // cols // 16) * 16
    sent, weights_t = kernel_call(
        prepare_body,
        [shape((tokens + small, cols)), shape((picks, tokens), f32)],
        ids, pick_scores.T, rows_t, grad_out,
        scratch=[pltpu.VMEM((small, cols), f32)],
    )
    sent_own = sent
    sent = lax.all_gather(sent_own, "dp", axis=0)
    joined = kernel_call(join_body, [shape((every, cols))], ids, *mine)[0]
    others = hop(joined, "core", 2, 1)
    first, second = kernel_call(
        gate_body,
        [shape((every // 2, cols))] * 2,
        ids, *mine, others, gate_weight,
        scratch=[pltpu.VMEM((dp, tokens, cols), jnp.bfloat16)],
    )
    value_own, value_send = kernel_call(
        columns_body, [shape((pairs * rows_here, cols))] * 2, ids, values
    )
    value_sent = kernel_call(
        halves_body, [shape((2 * rows_here, cols))] * pairs,
        ids, value_own, hop(value_send, "core", 2, 1),
    )
    value_got = swap(value_sent, "pair", pairs)
    first, second, *added, token = kernel_call(
        add_body,
        [shape((every // 2, cols))] * 4 + [TOKEN],
        ids, first, hop(first, "dp", dp, 1), second, hop(second, "dp", dp, 2),
        after=[sent] + value_got[1:3],
    )
    spread_all, spread_part = kernel_call(
        functools.partial(spread_body, picks, rows_here),
        [shape((2 * pairs * rows_here, every)), shape((2 * pairs * sub, every))],
        ids, sent,
        scratch=[pltpu.VMEM((picks, every), jnp.int32), pltpu.VMEM((picks, every), f32)],
        after=[token],
    )
    gates = [first, hop(added[0], "dp", dp, 2), second, hop(added[1], "dp", dp, 1)]

    mem_grad, factor, value_part, keep, send, token = kernel_call(
        values_body,
        [shape((every, cols)), shape((every, cols), f32), shape((tokens, cols), f32)]
        + [shape((pairs * sub, cols))] * 2
        + [TOKEN],
        ids, *gates, sent, spread_part,
        scratch=[pltpu.VMEM((every, cols), f32)],
    )
    *messages, sent_on = kernel_call(
        messages_body, [shape((2 * sub, cols))] * pairs + [TOKEN], ids, keep, hop(send, "core", 2, 1)
    )

    back = swap(messages, "pair", pairs)
    extra = 2 * picks * tokens // cols
    gate_grad, branch_out, term = kernel_call(
        functools.partial(grads_body, rows_here),
        [shape((every, cols)), shape((tokens, cols)), shape((every + extra, cols))],
        ids, factor, value_part, spread_all, mem_grad, rows_t, *value_got, gate_weight,
        scratch=[pltpu.VMEM((extra, cols), f32)],
        after=[sent_on],
    )
    *inputs, sent_inputs = kernel_call(
        inputs_body,
        [shape((tokens + extra, cols))] * pairs + [TOKEN],
        ids, gate_grad, gate_weight, term, hop(term, "core", 2, 1),
        after=back[1:2],
    )
    grad_gate, done = gate_grads(ids, mine, others, gate_grad, sent_inputs)
    grad_hidden, affinity = kernel_call(
        sums_body,
        [shape((tokens, cols)), shape((extra // 2, cols), f32)],
        ids, *swap(inputs, "pair", pairs), after=[done],
    )
    grad_scores = kernel_call(
        scores_body, [shape((picks, tokens), f32)], ids, affinity, weights_t
    )[0]
    perm = [
        ((d * pairs + z) * 2 + h, (z * pairs + d) * 2 + h)
        for d in range(dp)
        for z in range(pairs)
        for h in range(2)
    ]
    grad_hidden = lax.ppermute(grad_hidden, ("dp",) + TABLE, perm)
    first, second = kernel_call(
        rows_body, [shape((sub // 2, width))] * 2, ids, *back, after=[sent_inputs]
    )
    along_x, along_y = hop(first, "dp", dp, 1), hop(second, "dp", dp, 2)
    first = [first, along_x, hop(first, "dp", dp, 2), hop(along_x, "dp", dp, 2)]
    second = [second, hop(second, "dp", dp, 1), along_y, hop(along_y, "dp", dp, 1)]
    grad_values, token = widen(ids, first + second)
    return (branch_out, grad_hidden, grad_gate, grad_values, grad_scores.T)


def local(dp, pairs, *args):
    tokens, cols = args[0].shape
    square = dp == pairs == DIRECT and tokens == 128 and cols == 4 * tokens
    return (local_square if square else local_general)(dp, pairs, *args)


def solution(mesh):
    dp, table = mesh.shape["dp"], mesh.shape["table"]
    pairs = Mesh(mesh.devices.reshape(dp, table // 2, 2), ("dp",) + TABLE)
    split, rows, tokens = P("dp", TABLE), P(TABLE, None), P("dp", None)
    return jax.shard_map(
        functools.partial(local, dp, table // 2),
        mesh=pairs,
        in_specs=(split, split, rows, tokens, tokens, split),
        out_specs=(split, split, split, rows, tokens),
        check_vma=False,
    )
```

```python
import functools

import jax
import jax.numpy as jnp
from jax import lax
from jax.experimental import pallas as pl
from jax.experimental.pallas import tpu as pltpu
from jax.sharding import Mesh
from jax.sharding import PartitionSpec as P

DIRECT = 4
TABLE = ("pair", "core")


def block(x, index):
    return lax.dynamic_index_in_dim(x, index, 0, keepdims=False)


def placed(pieces, indices):
    out = jnp.zeros((len(pieces),) + pieces[0].shape, pieces[0].dtype)
    for piece, index in zip(pieces, indices):
        out = lax.dynamic_update_index_in_dim(out, piece, index, 0)
    return out


def hop(x, axis, size, mask):
    return lax.ppermute(x, axis, [(i, i ^ mask) for i in range(size)])


def order(axis, size):
    return [lax.axis_index(axis) ^ k for k in range(size)]


def gather(x, axis, size):
    if size <= DIRECT:
        return [x] + [hop(x, axis, size, k) for k in range(1, size)]
    whole = lax.all_gather(x, axis, axis=0)
    return [block(whole, k) for k in order(axis, size)]


def swap(pieces, axis, size):
    if size <= DIRECT:
        return [pieces[0]] + [hop(pieces[k], axis, size, k) for k in range(1, size)]
    ids = order(axis, size)
    whole = lax.all_to_all(placed(pieces, ids), axis, split_axis=0, concat_axis=0)
    return [block(whole, k) for k in ids]


def exchange(x, axis):
    return lax.all_to_all(x, axis, split_axis=0, concat_axis=0, tiled=True)


def total(terms):
    return functools.reduce(jnp.add, [t.astype(jnp.float32) for t in terms])


def spread_kernel(rows_ref, weights_ref, out_ref):
    tile = 32
    tokens = rows_ref.shape[1]

    def step(i, carry):
        base = pl.multiple_of(i * tile, tile)
        here = lax.broadcasted_iota(jnp.int32, (tile, tokens), 0) + base
        total = jnp.zeros((tile, tokens), jnp.float32)
        for k in range(rows_ref.shape[0]):
            hit = rows_ref[k : k + 1, :] == here
            total = jnp.where(hit, weights_ref[k : k + 1, :], total)
        out_ref[pl.ds(base, tile), :] = total.astype(out_ref.dtype)
        return carry

    lax.fori_loop(0, out_ref.shape[0] // tile, step, 0)


def spread(rows, weights, row_total):
    picks, tokens = rows.shape
    width = min(tokens, 512)
    return pl.pallas_call(
        spread_kernel,
        grid=(tokens // width,),
        in_specs=[pl.BlockSpec((picks, width), lambda i: (0, i))] * 2,
        out_specs=pl.BlockSpec((row_total, width), lambda i: (0, i)),
        out_shape=jax.ShapeDtypeStruct((row_total, tokens), jnp.bfloat16),
        compiler_params=pltpu.CompilerParams(vmem_limit_bytes=16 << 20),
        cost_estimate=pl.CostEstimate(
            flops=2 * picks * tokens * row_total,
            bytes_accessed=2 * tokens * row_total,
            transcendentals=0,
        ),
    )(rows, weights)


def pick_kernel(table_ref, rows_ref, out_ref):
    lanes = 128
    rows = rows_ref[...]
    inner = rows & (lanes - 1)
    outer = rows >> 7
    total = jnp.zeros(out_ref.shape, jnp.float32)
    for j in range(table_ref.shape[1] // lanes):
        part = table_ref[:, j * lanes : (j + 1) * lanes]
        found = jnp.take_along_axis(part, inner, axis=1)
        total = jnp.where(outer == j, found, total)
    out_ref[...] = total


def pick(table, rows):
    return pl.pallas_call(
        pick_kernel,
        out_shape=jax.ShapeDtypeStruct(rows.shape, jnp.float32),
        cost_estimate=pl.CostEstimate(
            flops=rows.size * 16, bytes_accessed=4 * table.size, transcendentals=0
        ),
    )(table, rows)


def pick_weights(pick_scores):
    row_max = jnp.max(pick_scores, axis=1, keepdims=True)
    exponent = jnp.exp(pick_scores - row_max)
    return exponent / jnp.sum(exponent, axis=1, keepdims=True)


def contract(a, b, dim_a, dim_b):
    return lax.dot_general(
        a, b, (((dim_a,), (dim_b,)), ((), ())), preferred_element_type=jnp.float32
    )


def local_general(dp, pairs, hidden_in, gate_weight, values, pick_rows, pick_scores, grad_out):
    tokens, cols = hidden_in.shape
    rows_here, width = values.shape
    picks = pick_rows.shape[1]
    table = 2 * pairs
    sub = rows_here // dp
    me, pair, core = (lax.axis_index(a) for a in ("dp",) + TABLE)
    here = 2 * pair + core
    f32, bf16 = jnp.float32, jnp.bfloat16

    wide = lax.all_gather(hidden_in, TABLE, axis=1, tiled=True)
    wide = wide.reshape(tokens, dp, table * cols // dp).transpose(1, 0, 2)
    hidden_all = exchange(wide, "dp").reshape(dp * tokens, -1)

    weights = pick_weights(pick_scores)
    weights_bf = weights.astype(bf16)
    small = jnp.concatenate([weights_bf, (pick_rows >> 5).astype(bf16), (pick_rows & 31).astype(bf16)], axis=1)
    small = small.T.reshape(-1, cols)
    sent = lax.all_gather(jnp.concatenate([grad_out, small], axis=0), "dp", axis=0)
    grad_out_all = sent[:, :tokens].reshape(dp * tokens, cols)
    small = sent[:, tokens:].reshape(dp, 3, picks, tokens).transpose(1, 2, 0, 3)
    small = small.reshape(3, picks, dp * tokens).astype(f32)
    rows_all = small[1].astype(jnp.int32) * 32 + small[2].astype(jnp.int32)

    def moved_row(row):
        return ((row // rows_here) ^ here) * rows_here + row % rows_here

    spread_all = spread(moved_row(rows_all), small[0], rows_here * table)

    by_core = values.reshape(rows_here, pairs, 2, cols).transpose(2, 1, 0, 3)
    mine = block(by_core, core)
    other = hop(block(by_core, 1 - core), "core", 2, 1)
    value_sent = [
        jnp.concatenate([block(mine, z), block(other, z)], axis=0) for z in order("pair", pairs)
    ]
    value_cols = jnp.concatenate(swap(value_sent, "pair", pairs), axis=0)

    partial_gate = contract(hidden_all, gate_weight, 1, 0).astype(bf16)
    terms = exchange(partial_gate.reshape(dp, tokens, cols), "dp")
    gate_own = total([terms[k] for k in range(dp)]).astype(bf16)
    gate_input = lax.all_gather(gate_own, "dp", axis=0, tiled=True).astype(f32)

    memory_read = contract(spread_all, value_cols, 0, 0)
    sigmoid_v = jax.nn.sigmoid(gate_input)
    gate_value = gate_input * sigmoid_v
    gate_slope = sigmoid_v * (1.0 + gate_input * (1.0 - sigmoid_v))
    upstream = grad_out_all.astype(f32)
    mem_grad = (upstream * gate_value).astype(bf16)
    gate_grad_in = (upstream * memory_read * gate_slope).astype(bf16)

    def own(x):
        return block(x.reshape(dp, tokens, cols), me)

    branch_out = (own(memory_read) * own(gate_value)).astype(bf16)

    input_term = contract(gate_grad_in, gate_weight, 1, 1).astype(bf16)
    input_got = exchange(input_term.reshape(dp, tokens, -1), "dp")

    spread_parts = spread_all.reshape(pairs, 2, dp, sub, dp * tokens)
    part = jnp.concatenate(
        [
            lax.dynamic_slice(
                spread_parts, (z ^ pair, 0, me, 0, 0), (1, 2, 1, sub, dp * tokens)
            ).reshape(2 * sub, dp * tokens)
            for z in range(pairs)
        ],
        axis=0,
    )
    value_term = contract(part, mem_grad, 1, 0).astype(bf16).reshape(pairs, 2, sub, cols)
    value_other = hop(value_term[:, 1], "core", 2, 1)

    affinity_all = contract(own(mem_grad), value_cols, 1, 1)
    own_rows = jnp.pad(moved_row(pick_rows), ((0, 0), (0, 128 - picks)))
    affinity = pick(affinity_all, own_rows)[:, :picks]
    affinity = affinity + hop(affinity, "core", 2, 1)
    high = affinity.astype(bf16)
    low = (affinity - high.astype(f32)).astype(bf16)
    parts = jnp.concatenate([high, low], axis=1).reshape(-1, cols)

    back = exchange(
        jnp.concatenate(
            [value_term[:, 0], value_other, jnp.broadcast_to(parts, (pairs,) + parts.shape)], axis=1
        ),
        "pair",
    )
    affinity = back[:, 2 * sub :].reshape(pairs, tokens, 2 * picks).astype(f32)
    affinity = jnp.sum(affinity[:, :, :picks] + affinity[:, :, picks:], axis=0)
    grad_scores = weights * (affinity - jnp.sum(weights * affinity, axis=1, keepdims=True))

    first, second = back[:, :sub], back[:, sub : 2 * sub]
    back = jnp.stack(
        [jnp.where(core == 0, first, second), jnp.where(core == 0, second, first)], axis=1
    )
    back = back.transpose(2, 0, 1, 3).reshape(sub, width)
    grad_values = placed(
        [r.astype(f32) for r in gather(back, "dp", dp)], order("dp", dp)
    ).reshape(rows_here, width)

    wide = input_got.transpose(1, 0, 2).reshape(tokens, table, cols)
    input_terms = exchange(wide.transpose(1, 0, 2), TABLE)
    grad_hidden = total([input_terms[k] for k in range(table)]).astype(bf16)
    grad_gate = contract(hidden_all, gate_grad_in, 0, 0)
    return (branch_out, grad_hidden, grad_gate, grad_values, grad_scores)


def kernel_call(body, outs, *args, scratch=(), after=()):
    count = len(args)

    def whole_body(*refs):
        body(*refs[:count], *refs[count + len(after) :])

    vmem = pl.BlockSpec(memory_space=pltpu.VMEM)
    return pl.pallas_call(
        whole_body,
        in_specs=[pl.BlockSpec(memory_space=pltpu.SMEM)] + [vmem] * (count + len(after) - 1),
        out_specs=[vmem] * len(outs),
        out_shape=list(outs),
        scratch_shapes=list(scratch),
        compiler_params=pltpu.CompilerParams(vmem_limit_bytes=12 << 20),
        cost_estimate=pl.CostEstimate(flops=0, bytes_accessed=0, transcendentals=0),
    )(*args, *after)


def shape(dims, dtype=jnp.bfloat16):
    return jax.ShapeDtypeStruct(dims, dtype)


TOKEN = shape((8, 128), jnp.float32)


def sign(token):
    token[...] = jnp.zeros(token.shape, token.dtype)


def aligned(index, size):
    return pl.ds(pl.multiple_of(index * size, size), size)


def pack_rows(out_ref, first, x):
    count, lanes = x.shape
    per = out_ref.shape[1] // lanes
    for j in range(count):
        row, lane = (first + j) // per, (first + j) % per * lanes
        out_ref[row : row + 1, lane : lane + lanes] = x[j : j + 1, :]


def row_of(packed, j, lanes):
    per = packed.shape[1] // lanes
    return packed[j // per : j // per + 1, j % per * lanes : (j % per + 1) * lanes]


def prepare_body(ids, scores, rows, grad_out, sent, weights, packed):
    tokens = grad_out.shape[0]
    x = scores[...]
    exponent = jnp.exp(x - jnp.max(x, axis=0, keepdims=True))
    w = exponent / jnp.sum(exponent, axis=0, keepdims=True)
    weights[...] = w
    packed[...] = jnp.zeros(packed.shape, packed.dtype)
    count = w.shape[0]
    pack_rows(packed, 0, w)
    pack_rows(packed, count, (rows[...] >> 5).astype(jnp.float32))
    pack_rows(packed, 2 * count, (rows[...] & 31).astype(jnp.float32))
    sent[:tokens, :] = grad_out[...]
    sent[tokens:, :] = packed[...].astype(sent.dtype)


def moved(row, rows_here, pair, core):
    owner, inner = lax.div(row, rows_here), lax.rem(row, rows_here)
    return (owner ^ (2 * pair + core)) * rows_here + inner


def spread_body(picks, rows_here, ids, sent, out, part, rows, weights):
    me, pair, core = ids[0], ids[1], ids[2]
    dp = sent.shape[0]
    tokens = rows.shape[1] // dp
    pairs = part.shape[0] // (2 * (rows_here // dp))
    for e in range(dp):
        packed = sent[e, tokens:, :].astype(jnp.float32)
        span = slice(e * tokens, (e + 1) * tokens)
        for k in range(picks):
            weights[k : k + 1, span] = row_of(packed, k, tokens)
            high, low = row_of(packed, picks + k, tokens), row_of(packed, 2 * picks + k, tokens)
            rows[k : k + 1, span] = (high * 32.0 + low).astype(jnp.int32)
    rows[...] = moved(rows[...], rows_here, pair, core)
    tile = 64

    def step(i, carry):
        base = pl.multiple_of(i * tile, tile)
        here = lax.broadcasted_iota(jnp.int32, (tile, rows.shape[1]), 0) + base
        acc = jnp.zeros((tile, rows.shape[1]), jnp.float32)
        for k in range(picks):
            acc = jnp.where(rows[k : k + 1, :] == here, weights[k : k + 1, :], acc)
        out[pl.ds(base, tile), :] = acc.astype(out.dtype)
        return carry

    lax.fori_loop(0, out.shape[0] // tile, step, 0, unroll=2)
    sub = rows_here // dp
    for g in range(2):
        for z in range(pairs):
            at = (2 * z + g) * rows_here + me * sub
            spot = (g * pairs + z) * sub
            part[spot : spot + sub, :] = out[pl.ds(pl.multiple_of(at, sub), sub), :]


def columns_body(ids, values, own, other):
    rows, cols = values.shape[0], own.shape[1]
    for k in range(own.shape[0] // rows):
        span, at = slice(k * rows, (k + 1) * rows), 2 * (ids[1] ^ k)
        own[span, :] = values[:, aligned(at + ids[2], cols)]
        other[span, :] = values[:, aligned(at + 1 - ids[2], cols)]


def halves_body(ids, own, got, *outs):
    rows = outs[0].shape[0] // 2
    for k, out in enumerate(outs):
        span = slice(k * rows, (k + 1) * rows)
        out[:rows, :] = own[span, :]
        out[rows:, :] = got[span, :]


def dot(a, b, dim_a=1, dim_b=0):
    return lax.dot_general(
        a, b, (((dim_a,), (dim_b,)), ((), ())), preferred_element_type=jnp.float32
    )


def join_body(ids, *refs):
    pieces, out = refs[:-1], refs[-1]
    rows = pieces[0].shape[0]
    for k, piece in enumerate(pieces):
        out[k * rows : (k + 1) * rows, :] = piece[...]


def gate_body(ids, *refs):
    pieces, (others, weight, first, second, stage) = refs[:-5], refs[-5:]
    dp, rows = len(pieces), stage.shape[1]
    cols = weight.shape[1]
    own, other = weight[aligned(ids[2], cols), :], weight[aligned(1 - ids[2], cols), :]
    for k, piece in enumerate(pieces):
        term = dot(piece[...], own) + dot(others[k * rows : (k + 1) * rows, :], other)
        stage[ids[1] ^ k] = term.astype(stage.dtype)
    half = dp // 2
    for e in range(half):
        first[e * rows : (e + 1) * rows, :] = stage[e]
        second[e * rows : (e + 1) * rows, :] = stage[half + e]


def add_body(ids, a, a_got, b, b_got, a_keep, b_keep, a_send, b_send, token):
    sign(token)
    f32 = jnp.float32
    for x, got, keep, send in ((a, a_got, a_keep, a_send), (b, b_got, b_keep, b_send)):
        keep[...] = (x[...].astype(f32) + got[...].astype(f32)).astype(keep.dtype)
        send[...] = keep[...]


def gate_value_of(stage, a0, a1, b0, b1):
    half = a0.shape[0]
    stage[:half, :] = a0[...].astype(jnp.float32) + a1[...].astype(jnp.float32)
    stage[half:, :] = b0[...].astype(jnp.float32) + b1[...].astype(jnp.float32)


def values_body(ids, a0, a1, b0, b1, sent, part, mem_grad, factor, value_own, keep, send, token, stage):
    tokens = value_own.shape[0]
    gate_value_of(stage, a0, a1, b0, b1)
    for k in range(sent.shape[0]):
        span = aligned(ids[0] ^ k, tokens)
        gate = stage[span, :]
        s = jax.nn.sigmoid(gate)
        upstream = sent[ids[0] ^ k, :tokens, :].astype(jnp.float32)
        mem_grad[span, :] = (upstream * (gate * s)).astype(mem_grad.dtype)
        factor[span, :] = upstream * (s * (1.0 + gate * (1.0 - s)))
        if k == 0:
            value_own[...] = gate * s
    half = keep.shape[0]
    term = dot(part[...], mem_grad[...])
    keep[...] = term[:half].astype(keep.dtype)
    send[...] = term[half:].astype(send.dtype)
    sign(token)


def messages_body(ids, keep, got, *refs):
    messages, token = refs[:-1], refs[-1]
    sign(token)
    sub = messages[0].shape[0] // 2
    for z, message in enumerate(messages):
        message[:sub, :] = keep[z * sub : (z + 1) * sub, :]
        message[sub:, :] = got[z * sub : (z + 1) * sub, :]


def grads_body(rows_here, ids, factor, value_own, spread_ref, mem_grad, rows_ref, *refs):
    values, (weight, gate_grad, branch, term, packed) = refs[:-5], refs[-5:]
    every = gate_grad.shape[0]
    tokens, rows = branch.shape[0], values[0].shape[0]
    for k in range(factor.shape[0] // tokens):
        span = aligned(ids[0] ^ k, tokens)
        memory = 0.0
        for i, piece in enumerate(values):
            memory = memory + dot(spread_ref[i * rows : (i + 1) * rows, span], piece[...], 0, 0)
        gate_grad[span, :] = (factor[span, :] * memory).astype(gate_grad.dtype)
        if k == 0:
            branch[...] = (memory * value_own[...]).astype(branch.dtype)
    across = weight[aligned(1 - ids[2], weight.shape[1]), :]
    term[:every, :] = dot(gate_grad[...], across, 1, 1).astype(term.dtype)
    term[every:, :] = affinity_part(rows_here, ids, mem_grad, values, rows_ref, packed)


def affinity_part(rows_here, ids, mem_grad, values, rows, packed):
    f32 = jnp.float32
    tokens = rows.shape[1]
    count = rows.shape[0]
    at = moved(rows[...], rows_here, ids[1], ids[2])
    at = jnp.concatenate([at] * (tokens // count), axis=0).T
    inner, outer = at & 127, at >> 7
    grads = mem_grad[aligned(ids[0], tokens), :]
    found = jnp.zeros(at.shape, f32)
    blocks = values[0].shape[0] // 128
    for j, table in enumerate(values):
        all_rows = dot(grads, table[...], 1, 1)
        for i in range(blocks):
            hit = jnp.take_along_axis(all_rows[:, i * 128 : (i + 1) * 128], inner, axis=1)
            found = jnp.where(outer == j * blocks + i, hit, found)
    affinity = found.T[:count]
    high = affinity.astype(jnp.bfloat16).astype(f32)
    pack_rows(packed, 0, high)
    pack_rows(packed, count, affinity - high)
    return packed[...].astype(jnp.bfloat16)


def inputs_body(ids, gate_grad, weight, term, arrived, *refs):
    f32 = jnp.float32
    outs, token = refs[:-1], refs[-1]
    sign(token)
    every = gate_grad.shape[0]
    whole = term[every:, :].astype(f32) + arrived[every:, :].astype(f32)
    extra = whole.shape[0]
    whole = whole[: extra // 2] + whole[extra // 2 :]
    high = whole.astype(jnp.bfloat16).astype(f32)
    affinity = jnp.concatenate([high, whole - high], axis=0).astype(jnp.bfloat16)
    tokens = outs[0].shape[0] - extra
    own = weight[aligned(ids[2], weight.shape[1]), :]
    for i, out in enumerate(outs):
        span = aligned(ids[1] ^ i, tokens)
        total_term = dot(gate_grad[span, :], own, 1, 1) + arrived[span, :].astype(f32)
        out[:tokens, :] = total_term.astype(out.dtype)
        out[tokens:, :] = affinity


def sums_body(ids, *refs):
    pieces, (out, affinity) = refs[:-2], refs[-2:]
    whole = 0.0
    for piece in pieces:
        whole = whole + piece[...].astype(jnp.float32)
    tokens = out.shape[0]
    out[...] = whole[:tokens].astype(out.dtype)
    half = (whole.shape[0] - tokens) // 2
    affinity[...] = whole[tokens : tokens + half] + whole[tokens + half :]


def scores_body(ids, whole_ref, weights, grads):
    whole, w = whole_ref[...], weights[...]
    count, lanes = w.shape
    affinity = jnp.concatenate([row_of(whole, k, lanes) for k in range(count)], axis=0)
    grads[...] = w * (affinity - jnp.sum(w * affinity, axis=0, keepdims=True))


def rows_body(ids, *refs):
    back, halves = refs[:-2], refs[-2:]
    cols = back[0].shape[1]
    sub, half = back[0].shape[0] // 2, halves[0].shape[0]
    for z, piece in enumerate(back):
        for j, out in enumerate(halves):
            at = 2 * (ids[1] ^ z)
            span = slice(j * half, (j + 1) * half)
            out[:, aligned(at + ids[2], cols)] = piece[span, :]
            out[:, aligned(at + 1 - ids[2], cols)] = piece[sub + j * half : sub + (j + 1) * half, :]


def widen_body(ids, *refs):
    pieces, (out, token) = refs[:-2], refs[-2:]
    sign(token)
    half, count = pieces[0].shape[0], len(pieces) // 2
    for k, piece in enumerate(pieces):
        at = (ids[0] ^ (k % count)) * 2 * half + k // count * half
        out[pl.ds(pl.multiple_of(at, half), half), :] = piece[...].astype(out.dtype)


def widen(ids, pieces):
    rows, width = pieces[0].shape
    cols = width // 4
    return pl.pallas_call(
        widen_body,
        grid=(width // cols,),
        in_specs=[pl.BlockSpec(memory_space=pltpu.SMEM)]
        + [pl.BlockSpec((rows, cols), lambda i: (0, i))] * len(pieces),
        out_specs=[
            pl.BlockSpec((len(pieces) * rows, cols), lambda i: (0, i)),
            pl.BlockSpec(TOKEN.shape, lambda i: (0, 0)),
        ],
        out_shape=[shape((len(pieces) * rows, width), jnp.float32), TOKEN],
        compiler_params=pltpu.CompilerParams(vmem_limit_bytes=12 << 20),
        cost_estimate=pl.CostEstimate(flops=0, bytes_accessed=0, transcendentals=0),
    )(ids, *pieces)


def gate_grads_body(ids, *refs):
    pieces, (others, gate_grad, out, token) = refs[:-4], refs[-4:]
    sign(token)
    tokens = pieces[0].shape[0]
    for j in range(2):

        @pl.when(pl.program_id(0) == j)
        def _():
            acc = 0.0
            for k, piece in enumerate(pieces):
                grads = gate_grad[aligned(ids[1] ^ k, tokens), :]
                part = others[k * tokens : (k + 1) * tokens, :] if j else piece[...]
                acc = acc + dot(part, grads, 0, 0)
            out[...] = acc


def gate_grads(ids, pieces, others, gate_grad, after):
    cols = gate_grad.shape[1]
    vmem = pl.BlockSpec(memory_space=pltpu.VMEM)
    count = len(pieces) + 2

    def whole_body(ids, *refs):
        gate_grads_body(ids, *refs[:count], *refs[count + 1 :])

    return pl.pallas_call(
        whole_body,
        grid_spec=pltpu.PrefetchScalarGridSpec(
            num_scalar_prefetch=1,
            grid=(2,),
            in_specs=[vmem] * (count + 1),
            out_specs=[
                pl.BlockSpec((cols, cols), lambda j, ids: (ids[2] ^ j, 0)),
                pl.BlockSpec(TOKEN.shape, lambda j, ids: (0, 0)),
            ],
        ),
        out_shape=[shape((2 * cols, cols), jnp.float32), TOKEN],
        compiler_params=pltpu.CompilerParams(vmem_limit_bytes=12 << 20),
        cost_estimate=pl.CostEstimate(flops=0, bytes_accessed=0, transcendentals=0),
    )(ids, *pieces, others, gate_grad, after)


def local_square(dp, pairs, hidden_in, gate_weight, values, pick_rows, pick_scores, grad_out):
    tokens, cols = hidden_in.shape
    rows_here, width = values.shape
    picks = pick_rows.shape[1]
    sub = rows_here // dp
    f32 = jnp.float32
    me, pair, core = (lax.axis_index(a) for a in ("dp",) + TABLE)
    ids = jnp.stack([me, pair, core]).astype(jnp.int32)
    every = dp * tokens

    mine = []
    for k in range(dp):
        perm = [
            ((e * pairs + z) * 2 + h, (z * pairs + (e ^ k)) * 2 + h)
            for e in range(dp)
            for z in range(pairs)
            for h in range(2)
        ]
        mine.append(lax.ppermute(hidden_in, ("dp",) + TABLE, perm))
    rows_t = pick_rows.T
    small = -(-3 * picks * tokens // cols // 16) * 16
    sent, weights_t = kernel_call(
        prepare_body,
        [shape((tokens + small, cols)), shape((picks, tokens), f32)],
        ids, pick_scores.T, rows_t, grad_out,
        scratch=[pltpu.VMEM((small, cols), f32)],
    )
    sent_own = sent
    sent = lax.all_gather(sent_own, "dp", axis=0)
    joined = kernel_call(join_body, [shape((every, cols))], ids, *mine)[0]
    others = hop(joined, "core", 2, 1)
    first, second = kernel_call(
        gate_body,
        [shape((every // 2, cols))] * 2,
        ids, *mine, others, gate_weight,
        scratch=[pltpu.VMEM((dp, tokens, cols), jnp.bfloat16)],
    )
    value_own, value_send = kernel_call(
        columns_body, [shape((pairs * rows_here, cols))] * 2, ids, values
    )
    value_sent = kernel_call(
        halves_body, [shape((2 * rows_here, cols))] * pairs,
        ids, value_own, hop(value_send, "core", 2, 1),
    )
    value_got = swap(value_sent, "pair", pairs)
    first, second, *added, token = kernel_call(
        add_body,
        [shape((every // 2, cols))] * 4 + [TOKEN],
        ids, first, hop(first, "dp", dp, 1), second, hop(second, "dp", dp, 2),
        after=[sent] + value_got[1:3],
    )
    spread_all, spread_part = kernel_call(
        functools.partial(spread_body, picks, rows_here),
        [shape((2 * pairs * rows_here, every)), shape((2 * pairs * sub, every))],
        ids, sent,
        scratch=[pltpu.VMEM((picks, every), jnp.int32), pltpu.VMEM((picks, every), f32)],
        after=[token],
    )
    gates = [first, hop(added[0], "dp", dp, 2), second, hop(added[1], "dp", dp, 1)]

    mem_grad, factor, value_part, keep, send, token = kernel_call(
        values_body,
        [shape((every, cols)), shape((every, cols), f32), shape((tokens, cols), f32)]
        + [shape((pairs * sub, cols))] * 2
        + [TOKEN],
        ids, *gates, sent, spread_part,
        scratch=[pltpu.VMEM((every, cols), f32)],
    )
    *messages, sent_on = kernel_call(
        messages_body, [shape((2 * sub, cols))] * pairs + [TOKEN], ids, keep, hop(send, "core", 2, 1)
    )

    back = swap(messages, "pair", pairs)
    extra = 2 * picks * tokens // cols
    gate_grad, branch_out, term = kernel_call(
        functools.partial(grads_body, rows_here),
        [shape((every, cols)), shape((tokens, cols)), shape((every + extra, cols))],
        ids, factor, value_part, spread_all, mem_grad, rows_t, *value_got, gate_weight,
        scratch=[pltpu.VMEM((extra, cols), f32)],
        after=[sent_on],
    )
    *inputs, sent_inputs = kernel_call(
        inputs_body,
        [shape((tokens + extra, cols))] * pairs + [TOKEN],
        ids, gate_grad, gate_weight, term, hop(term, "core", 2, 1),
        after=back[1:2],
    )
    grad_gate, done = gate_grads(ids, mine, others, gate_grad, sent_inputs)
    grad_hidden, affinity = kernel_call(
        sums_body,
        [shape((tokens, cols)), shape((extra // 2, cols), f32)],
        ids, *swap(inputs, "pair", pairs), after=[done],
    )
    grad_scores = kernel_call(
        scores_body, [shape((picks, tokens), f32)], ids, affinity, weights_t
    )[0]
    perm = [
        ((d * pairs + z) * 2 + h, (z * pairs + d) * 2 + h)
        for d in range(dp)
        for z in range(pairs)
        for h in range(2)
    ]
    grad_hidden = lax.ppermute(grad_hidden, ("dp",) + TABLE, perm)
    first, second = kernel_call(
        rows_body, [shape((sub // 2, width))] * 2, ids, *back, after=[sent_inputs]
    )
    along_x, along_y = hop(first, "dp", dp, 1), hop(second, "dp", dp, 2)
    first = [first, along_x, hop(first, "dp", dp, 2), hop(along_x, "dp", dp, 2)]
    second = [second, hop(second, "dp", dp, 1), along_y, hop(along_y, "dp", dp, 1)]
    grad_values, token = widen(ids, first + second)
    return (branch_out, grad_hidden, grad_gate, grad_values, grad_scores.T)


def local(dp, pairs, *args):
    tokens, cols = args[0].shape
    square = dp == pairs == DIRECT and tokens == 128 and cols == 4 * tokens
    return (local_square if square else local_general)(dp, pairs, *args)


def solution(mesh):
    dp, table = mesh.shape["dp"], mesh.shape["table"]
    pairs = Mesh(mesh.devices.reshape(dp, table // 2, 2), ("dp",) + TABLE)
    split, rows, tokens = P("dp", TABLE), P(TABLE, None), P("dp", None)
    return jax.shard_map(
        functools.partial(local, dp, table // 2),
        mesh=pairs,
        in_specs=(split, split, rows, tokens, tokens, split),
        out_specs=(split, split, split, rows, tokens),
        check_vma=False,
    )
```
